256 devices in a mesh: seq: 128 (over z, x_lo, y, core), head: 2 (over x_hi).
Axes of the slice: x: 4 (x_hi: 2, x_lo: 2; x = x_hi * 2 + x_lo), y: 4, z: 8, core: 2. Of those that a mesh axis runs over, the one named last changes fastest.
Arguments:
- queries: bfloat16 [65536, 2, 1024], P('seq', None, 'head'), may hold values from -6 to 6
- key_rows: bfloat16 [65536, 2, 1024], P('seq', None, 'head'), may hold values from -6 to 6
- value_rows: bfloat16 [65536, 2, 1024], P('seq', None, 'head'), may hold values from -32 to 32
- cotangent: bfloat16 [65536, 2, 1024], P('seq', None, 'head'), may hold values from -6 to 6
Outputs:
- normed: bfloat16 [65536, 2, 1024], P('seq', None, 'head')
- grad_queries: bfloat16 [65536, 2, 1024], P('seq', None, 'head')
- grad_keys: bfloat16 [65536, 2, 1024], P('seq', None, 'head')
- grad_values: bfloat16 [65536, 2, 1024], P('seq', None, 'head')
The draws below stay inside these ranges and needn't reach their ends.
All inputs are finite; a program needn't handle non-finite values.
Results may differ from the reference program's by a relative error of at most 0.018.
Values may be sent and summed in bfloat16 or wider, within the bound.
No kernel may reach another device: no remote copies, remote signals or barrier semaphores. Data moves between devices by JAX's collectives and lax.ppermute only.
A program may use at most 128 MiB of HBM per device.

```python
import jax
import jax.numpy as jnp
from jax import lax

BLOCK = 512
SUMM = 4
HALF = 8
HD = 128
NB = 128
TOKENS = 65536
NSUM = 512
COLS = 1024


def draw_queries(key, part):
    key = jax.random.fold_in(key, 11)
    entries = jnp.clip(jax.random.normal(key, (TOKENS, 2, COLS), jnp.float32), -6.0, 6.0)
    return entries.astype(jnp.bfloat16)


def draw_key_rows(key, part):
    key = jax.random.fold_in(key, 17)
    entries = jnp.clip(jax.random.normal(key, (TOKENS, 2, COLS), jnp.float32), -6.0, 6.0)
    return entries.astype(jnp.bfloat16)


def draw_value_rows(key, part):
    key = jax.random.fold_in(key, 23)
    noise_key, scale_key = jax.random.split(key)
    head_frac = (jnp.arange(COLS) // HD).astype(jnp.float32) / HALF
    row_scale = jnp.exp(jax.random.uniform(scale_key, (TOKENS, 1, 1), jnp.float32, -1.15, 1.15))
    normal_part = jnp.clip(jax.random.normal(noise_key, (TOKENS, 2, COLS), jnp.float32), -3.0, 3.0)
    col_scale = 0.3 * 10.0 ** head_frac
    return (normal_part * col_scale[None, None, :] * row_scale).astype(jnp.bfloat16)


def steps_of(stream_key, dims, cuts, smallest, top_value):
    def one(dim, parts):
        steps = jax.random.uniform(jax.random.fold_in(jax.random.fold_in(stream_key, 6), dim), (parts,), jnp.float32, smallest / len(cuts), top_value / len(cuts))
        return jnp.repeat(jnp.exp(steps), dims[dim] // parts).reshape((-1,) + (1,) * (len(dims) - dim - 1))

    level = one(*cuts[0])
    for cut in cuts[1:]:
        level = level * one(*cut)
    return level


def normal_values(stream_key, dims, spread, bound, cuts=(), kind=jnp.bfloat16):
    values = spread * jax.random.normal(stream_key, dims, jnp.float32)
    if cuts:
        values = values * steps_of(stream_key, dims, cuts, -0.22, 0.18)
    return jnp.clip(values, -bound, bound).astype(kind)


def setup_inputs(seed: int = 0) -> dict:
    splits = jax.random.split(jax.random.key(seed), 5)
    queries = draw_queries(jax.random.fold_in(splits[4], 71), 0)
    key_rows = draw_key_rows(jax.random.fold_in(splits[4], 71), 0)
    value_rows = draw_value_rows(jax.random.fold_in(splits[4], 71), 0)
    cotangent = normal_values(splits[3], (TOKENS, 2, COLS), 1.0, 6.0, ((0, 128), (2, 2)))
    return dict(queries=queries, key_rows=key_rows, value_rows=value_rows, cotangent=cotangent)


epsilon = 1e-06

def to_wide(array):
    return array.astype(jnp.float32)

def softmax_rows(query_grp, key_grp, value_grp, visible):
    scores = jnp.einsum('gqd,gkd->gqk', to_wide(query_grp), to_wide(key_grp)) * HD ** (-0.5)
    scores = jnp.where(visible, scores, -jnp.inf)
    row_max = lax.optimization_barrier(jnp.max(scores, axis=-1, keepdims=True))
    expo_rows = jnp.exp(scores - row_max)
    probability = expo_rows / lax.optimization_barrier(jnp.sum(expo_rows, axis=-1, keepdims=True))
    weights = lax.optimization_barrier(probability.astype(jnp.bfloat16))
    attended = jnp.einsum('gqk,gkd->gqd', to_wide(weights), to_wide(value_grp)).astype(jnp.bfloat16)
    return (probability, weights, attended)

def back_scores(key_grp, value_grp, probability, attended, grad_attn):
    grad_prob = jnp.einsum('gqd,gkd->gqk', to_wide(grad_attn), to_wide(value_grp))
    row_dot = lax.optimization_barrier(jnp.sum(to_wide(grad_attn) * to_wide(attended), axis=-1, keepdims=True))
    grad_score = lax.optimization_barrier((probability * (grad_prob - row_dot) * HD ** (-0.5)).astype(jnp.bfloat16))
    grad_query = jnp.einsum('gqk,gkd->gqd', to_wide(grad_score), to_wide(key_grp))
    return (grad_score, grad_query)

def heads_grouped(array):
    return array.reshape(NB, BLOCK, HALF, HD).transpose(2, 1, 0, 3)

def heads_back(array):
    return array.transpose(2, 1, 0, 3).reshape(TOKENS, COLS)

def fixed_grouped(array):
    return array.reshape(NB, BLOCK, HALF, HD).transpose(0, 2, 1, 3)

def fixed_back(array):
    return array.transpose(0, 2, 1, 3).reshape(TOKENS, COLS)

def reference(queries, key_rows, value_rows, cotangent):
    causal = jnp.tril(jnp.ones((NB, NB), jnp.bool_))[None]
    strided_in = (heads_grouped(queries[:, 0]), heads_grouped(key_rows[:, 0]), heads_grouped(value_rows[:, 0]))

    def strided_forward(pieces):
        return softmax_rows(pieces[0], pieces[1], pieces[2], causal)[2]
    strided_attn = heads_back(lax.map(strided_forward, strided_in))
    summary_index = jnp.arange(NSUM, dtype=jnp.int32) // SUMM
    own_mask = jnp.tril(jnp.ones((BLOCK, BLOCK), jnp.bool_))
    fixed_query = fixed_grouped(queries[:, 1])
    fixed_key = fixed_grouped(key_rows[:, 1])
    fixed_value = fixed_grouped(value_rows[:, 1])
    summ_key = fixed_key[:, :, BLOCK - SUMM:].transpose(1, 0, 2, 3).reshape(HALF, NSUM, HD)
    summ_value = fixed_value[:, :, BLOCK - SUMM:].transpose(1, 0, 2, 3).reshape(HALF, NSUM, HD)
    block_numbers = jnp.arange(NB, dtype=jnp.int32)

    def fixed_inputs(block_index, key_block, value_block):
        key_cat = jnp.concatenate([key_block, summ_key], 1)
        value_cat = jnp.concatenate([value_block, summ_value], 1)
        earlier = jnp.broadcast_to((summary_index < block_index)[None], (BLOCK, NSUM))
        visible = jnp.concatenate([own_mask, earlier], 1)[None]
        return (key_cat, value_cat, visible)

    def fixed_forward(pieces):
        query_block, key_block, value_block, block_index = pieces
        key_cat, value_cat, visible = fixed_inputs(block_index, key_block, value_block)
        return softmax_rows(query_block, key_cat, value_cat, visible)[2]
    fixed_attn = fixed_back(lax.map(fixed_forward, (fixed_query, fixed_key, fixed_value, block_numbers)))
    attention = jnp.stack([strided_attn, fixed_attn], 1)
    attn_wide = to_wide(attention)
    cot_wide = to_wide(cotangent)
    square_sum = lax.optimization_barrier(jnp.sum(attn_wide * attn_wide, axis=(1, 2)))
    scaling = lax.rsqrt(square_sum / (2 * COLS) + epsilon)[:, None, None]
    normed = (attn_wide * scaling).astype(jnp.bfloat16)
    cross_sum = lax.optimization_barrier(jnp.sum(cot_wide * attn_wide, axis=(1, 2)))
    grad_attention = (scaling * cot_wide - attn_wide * scaling ** 3 * cross_sum[:, None, None] / (2 * COLS)).astype(jnp.bfloat16)

    def strided_backward(pieces):
        query_grp, key_grp, value_grp, grad_grp = pieces
        probability, weights, attended = softmax_rows(query_grp, key_grp, value_grp, causal)
        grad_score, grad_query = back_scores(key_grp, value_grp, probability, attended, grad_grp)
        grad_key = jnp.einsum('gqk,gqd->gkd', to_wide(grad_score), to_wide(query_grp))
        grad_value = jnp.einsum('gqk,gqd->gkd', to_wide(weights), to_wide(grad_grp))
        return (grad_query.astype(jnp.bfloat16), grad_key.astype(jnp.bfloat16), grad_value.astype(jnp.bfloat16))
    strided_grads = lax.map(strided_backward, strided_in + (heads_grouped(grad_attention[:, 0]),))
    strided_gq, strided_gk, strided_gv = [heads_back(piece) for piece in strided_grads]

    def fixed_step(totals, pieces):
        query_block, key_block, value_block, grad_block, block_index = pieces
        key_cat, value_cat, visible = fixed_inputs(block_index, key_block, value_block)
        probability, weights, attended = softmax_rows(query_block, key_cat, value_cat, visible)
        grad_score, grad_query = back_scores(key_cat, value_cat, probability, attended, grad_block)
        grad_key = jnp.einsum('gqk,gqd->gkd', to_wide(grad_score), to_wide(query_block))
        grad_value = jnp.einsum('gqk,gqd->gkd', to_wide(weights), to_wide(grad_block))
        totals = (totals[0] + grad_key[:, BLOCK:], totals[1] + grad_value[:, BLOCK:])
        return (totals, (grad_query.astype(jnp.bfloat16), grad_key[:, :BLOCK], grad_value[:, :BLOCK]))
    empty = jnp.zeros((HALF, NSUM, HD), jnp.float32)
    summ_totals, fixed_grads = lax.scan(fixed_step, (empty, empty), (fixed_query, fixed_key, fixed_value, fixed_grouped(grad_attention[:, 1]), block_numbers))

    def add_summary(own_part, summ_part):
        summ_blocks = summ_part.reshape(HALF, NB, SUMM, HD).transpose(1, 0, 2, 3)
        return fixed_back(own_part.at[:, :, BLOCK - SUMM:].add(summ_blocks).astype(jnp.bfloat16))
    grad_queries = jnp.stack([strided_gq, fixed_back(fixed_grads[0])], 1)
    grad_keys = jnp.stack([strided_gk, add_summary(fixed_grads[1], summ_totals[0])], 1)
    grad_values = jnp.stack([strided_gv, add_summary(fixed_grads[2], summ_totals[1])], 1)
    return (normed, grad_queries, grad_keys, grad_values)
```

```python
import jax
import jax.numpy as jnp
from jax import lax
from jax.sharding import PartitionSpec as P

BLOCK = 512
SUMM = 4
HD = 128
COLS = 1024


epsilon = 1e-06


def softmax_rows(query_grp, key_grp, value_grp, visible):
    scores = jnp.einsum(
        "gqd,gkd->gqk", query_grp, key_grp, preferred_element_type=jnp.float32
    ) * HD ** (-0.5)
    scores = jnp.where(visible, scores, -jnp.inf)
    row_max = jnp.max(scores, axis=-1, keepdims=True)
    expo_rows = jnp.exp(scores - row_max)
    probability = expo_rows / jnp.sum(expo_rows, axis=-1, keepdims=True)
    weights = probability.astype(jnp.bfloat16)
    attended = jnp.einsum(
        "gqk,gkd->gqd", weights, value_grp, preferred_element_type=jnp.float32
    ).astype(jnp.bfloat16)
    return (probability, weights, attended)


def back_scores(key_grp, value_grp, probability, attended, grad_attn):
    grad_prob = jnp.einsum("gqd,gkd->gqk", grad_attn, value_grp, preferred_element_type=jnp.float32)
    row_dot = jnp.sum(
        grad_attn.astype(jnp.float32) * attended.astype(jnp.float32), axis=-1, keepdims=True
    )
    grad_score = (probability * (grad_prob - row_dot) * HD ** (-0.5)).astype(jnp.bfloat16)
    grad_query = jnp.einsum("gqk,gkd->gqd", grad_score, key_grp, preferred_element_type=jnp.float32)
    return (grad_score, grad_query)


def normalize(attn_part, cot_part, square_sum, cross_sum):
    scaling = lax.rsqrt(square_sum / (2 * COLS) + epsilon)[..., None]
    attn_wide = attn_part.astype(jnp.float32)
    normed_part = (attn_wide * scaling).astype(jnp.bfloat16)
    grad_part = (
        scaling * cot_part.astype(jnp.float32)
        - attn_wide * scaling**3 * cross_sum[..., None] / (2 * COLS)
    ).astype(jnp.bfloat16)
    return (normed_part, grad_part)


def head_totals(square_part, cross_part):
    return lax.psum((square_part, cross_part), "head")


def shards(queries, key_rows, value_rows, cotangent):
    tok_rows, kind_count, width = queries.shape
    seq_count = lax.axis_size("seq")
    local_blocks = tok_rows // BLOCK
    all_blocks = local_blocks * seq_count
    offsets = BLOCK // seq_count
    heads_dev = width // HD
    groups = offsets * heads_dev
    fixed_groups = local_blocks * heads_dev
    first_block = lax.axis_index("seq") * local_blocks

    def blocked(array):
        return array.reshape(local_blocks, BLOCK, width)

    def grouped(array):
        return (
            array.reshape(all_blocks, offsets, heads_dev, HD)
            .transpose(1, 2, 0, 3)
            .reshape(groups, all_blocks, HD)
        )

    def ungrouped(array):
        return (
            array.reshape(offsets, heads_dev, all_blocks, HD)
            .transpose(2, 0, 1, 3)
            .reshape(all_blocks, offsets, width)
        )

    def head_major(array):
        return (
            array.reshape(local_blocks, BLOCK, heads_dev, HD)
            .transpose(0, 2, 1, 3)
            .reshape(fixed_groups, BLOCK, HD)
        )

    def token_major(array):
        return (
            array.reshape(local_blocks, heads_dev, BLOCK, HD)
            .transpose(0, 2, 1, 3)
            .reshape(local_blocks, BLOCK, width)
        )

    causal = jnp.tril(jnp.ones((all_blocks, all_blocks), jnp.bool_))[None]
    fixed_query = head_major(queries[:, 1])
    fixed_key = head_major(key_rows[:, 1])
    fixed_value = head_major(value_rows[:, 1])
    summary_keys = blocked(key_rows[:, 1])[:, BLOCK - SUMM :].reshape(local_blocks * SUMM, width)
    summary_values = blocked(value_rows[:, 1])[:, BLOCK - SUMM :].reshape(
        local_blocks * SUMM, width
    )
    first_send = jnp.concatenate(
        [queries[:, 0].reshape(seq_count, offsets, width), key_rows[:, 0].reshape(seq_count, offsets, width),
         value_rows[:, 0].reshape(seq_count, offsets, width),
         jnp.broadcast_to(summary_keys[None], (seq_count, SUMM, width)),
         jnp.broadcast_to(summary_values[None], (seq_count, SUMM, width))], 1)
    first_recv = lax.all_to_all(first_send, "seq", 0, 0, tiled=True)
    all_keys = first_recv[:, 12:16].reshape(seq_count * SUMM, width)
    all_values = first_recv[:, 16:20].reshape(seq_count * SUMM, width)
    total_summ = all_keys.shape[0]

    def spread(array):
        heads_first = array.reshape(total_summ, heads_dev, HD).transpose(1, 0, 2)
        return heads_first[None].reshape(fixed_groups, total_summ, HD)

    key_cat = jnp.concatenate([fixed_key, spread(all_keys)], 1)
    value_cat = jnp.concatenate([fixed_value, spread(all_values)], 1)
    own_mask = jnp.tril(jnp.ones((BLOCK, BLOCK), jnp.bool_))
    summ_block = jnp.arange(total_summ, dtype=jnp.int32) // SUMM
    earlier = (
        summ_block[None, :] < (first_block + jnp.arange(local_blocks, dtype=jnp.int32))[:, None]
    )
    visible = jnp.concatenate(
        [own_mask[None], jnp.broadcast_to(earlier[:, None, :], (local_blocks, BLOCK, total_summ))],
        2,
    )
    visible = jnp.broadcast_to(
        visible[:, None], (local_blocks, heads_dev, BLOCK, BLOCK + total_summ)
    ).reshape(fixed_groups, BLOCK, BLOCK + total_summ)
    fixed_prob, fixed_weights, fixed_attended = softmax_rows(
        fixed_query, key_cat, value_cat, visible
    )
    fixed_attn = token_major(fixed_attended)
    fixed_cot = blocked(cotangent[:, 1])
    fixed_wide = fixed_attn.astype(jnp.float32)
    fixed_square = jnp.sum(fixed_wide * fixed_wide, axis=-1)
    fixed_cross = jnp.sum(fixed_cot.astype(jnp.float32) * fixed_wide, axis=-1)
    strided_cot = blocked(cotangent[:, 0])
    query_off, key_off, value_off = (
        first_recv[:, 0:4],
        first_recv[:, 4:8],
        first_recv[:, 8:12],
    )
    query_grp, key_grp, value_grp = (grouped(query_off), grouped(key_off), grouped(value_off))
    strided_prob, strided_weights, strided_attended = softmax_rows(
        query_grp, key_grp, value_grp, causal
    )
    strided_attn = lax.all_to_all(
        ungrouped(strided_attended), "seq", split_axis=0, concat_axis=1, tiled=True
    )
    strided_wide = strided_attn.astype(jnp.float32)
    square_sum, cross_sum = head_totals(
        fixed_square + jnp.sum(strided_wide * strided_wide, axis=-1),
        fixed_cross + jnp.sum(strided_cot.astype(jnp.float32) * strided_wide, axis=-1),
    )
    strided_normed, strided_grad = normalize(strided_attn, strided_cot, square_sum, cross_sum)
    grad_grp = grouped(lax.all_to_all(strided_grad, "seq", split_axis=1, concat_axis=0, tiled=True))
    grad_score, grad_query = back_scores(
        key_grp, value_grp, strided_prob, strided_attended, grad_grp
    )
    grad_key = jnp.einsum("gqk,gqd->gkd", grad_score, query_grp, preferred_element_type=jnp.float32)
    grad_value = jnp.einsum(
        "gqk,gqd->gkd", strided_weights, grad_grp, preferred_element_type=jnp.float32
    )
    grad_query_off = ungrouped(grad_query.astype(jnp.bfloat16))
    grad_key_off = ungrouped(grad_key.astype(jnp.bfloat16))
    grad_value_off = ungrouped(grad_value.astype(jnp.bfloat16))
    fixed_normed, fixed_grad = normalize(fixed_attn, fixed_cot, square_sum, cross_sum)
    fixed_grad_grp = head_major(fixed_grad)
    grad_score, fixed_gq = back_scores(
        key_cat, value_cat, fixed_prob, fixed_attended, fixed_grad_grp
    )
    fixed_gk = jnp.einsum(
        "gqk,gqd->gkd", grad_score[:, :, :BLOCK], fixed_query, preferred_element_type=jnp.float32
    )
    fixed_gv = jnp.einsum(
        "gqk,gqd->gkd",
        fixed_weights[:, :, :BLOCK],
        fixed_grad_grp,
        preferred_element_type=jnp.float32,
    )
    summ_score = grad_score[:, :, BLOCK:].reshape(local_blocks, heads_dev, BLOCK, total_summ)
    summ_weights = fixed_weights[:, :, BLOCK:].reshape(local_blocks, heads_dev, BLOCK, total_summ)
    query_four = fixed_query.reshape(local_blocks, heads_dev, BLOCK, HD)
    grad_four = fixed_grad_grp.reshape(local_blocks, heads_dev, BLOCK, HD)
    key_term = jnp.einsum(
        "bhqs,bhqd->shd", summ_score, query_four, preferred_element_type=jnp.float32
    ).reshape(local_blocks * SUMM * lax.axis_size("seq"), width)
    value_term = jnp.einsum(
        "bhqs,bhqd->shd", summ_weights, grad_four, preferred_element_type=jnp.float32
    ).reshape(local_blocks * SUMM * lax.axis_size("seq"), width)
    last_send = jnp.concatenate(
        [grad_query_off, grad_key_off, grad_value_off,
         key_term.astype(jnp.bfloat16).reshape(seq_count, SUMM, width),
         value_term.astype(jnp.bfloat16).reshape(seq_count, SUMM, width)], 1)
    last_recv = lax.all_to_all(last_send, "seq", 0, 0, tiled=True)
    strided_gq, strided_gk, strided_gv = (last_recv[:, 0:4], last_recv[:, 4:8], last_recv[:, 8:12])
    summ_grads = jnp.sum(last_recv[:, 12:20].astype(jnp.float32), axis=0)
    summ_grads = summ_grads.reshape(2, SUMM, width).transpose(1, 0, 2)[None]
    key_total = token_major(fixed_gk).at[:, BLOCK - SUMM :].add(summ_grads[:, :, 0])
    value_total = token_major(fixed_gv).at[:, BLOCK - SUMM :].add(summ_grads[:, :, 1])

    def kinds_stacked(strided_part, fixed_part):
        return jnp.stack(
            [
                strided_part.reshape(tok_rows, width),
                fixed_part.reshape(tok_rows, width).astype(jnp.bfloat16),
            ],
            1,
        )

    return (
        kinds_stacked(strided_normed, fixed_normed),
        kinds_stacked(strided_gq, token_major(fixed_gq)),
        kinds_stacked(strided_gk, key_total),
        kinds_stacked(strided_gv, value_total),
    )


def solution(mesh):
    in_specs = (
        P("seq", None, "head"),
        P("seq", None, "head"),
        P("seq", None, "head"),
        P("seq", None, "head"),
    )
    out_specs = (
        P("seq", None, "head"),
        P("seq", None, "head"),
        P("seq", None, "head"),
        P("seq", None, "head"),
    )
    return jax.shard_map(shards, mesh=mesh, in_specs=in_specs, out_specs=out_specs, check_vma=False)
```

```python
import jax
import jax.numpy as jnp
from jax import lax
from jax.experimental import pallas as pl
from jax.experimental.pallas import tpu as pltpu
from jax.sharding import PartitionSpec as P

BLOCK = 512
SUMM = 4
HD = 128
COLS = 1024
NB = 128
HEADS = 4
OFFS = 4
WIDTH = HEADS * HD
PARTS = (8, 2, 4, 2)

epsilon = 1e-06
scale = HD ** (-0.5)
F32 = jnp.float32
BF16 = jnp.bfloat16


def iotas(shape):
    return (
        lax.broadcasted_iota(jnp.int32, shape, 0),
        lax.broadcasted_iota(jnp.int32, shape, 1),
    )


def one_hot(hit):
    return jnp.where(hit, 1.0, 0.0).astype(BF16)


def dot(a, b):
    return jnp.dot(a, b, preferred_element_type=F32)


def dot_nt(a, b):
    return lax.dot_general(a, b, (((1,), (1,)), ((), ())), preferred_element_type=F32)


def dot_tn(a, b):
    return lax.dot_general(a, b, (((0,), (0,)), ((), ())), preferred_element_type=F32)


def call(kernel, grid, in_specs, out_specs, out_shape, flops, nbytes, scratch=(), vmem=60):
    return pl.pallas_call(
        kernel,
        grid=(grid,),
        in_specs=in_specs,
        out_specs=out_specs,
        out_shape=out_shape,
        scratch_shapes=list(scratch),
        compiler_params=pltpu.CompilerParams(vmem_limit_bytes=vmem * 2**20),
        cost_estimate=pl.CostEstimate(flops=flops, bytes_accessed=nbytes, transcendentals=0),
    )


def spec(block, *index):
    return pl.BlockSpec(block, lambda i: tuple(i if at == "i" else at for at in index))


def pack_strided_kernel(q_ref, k_ref, v_ref, c_ref, send_ref, pick_ref):
    @pl.when(pl.program_id(0) == 0)
    def _():
        row, col = iotas((256, 512))
        home, array, offset = row >> 4, (row >> 2) & 3, row & 3
        pick_ref[...] = one_hot(col == array * 128 + (home * OFFS + offset) * 2)

    rows = jnp.concatenate(
        [ref[...].reshape(128, WIDTH) for ref in (q_ref, k_ref, v_ref, c_ref)], 0
    )
    send_ref[...] = dot(pick_ref[...], rows).astype(BF16).reshape(16, 16, WIDTH)


def pack_strided(arrays):
    return call(
        pack_strided_kernel,
        8,
        [spec((64, 2, WIDTH), "i", 0, 0)] * 4,
        spec((16, 16, WIDTH), "i", 0, 0),
        jax.ShapeDtypeStruct((NB, 16, WIDTH), BF16),
        10**9,
        6 * 2**20,
        [pltpu.VMEM((256, 512), BF16)],
    )(*arrays)


def pack_fixed_kernel(q_ref, k_ref, v_ref, c_ref, out_ref):
    row, col = iotas((64, 128))
    pick = one_hot(col == 2 * row + 1)
    for at, ref in enumerate((q_ref, k_ref, v_ref, c_ref)):
        out_ref[at] = dot(pick, ref[...].reshape(128, WIDTH)).astype(BF16)


def pack_fixed(arrays):
    return call(
        pack_fixed_kernel,
        8,
        [spec((64, 2, WIDTH), "i", 0, 0)] * 4,
        spec((4, 64, WIDTH), 0, "i", 0),
        jax.ShapeDtypeStruct((4, BLOCK, WIDTH), BF16),
        10**9,
        6 * 2**20,
    )(*arrays)


def fixed_probabilities(query, key, summ_key, seen):
    row, col = iotas((BLOCK, BLOCK))
    own = jnp.where(col <= row, dot_nt(query, key) * scale, -jnp.inf)
    far = jnp.where(seen > 0, dot_nt(query, summ_key) * scale, -jnp.inf)
    top = jnp.maximum(
        jnp.max(own, axis=-1, keepdims=True), jnp.max(far, axis=-1, keepdims=True)
    )
    own = jnp.exp(own - top)
    far = jnp.exp(far - top)
    total = jnp.sum(own, axis=-1, keepdims=True) + jnp.sum(far, axis=-1, keepdims=True)
    inverse = 1.0 / total
    return own * inverse, far * inverse


def fixed_forward_kernel(rows_ref, summ_ref, seen_ref, attn_ref, sums_ref):
    own, far = fixed_probabilities(rows_ref[0], rows_ref[1], summ_ref[:, :HD], seen_ref[...])
    attn = (
        dot(own.astype(BF16), rows_ref[2]) + dot(far.astype(BF16), summ_ref[:, HD:])
    ).astype(BF16)
    attn_ref[...] = attn
    wide = attn.astype(F32)
    square = jnp.sum(wide * wide, axis=-1, keepdims=True)
    cross = jnp.sum(wide * rows_ref[3].astype(F32), axis=-1, keepdims=True)
    lane = lax.broadcasted_iota(jnp.int32, (BLOCK, 8), 1)
    part = jnp.where(lane == 0, square, jnp.where(lane == 1, cross, 0.0))

    @pl.when(pl.program_id(0) == 0)
    def _():
        sums_ref[...] = part

    @pl.when(pl.program_id(0) > 0)
    def _():
        sums_ref[...] += part


def fixed_forward(rows, summ, seen):
    return call(
        fixed_forward_kernel,
        HEADS,
        [
            spec((4, BLOCK, HD), 0, 0, "i"),
            spec((BLOCK, 2 * HD), 0, "i"),
            spec((1, BLOCK), 0, 0),
        ],
        [spec((BLOCK, HD), 0, "i"), spec((BLOCK, 8), 0, 0)],
        [
            jax.ShapeDtypeStruct((BLOCK, WIDTH), BF16),
            jax.ShapeDtypeStruct((BLOCK, 8), F32),
        ],
        4 * 10**9,
        4 * 2**20,
    )(rows, summ, seen)


def swap_matrix():
    row, col = iotas((256, 256))
    return one_hot(col == ((row & 15) << 4) + (row >> 4))


def strided_forward_kernel(recv_ref, fixed_ref, grp_ref, attn_ref, prob_ref, sums_ref):
    swap = swap_matrix()
    for at in range(0, NB, 16):
        rows = recv_ref[at : at + 16].reshape(256, HD)
        grp_ref[0, :, :, at : at + 16, :] = (
            dot(swap, rows).astype(BF16).reshape(4, OFFS, 16, HD)
        )
    row, col = iotas((NB, NB))
    lane = lax.broadcasted_iota(jnp.int32, (NB, 16), 1)
    part = jnp.zeros((NB, 16), F32)
    for at in range(OFFS):
        scores = jnp.where(col <= row, dot_nt(grp_ref[0, 0, at], grp_ref[0, 1, at]) * scale, -jnp.inf)
        expo = jnp.exp(scores - jnp.max(scores, axis=-1, keepdims=True))
        prob = expo * (1.0 / jnp.sum(expo, axis=-1, keepdims=True))
        attn = dot(prob.astype(BF16), grp_ref[0, 2, at]).astype(BF16)
        prob_ref[0, at] = prob
        attn_ref[0, at] = attn
        wide = attn.astype(F32)
        square = jnp.sum(wide * wide, axis=-1, keepdims=True)
        cross = jnp.sum(wide * grp_ref[0, 3, at].astype(F32), axis=-1, keepdims=True)
        part += jnp.where(lane == 8 + at, square, jnp.where(lane == 12 + at, cross, 0.0))

    @pl.when(pl.program_id(0) == 0)
    def _():
        sums_ref[...] = fixed_ref[...] + part

    @pl.when(pl.program_id(0) > 0)
    def _():
        sums_ref[...] += part


def strided_forward(recv, fixed_sums):
    return call(
        strided_forward_kernel,
        HEADS,
        [spec((NB, 16, HD), 0, 0, "i"), spec((NB, 16), 0, 0)],
        [
            spec((1, 4, OFFS, NB, HD), "i", 0, 0, 0, 0),
            spec((1, OFFS, NB, HD), "i", 0, 0, 0),
            spec((1, OFFS, NB, NB), "i", 0, 0, 0),
            spec((NB, 16), 0, 0),
        ],
        [
            jax.ShapeDtypeStruct((HEADS, 4, OFFS, NB, HD), BF16),
            jax.ShapeDtypeStruct((HEADS, OFFS, NB, HD), BF16),
            jax.ShapeDtypeStruct((HEADS, OFFS, NB, NB), F32),
            jax.ShapeDtypeStruct((NB, 16), F32),
        ],
        10**9,
        6 * 2**20,
    )(recv, fixed_sums)


def normalize(wide, cotangent, square, cross):
    scaling = lax.rsqrt(square / (2 * COLS) + epsilon)
    normed = (wide * scaling).astype(BF16)
    grad = (
        scaling * cotangent.astype(F32) - wide * (scaling * scaling * scaling * cross / (2 * COLS))
    ).astype(BF16)
    return normed, grad, jnp.sum(grad.astype(F32) * wide, axis=-1, keepdims=True)


def strided_backward_kernel(grp_ref, attn_ref, prob_ref, mine_ref, other_ref, send_ref, out_ref):
    total = mine_ref[...] + other_ref[...]
    for at in range(OFFS):
        wide = attn_ref[0, at].astype(F32)
        normed, grad, row_dot = normalize(
            wide, grp_ref[0, 3, at], total[:, at : at + 1], total[:, 4 + at : 5 + at]
        )
        prob = prob_ref[0, at]
        grad_prob = dot_nt(grad, grp_ref[0, 2, at])
        grad_score = (prob * (grad_prob - row_dot) * scale).astype(BF16)
        out_ref[0, at] = normed
        out_ref[1, at] = dot(grad_score, grp_ref[0, 1, at]).astype(BF16)
        out_ref[2, at] = dot_tn(grad_score, grp_ref[0, 0, at]).astype(BF16)
        out_ref[3, at] = dot_tn(prob.astype(BF16), grad).astype(BF16)
    swap = swap_matrix()
    for at in range(0, NB, 16):
        rows = out_ref[:, :, at : at + 16, :].reshape(256, HD)
        send_ref[at : at + 16] = dot(swap, rows).astype(BF16).reshape(16, 16, HD)


def strided_backward(grp, attn, prob, mine, other):
    return call(
        strided_backward_kernel,
        HEADS,
        [
            spec((1, 4, OFFS, NB, HD), "i", 0, 0, 0, 0),
            spec((1, OFFS, NB, HD), "i", 0, 0, 0),
            spec((1, OFFS, NB, NB), "i", 0, 0, 0),
            spec((NB, 16), 0, 0),
            spec((NB, 16), 0, 0),
        ],
        spec((NB, 16, HD), 0, 0, "i"),
        jax.ShapeDtypeStruct((NB, 16, WIDTH), BF16),
        10**9,
        6 * 2**20,
        [pltpu.VMEM((4, OFFS, NB, HD), BF16)],
    )(grp, attn, prob, mine, other)


def fixed_backward_kernel(rows_ref, summ_ref, seen_ref, attn_ref, sums_ref, out_ref, part_ref):
    query, key, value = rows_ref[0], rows_ref[1], rows_ref[2]
    summ_key, summ_value = summ_ref[:, :HD], summ_ref[:, HD:]
    own, far = fixed_probabilities(query, key, summ_key, seen_ref[...])
    wide = attn_ref[...].astype(F32)
    normed, grad, row_dot = normalize(wide, rows_ref[3], sums_ref[:, 0:1], sums_ref[:, 1:2])
    out_ref[0] = normed
    own_score = (own * (dot_nt(grad, value) - row_dot) * scale).astype(BF16)
    far_score = (far * (dot_nt(grad, summ_value) - row_dot) * scale).astype(BF16)
    out_ref[1] = (dot(own_score, key) + dot(far_score, summ_key)).astype(BF16)
    grad_key = dot_tn(own_score, query)
    grad_value = dot_tn(own.astype(BF16), grad)
    out_ref[2] = grad_key.astype(BF16)
    out_ref[3] = grad_value.astype(BF16)
    part_ref[:, :HD] = dot_tn(far_score, query)
    part_ref[:, HD:] = dot_tn(far.astype(BF16), grad)
    row = lax.broadcasted_iota(jnp.int32, (8, HD), 0)
    for at, grads in ((0, grad_key), (HD, grad_value)):
        tail = pltpu.roll(grads[BLOCK - 8 :], SUMM, 0)
        part_ref[0:8, at : at + HD] += jnp.where(row < SUMM, tail, 0.0)


def fixed_backward(rows, summ, seen, attn, sums):
    return call(
        fixed_backward_kernel,
        HEADS,
        [
            spec((4, BLOCK, HD), 0, 0, "i"),
            spec((BLOCK, 2 * HD), 0, "i"),
            spec((1, BLOCK), 0, 0),
            spec((BLOCK, HD), 0, "i"),
            spec((BLOCK, 2), 0, 0),
        ],
        [spec((4, BLOCK, HD), 0, 0, "i"), spec((BLOCK, 2 * HD), 0, "i")],
        [
            jax.ShapeDtypeStruct((4, BLOCK, WIDTH), BF16),
            jax.ShapeDtypeStruct((BLOCK, 2 * WIDTH), F32),
        ],
        8 * 10**9,
        8 * 2**20,
    )(rows, summ, seen, attn, sums)


def unpack_kernel(recv_ref, fixed_ref, *refs):
    out_refs, pick_ref = refs[:4], refs[4]

    @pl.when(pl.program_id(0) == 0)
    def _():
        row, col = iotas((512, 512))
        array, token, kind = row >> 7, (row & 127) >> 1, row & 1
        strided = ((token >> 2) << 4) + array * OFFS + (token & 3)
        fixed = 256 + array * 64 + token
        pick_ref[...] = one_hot(col == jnp.where(kind == 0, strided, fixed))

    rows = jnp.concatenate(
        [recv_ref[...].reshape(256, WIDTH), fixed_ref[...].reshape(256, WIDTH)], 0
    )
    for at, ref in enumerate(out_refs):
        picked = dot(pick_ref[at * 128 : (at + 1) * 128], rows).astype(BF16)
        ref[...] = picked.reshape(64, 2, WIDTH)


def unpack(recv, fixed):
    return call(
        unpack_kernel,
        8,
        [spec((16, 16, WIDTH), "i", 0, 0), spec((4, 64, WIDTH), 0, "i", 0)],
        [spec((64, 2, WIDTH), "i", 0, 0)] * 4,
        [jax.ShapeDtypeStruct((BLOCK, 2, WIDTH), BF16)] * 4,
        2 * 10**9,
        8 * 2**20,
        [pltpu.VMEM((512, 512), BF16)],
    )(recv, fixed)


def place(index):
    coords = []
    for size in PARTS[::-1]:
        coords.append(index % size)
        index = index // size
    return coords[::-1]


def joined(coords):
    index = 0
    for size, at in zip(PARTS, coords):
        index = index * size + at
    return index


def shift(array, part, step):
    perm = []
    for source in range(NB):
        coords = place(source)
        coords[part] = (coords[part] + step) % PARTS[part]
        perm.append((source, joined(coords)))
    return lax.ppermute(array, "seq", perm)


ROUNDS = (
    ((0, 1, 1), (0, -1, 1)),
    ((0, 3, 3), (0, -3, 2)),
    ((2, 1, 8), (2, -1, 8), (2, 2, 8)),
    ((1, 1, 32),),
    ((3, 1, 64),),
)


def gather_summaries(held, rounds):
    for steps in rounds:
        moved = [shift(held[: slots * SUMM], part, step) for part, step, slots in steps]
        held = jnp.concatenate([held] + moved, 0)
    return held


def scatter_summaries(parts):
    for steps in ROUNDS[::-1]:
        kept = parts.shape[0] - SUMM * sum(slots for _, _, slots in steps)
        total, at = parts[:kept], kept
        for part, step, slots in steps:
            rows = slots * SUMM
            moved = shift(parts[at : at + rows].astype(BF16), part, -step).astype(F32)
            total = total + jnp.pad(moved, ((0, kept - rows), (0, 0)))
            at += rows
        parts = total
    return parts


def slot_blocks(me):
    back = [(0,) * len(PARTS)]
    for steps in ROUNDS:
        back = back + [
            tuple(by + step * (at == part) for at, by in enumerate(slot))
            for part, step, slots in steps
            for slot in back[:slots]
        ]
    back = jnp.array(back, jnp.int32)
    coords = [(at - back[:, n]) % size for n, (at, size) in enumerate(zip(place(me), PARTS))]
    return joined(coords)


def shards(queries, key_rows, value_rows, cotangent):
    me = lax.axis_index("seq")
    arrays = (queries, key_rows, value_rows, cotangent)
    send = pack_strided(arrays)
    tails = [a[BLOCK - SUMM :, 1].reshape(SUMM, HEADS, 1, HD) for a in (key_rows, value_rows)]
    own_summ = jnp.concatenate(tails, 2).reshape(SUMM, 2 * WIDTH)
    summ = gather_summaries(own_summ, ROUNDS[:2])
    send, summ = lax.optimization_barrier((send, summ))
    recv = lax.all_to_all(send, "seq", 0, 0, tiled=True)
    summ = gather_summaries(summ, ROUNDS[2:])
    seen = jnp.repeat((slot_blocks(me) < me).astype(jnp.int32), SUMM)[None]
    rows = pack_fixed(arrays)
    fixed_attn, fixed_sums = fixed_forward(rows, summ, seen)
    fixed_send = fixed_sums[:, :2].reshape(NB, OFFS, 2).transpose(0, 2, 1).reshape(NB, 8)
    fixed_send = jnp.pad(fixed_send, ((0, 0), (0, 8)))
    grp, attn, prob, sums = strided_forward(recv, fixed_send)
    sums_other = lax.ppermute(sums, "head", [(0, 1), (1, 0)])
    sums_both = jnp.broadcast_to(sums[:, None], (NB, 2, 16)).reshape(2 * NB, 16)
    sums_in = lax.all_to_all(sums_both, ("seq", "head"), 0, 0, tiled=True).reshape(NB, 2, 16)
    mine = jnp.sum(sums_in, 1)
    other = sums + sums_other
    other = jnp.concatenate([other[:, 8:], other[:, :8]], 1)
    send_back = strided_backward(grp, attn, prob, mine, other)
    recv_back = lax.all_to_all(send_back, "seq", 0, 0, tiled=True)
    block_sums = (mine + other)[:, 8:].reshape(NB, 2, OFFS).transpose(0, 2, 1).reshape(BLOCK, 2)
    fixed_out, parts = fixed_backward(rows, summ, seen, fixed_attn, block_sums)
    totals = scatter_summaries(parts).astype(BF16).reshape(SUMM, HEADS, 2, HD)
    totals = totals.transpose(2, 0, 1, 3).reshape(2, SUMM, WIDTH)
    fixed_out = lax.dynamic_update_slice(fixed_out, totals, (2, BLOCK - SUMM, 0))
    return tuple(unpack(recv_back, fixed_out))


def solution(mesh):
    specs = (P("seq", None, "head"),) * 4
    return jax.shard_map(shards, mesh=mesh, in_specs=specs, out_specs=specs, check_vma=False)
```

```python
import jax
import jax.numpy as jnp
from jax import lax
from jax.experimental import pallas as pl
from jax.experimental.pallas import tpu as pltpu
from jax.sharding import PartitionSpec as P

BLOCK = 512
SUMM = 4
HD = 128
COLS = 1024
NB = 128
HEADS = 4
OFFS = 4
WIDTH = HEADS * HD
PARTS = (8, 2, 4, 2)
VMEM3, VMEM4, VMEM6 = 32, 32, 32

epsilon = 1e-06
scale = HD ** (-0.5)
F32 = jnp.float32
BF16 = jnp.bfloat16


def iotas(shape):
    return (
        lax.broadcasted_iota(jnp.int32, shape, 0),
        lax.broadcasted_iota(jnp.int32, shape, 1),
    )


def one_hot(hit):
    return jnp.where(hit, 1.0, 0.0).astype(BF16)


def dot(a, b):
    return jnp.dot(a, b, preferred_element_type=F32)


def dot_nt(a, b):
    return lax.dot_general(a, b, (((1,), (1,)), ((), ())), preferred_element_type=F32)


def dot_tn(a, b):
    return lax.dot_general(a, b, (((0,), (0,)), ((), ())), preferred_element_type=F32)


def batch_dot(a, b, left, right):
    return lax.dot_general(
        a, b, (((left,), (right,)), ((0,), (0,))), preferred_element_type=F32
    )


def flat(array):
    split = array.reshape(BLOCK, 2, HEADS, HD).transpose(0, 2, 1, 3)
    return split.reshape(BLOCK * HEADS * 2, HD)


def unflat(rows):
    return rows.reshape(BLOCK, HEADS, 2, HD).transpose(0, 2, 1, 3).reshape(BLOCK, 2, WIDTH)


def call(kernel, grid, in_specs, out_specs, out_shape, flops, nbytes, scratch=(), vmem=60):
    return pl.pallas_call(
        kernel,
        grid=(grid,),
        in_specs=in_specs,
        out_specs=out_specs,
        out_shape=out_shape,
        scratch_shapes=list(scratch),
        compiler_params=pltpu.CompilerParams(vmem_limit_bytes=vmem * 2**20),
        cost_estimate=pl.CostEstimate(flops=flops, bytes_accessed=nbytes, transcendentals=0),
    )


def spec(block, *index):
    return pl.BlockSpec(block, lambda i: tuple(i if at == "i" else at for at in index))


def pack_strided_kernel(q_ref, k_ref, v_ref, c_ref, send_ref, pick_ref):
    @pl.when(pl.program_id(0) == 0)
    def _():
        row, col = iotas((128, 256))
        home, head, array, offset = row >> 6, (row >> 4) & 3, (row >> 2) & 3, row & 3
        pick_ref[...] = one_hot(col == array * 64 + ((home * OFFS + offset) * HEADS + head) * 2)

    pick = pick_ref[...]
    for at in range(0, 32, 2):
        pair = [
            jnp.concatenate([ref[64 * n : 64 * (n + 1)] for n in (at, at + 1)], 1)
            for ref in (q_ref, k_ref, v_ref, c_ref)
        ]
        picked = dot(pick, jnp.concatenate(pair, 0)).astype(BF16)
        for n in range(2):
            for home in range(2):
                for head in range(HEADS):
                    row = home * 64 + head * 16
                    send_ref[2 * (at + n) + home, :, head * HD : (head + 1) * HD] = picked[
                        row : row + 16, n * HD : (n + 1) * HD
                    ]


def pack_strided(arrays):
    return call(
        pack_strided_kernel,
        2,
        [spec((2048, HD), "i", 0)] * 4,
        spec((64, 16, WIDTH), "i", 0, 0),
        jax.ShapeDtypeStruct((NB, 16, WIDTH), BF16),
        10**9,
        6 * 2**20,
        [pltpu.VMEM((128, 256), BF16)],
    )(*arrays)


def pack_fixed_kernel(q_ref, k_ref, v_ref, c_ref, out_ref):
    row, col = iotas((64, 128))
    pick = one_hot(col == ((row & 15) * HEADS + (row >> 4)) * 2 + 1)
    for at in range(16):
        rows = [ref[128 * at : 128 * (at + 1)] for ref in (q_ref, k_ref, v_ref, c_ref)]
        picked = dot(pick, jnp.concatenate(rows, 1)).astype(BF16)
        for array in range(4):
            for head in range(HEADS):
                out_ref[array, 16 * at : 16 * (at + 1), head * HD : (head + 1) * HD] = picked[
                    16 * head : 16 * (head + 1), array * HD : (array + 1) * HD
                ]


def pack_fixed(arrays):
    return call(
        pack_fixed_kernel,
        2,
        [spec((2048, HD), "i", 0)] * 4,
        spec((4, BLOCK // 2, WIDTH), 0, "i", 0),
        jax.ShapeDtypeStruct((4, BLOCK, WIDTH), BF16),
        10**9,
        6 * 2**20,
    )(*arrays)


def fixed_probabilities(query, key, summ_key, seen):
    row, col = iotas((BLOCK, BLOCK))
    own = jnp.where(col <= row, dot_nt(query, key) * scale, -jnp.inf)
    far = jnp.where(seen > 0, dot_nt(query, summ_key) * scale, -jnp.inf)
    top = jnp.maximum(
        jnp.max(own, axis=-1, keepdims=True), jnp.max(far, axis=-1, keepdims=True)
    )
    own = jnp.exp(own - top)
    far = jnp.exp(far - top)
    total = jnp.sum(own, axis=-1, keepdims=True) + jnp.sum(far, axis=-1, keepdims=True)
    inverse = 1.0 / total
    return own * inverse, far * inverse


def fixed_forward_kernel(rows_ref, summ_ref, seen_ref, attn_ref, sums_ref):
    own, far = fixed_probabilities(rows_ref[0], rows_ref[1], summ_ref[:, :HD], seen_ref[...])
    attn = (
        dot(own.astype(BF16), rows_ref[2]) + dot(far.astype(BF16), summ_ref[:, HD:])
    ).astype(BF16)
    attn_ref[...] = attn
    wide = attn.astype(F32)
    square = jnp.sum(wide * wide, axis=-1, keepdims=True)
    cross = jnp.sum(wide * rows_ref[3].astype(F32), axis=-1, keepdims=True)
    lane = lax.broadcasted_iota(jnp.int32, (BLOCK, 8), 1)
    part = jnp.where(lane == 0, square, jnp.where(lane == 1, cross, 0.0))

    @pl.when(pl.program_id(0) == 0)
    def _():
        sums_ref[...] = part

    @pl.when(pl.program_id(0) > 0)
    def _():
        sums_ref[...] += part


def fixed_forward(rows, summ, seen):
    return call(
        fixed_forward_kernel,
        HEADS,
        [
            spec((4, BLOCK, HD), 0, 0, "i"),
            spec((BLOCK, 2 * HD), 0, "i"),
            spec((1, BLOCK), 0, 0),
        ],
        [spec((BLOCK, HD), 0, "i"), spec((BLOCK, 8), 0, 0)],
        [
            jax.ShapeDtypeStruct((BLOCK, WIDTH), BF16),
            jax.ShapeDtypeStruct((BLOCK, 8), F32),
        ],
        4 * 10**9,
        4 * 2**20,
    )(rows, summ, seen)


def swap_matrix():
    row, col = iotas((256, 256))
    return one_hot(col == ((row & 15) << 4) + (row >> 4))


def strided_forward_kernel(recv_ref, fixed_ref, grp_ref, attn_ref, prob_ref, sums_ref, send_ref):
    swap = swap_matrix()
    for at in range(0, NB, 16):
        rows = dot(swap, recv_ref[at : at + 16].reshape(256, WIDTH)).astype(BF16)
        for head in range(HEADS):
            grp_ref[head, :, :, at : at + 16, :] = rows[:, head * HD : (head + 1) * HD].reshape(
                4, OFFS, 16, HD
            )
    row, col = iotas((NB, NB))
    square, cross = 0.0, 0.0
    for head in range(HEADS):
        scores = batch_dot(grp_ref[head, 0], grp_ref[head, 1], 2, 2) * scale
        scores = jnp.where((col <= row)[None], scores, -jnp.inf)
        expo = jnp.exp(scores - jnp.max(scores, axis=-1, keepdims=True))
        prob = expo * (1.0 / jnp.sum(expo, axis=-1, keepdims=True))
        attn = batch_dot(prob.astype(BF16), grp_ref[head, 2], 2, 1).astype(BF16)
        prob_ref[head] = prob
        attn_ref[head] = attn
        wide = attn.astype(F32)
        square += wide * wide
        cross += wide * grp_ref[head, 3].astype(F32)
    square = jnp.sum(square, axis=-1, keepdims=True)
    cross = jnp.sum(cross, axis=-1, keepdims=True)
    lane = lax.broadcasted_iota(jnp.int32, (NB, HD), 1)
    part = fixed_ref[...]
    for at in range(OFFS):
        part += jnp.where(lane == 8 + at, square[at], jnp.where(lane == 12 + at, cross[at], 0.0))
    sums_ref[...] = part
    for head in range(2):
        send_ref[head * NB : (head + 1) * NB] = part.reshape(NB, 1, HD)


def strided_forward(recv, fixed_sums):
    return call(
        strided_forward_kernel,
        1,
        [spec((NB, 16, WIDTH), 0, 0, 0), spec((NB, HD), 0, 0)],
        [
            spec((HEADS, 4, OFFS, NB, HD), 0, 0, 0, 0, 0),
            spec((HEADS, OFFS, NB, HD), 0, 0, 0, 0),
            spec((HEADS, OFFS, NB, NB), 0, 0, 0, 0),
            spec((NB, HD), 0, 0),
            spec((2 * NB, 1, HD), 0, 0, 0),
        ],
        [
            jax.ShapeDtypeStruct((HEADS, 4, OFFS, NB, HD), BF16),
            jax.ShapeDtypeStruct((HEADS, OFFS, NB, HD), BF16),
            jax.ShapeDtypeStruct((HEADS, OFFS, NB, NB), F32),
            jax.ShapeDtypeStruct((NB, HD), F32),
            jax.ShapeDtypeStruct((2 * NB, 1, HD), F32),
        ],
        10**9,
        6 * 2**20,
        vmem=VMEM3,
    )(recv, fixed_sums)


def normalize(wide, cotangent, square, cross):
    scaling = lax.rsqrt(square / (2 * COLS) + epsilon)
    normed = (wide * scaling).astype(BF16)
    grad = (
        scaling * cotangent.astype(F32) - wide * (scaling * scaling * scaling * cross / (2 * COLS))
    ).astype(BF16)
    return normed, grad, jnp.sum(grad.astype(F32) * wide, axis=-1, keepdims=True)


def strided_backward_kernel(
    grp_ref, attn_ref, prob_ref, sums_ref, other_ref, recv_ref, send_ref, block_ref, out_ref
):
    both = sums_ref[:, :16] + other_ref[...]
    moved = (recv_ref[:NB] + recv_ref[NB:]).reshape(NB, HD)
    block_ref[...] = both[:, :8] + moved[:, 8:16]
    total = both[:, 8:] + moved[:, :8]
    square = jnp.stack([total[:, at : at + 1] for at in range(OFFS)])
    cross = jnp.stack([total[:, OFFS + at : OFFS + at + 1] for at in range(OFFS)])
    for head in range(HEADS):
        wide = attn_ref[head].astype(F32)
        normed, grad, row_dot = normalize(wide, grp_ref[head, 3], square, cross)
        prob = prob_ref[head]
        grad_prob = batch_dot(grad, grp_ref[head, 2], 2, 2)
        grad_score = (prob * (grad_prob - row_dot) * scale).astype(BF16)
        out_ref[head, 0] = normed
        out_ref[head, 1] = batch_dot(grad_score, grp_ref[head, 1], 2, 1).astype(BF16)
        out_ref[head, 2] = batch_dot(grad_score, grp_ref[head, 0], 1, 1).astype(BF16)
        out_ref[head, 3] = batch_dot(prob.astype(BF16), grad, 1, 1).astype(BF16)
    swap = swap_matrix()
    for at in range(0, NB, 16):
        rows = [out_ref[head, :, :, at : at + 16, :].reshape(256, HD) for head in range(HEADS)]
        moved = dot(swap, jnp.concatenate(rows, 1)).astype(BF16)
        send_ref[at : at + 16] = moved.reshape(16, 16, WIDTH)


def strided_backward(grp, attn, prob, sums, other, recv):
    return call(
        strided_backward_kernel,
        1,
        [
            spec((HEADS, 4, OFFS, NB, HD), 0, 0, 0, 0, 0),
            spec((HEADS, OFFS, NB, HD), 0, 0, 0, 0),
            spec((HEADS, OFFS, NB, NB), 0, 0, 0, 0),
            spec((NB, HD), 0, 0),
            spec((NB, 16), 0, 0),
            spec((2 * NB, 1, HD), 0, 0, 0),
        ],
        [spec((NB, 16, WIDTH), 0, 0, 0), spec((NB, 8), 0, 0)],
        [
            jax.ShapeDtypeStruct((NB, 16, WIDTH), BF16),
            jax.ShapeDtypeStruct((NB, 8), F32),
        ],
        10**9,
        6 * 2**20,
        [pltpu.VMEM((HEADS, 4, OFFS, NB, HD), BF16)],
        vmem=VMEM4,
    )(grp, attn, prob, sums, other, recv)


def fixed_backward_kernel(rows_ref, summ_ref, seen_ref, attn_ref, sums_ref, out_ref, part_ref):
    query, key, value = rows_ref[0], rows_ref[1], rows_ref[2]
    summ_key, summ_value = summ_ref[:, :HD], summ_ref[:, HD:]
    own, far = fixed_probabilities(query, key, summ_key, seen_ref[...])
    wide = attn_ref[...].astype(F32)
    normed, grad, row_dot = normalize(wide, rows_ref[3], sums_ref[:, 0:1], sums_ref[:, 1:2])
    out_ref[0] = normed
    own_score = (own * (dot_nt(grad, value) - row_dot) * scale).astype(BF16)
    far_score = (far * (dot_nt(grad, summ_value) - row_dot) * scale).astype(BF16)
    out_ref[1] = (dot(own_score, key) + dot(far_score, summ_key)).astype(BF16)
    grad_key = dot_tn(own_score, query)
    grad_value = dot_tn(own.astype(BF16), grad)
    out_ref[2] = grad_key.astype(BF16)
    out_ref[3] = grad_value.astype(BF16)
    part_ref[:, :HD] = dot_tn(far_score, query)
    part_ref[:, HD:] = dot_tn(far.astype(BF16), grad)
    row = lax.broadcasted_iota(jnp.int32, (8, HD), 0)
    for at, grads in ((0, grad_key), (HD, grad_value)):
        tail = pltpu.roll(grads[BLOCK - 8 :], SUMM, 0)
        part_ref[0:8, at : at + HD] += jnp.where(row < SUMM, tail, 0.0)


def fixed_backward(rows, summ, seen, attn, sums):
    return call(
        fixed_backward_kernel,
        HEADS,
        [
            spec((4, BLOCK, HD), 0, 0, "i"),
            spec((BLOCK, 2 * HD), 0, "i"),
            spec((1, BLOCK), 0, 0),
            spec((BLOCK, HD), 0, "i"),
            spec((BLOCK, 2), 0, 0),
        ],
        [spec((4, BLOCK, HD), 0, 0, "i"), spec((BLOCK, 2 * HD), 0, "i")],
        [
            jax.ShapeDtypeStruct((4, BLOCK, WIDTH), BF16),
            jax.ShapeDtypeStruct((BLOCK, 2 * WIDTH), F32),
        ],
        8 * 10**9,
        8 * 2**20,
    )(rows, summ, seen, attn, sums)


def unpack_kernel(recv_ref, fixed_ref, tail_ref, *refs):
    out_refs, strided_ref, own_ref = refs[:4], refs[4], refs[5]

    @pl.when(pl.program_id(0) == 0)
    def _():
        row, col = iotas((512, 256))
        array, token, head, kind = row >> 7, (row >> 3) & 15, (row >> 1) & 3, row & 1
        source = (token >> 2) * 64 + head * 16 + array * OFFS + (token & 3)
        strided_ref[...] = one_hot((kind == 0) & (col == source))
        row, col = iotas((128, 64))
        token, head, kind = row >> 3, (row >> 1) & 3, row & 1
        own_ref[...] = one_hot((kind == 1) & (col == head * 16 + token))

    last = pl.program_id(0) == 1
    end = lax.broadcasted_iota(jnp.int32, (16, WIDTH), 0) >= 16 - SUMM
    for at in range(0, 16, 2):
        rows = [
            jnp.concatenate(
                [
                    recv_ref[4 * n + home, :, head * HD : (head + 1) * HD]
                    for home in range(4)
                    for head in range(HEADS)
                ],
                0,
            )
            for n in (at, at + 1)
        ]
        strided = dot(strided_ref[...], jnp.concatenate(rows, 1))
        for n in range(2):
            tile = 16 * (at + n)
            fixed = [fixed_ref[array, tile : tile + 16] for array in range(4)]
            if tile == BLOCK // 2 - 16:
                for array in (2, 3):
                    fixed[array] = jnp.where(end & last, tail_ref[array - 2], fixed[array])
            rows = [
                jnp.concatenate([part[:, head * HD : (head + 1) * HD] for part in fixed], 1)
                for head in range(HEADS)
            ]
            own = dot(own_ref[...], jnp.concatenate(rows, 0))
            for array in range(4):
                out_refs[array][8 * tile : 8 * tile + 128] = (
                    strided[array * 128 : (array + 1) * 128, n * HD : (n + 1) * HD]
                    + own[:, array * HD : (array + 1) * HD]
                ).astype(BF16)


def unpack(recv, fixed, tail):
    rows = call(
        unpack_kernel,
        2,
        [
            spec((NB // 2, 16, WIDTH), "i", 0, 0),
            spec((4, BLOCK // 2, WIDTH), 0, "i", 0),
            spec((2, 16, WIDTH), 0, 0, 0),
        ],
        [spec((BLOCK * 4, HD), "i", 0)] * 4,
        [jax.ShapeDtypeStruct((BLOCK * 8, HD), BF16)] * 4,
        2 * 10**9,
        8 * 2**20,
        [pltpu.VMEM((512, 256), BF16), pltpu.VMEM((128, 64), BF16)],
        vmem=VMEM6,
    )(recv, fixed, tail)
    return tuple(unflat(array) for array in rows)


def place(index):
    coords = []
    for size in PARTS[::-1]:
        coords.append(index % size)
        index = index // size
    return coords[::-1]


def joined(coords):
    index = 0
    for size, at in zip(PARTS, coords):
        index = index * size + at
    return index


def shift(array, part, step):
    perm = []
    for source in range(NB):
        coords = place(source)
        coords[part] = (coords[part] + step) % PARTS[part]
        perm.append((source, joined(coords)))
    return lax.ppermute(array, "seq", perm)


ROUNDS = (
    ((0, 1, 1), (0, -1, 1)),
    ((0, 3, 3), (0, -3, 2)),
    ((2, 1, 8), (2, -1, 8), (2, 2, 8)),
    ((1, 1, 32),),
    ((3, 1, 64),),
)


def gather_summaries(held, rounds):
    for steps in rounds:
        moved = [shift(held[: slots * SUMM], part, step) for part, step, slots in steps]
        held = jnp.concatenate([held] + moved, 0)
    return held


def scatter_summaries(parts):
    for steps in ROUNDS[::-1]:
        kept = parts.shape[0] - SUMM * sum(slots for _, _, slots in steps)
        total, at = parts[:kept], kept
        for part, step, slots in steps:
            rows = slots * SUMM
            moved = shift(parts[at : at + rows].astype(BF16), part, -step).astype(F32)
            total = total + jnp.pad(moved, ((0, kept - rows), (0, 0)))
            at += rows
        parts = total
    return parts


def slot_blocks(me):
    back = [(0,) * len(PARTS)]
    for steps in ROUNDS:
        back = back + [
            tuple(by + step * (at == part) for at, by in enumerate(slot))
            for part, step, slots in steps
            for slot in back[:slots]
        ]
    back = jnp.array(back, jnp.int32)
    coords = [(at - back[:, n]) % size for n, (at, size) in enumerate(zip(place(me), PARTS))]
    return joined(coords)


def shards(queries, key_rows, value_rows, cotangent):
    me = lax.axis_index("seq")
    arrays = tuple(flat(array) for array in (queries, key_rows, value_rows, cotangent))
    send = pack_strided(arrays)
    tails = [a[BLOCK - SUMM :, 1].reshape(SUMM, HEADS, 1, HD) for a in (key_rows, value_rows)]
    own_summ = jnp.concatenate(tails, 2).reshape(SUMM, 2 * WIDTH)
    summ = gather_summaries(own_summ, ROUNDS[:2])
    send, summ = lax.optimization_barrier((send, summ))
    recv = lax.all_to_all(send, "seq", 0, 0, tiled=True)
    summ = gather_summaries(summ, ROUNDS[2:])
    seen = jnp.repeat((slot_blocks(me) < me).astype(jnp.int32), SUMM)[None]
    rows = pack_fixed(arrays)
    fixed_attn, fixed_sums = fixed_forward(rows, summ, seen)
    fixed_send = fixed_sums[:, :2].reshape(NB, OFFS, 2).transpose(0, 2, 1).reshape(NB, 8)
    fixed_send = jnp.pad(fixed_send, ((0, 0), (0, HD - 8)))
    grp, attn, prob, sums, sums_both = strided_forward(recv, fixed_send)
    sums_in = lax.all_to_all(sums_both, ("head", "seq"), 0, 0, tiled=True)
    sums_other = lax.ppermute(sums[:, :16], "head", [(0, 1), (1, 0)])
    send_back, block_sums = strided_backward(grp, attn, prob, sums, sums_other, sums_in)
    recv_back = lax.all_to_all(send_back, "seq", 0, 0, tiled=True)
    block_sums = block_sums.reshape(NB, 2, OFFS).transpose(0, 2, 1).reshape(BLOCK, 2)
    fixed_out, parts = fixed_backward(rows, summ, seen, fixed_attn, block_sums)
    totals = scatter_summaries(parts).astype(BF16).reshape(SUMM, HEADS, 2, HD)
    totals = totals.transpose(2, 0, 1, 3).reshape(2, SUMM, WIDTH)
    tail = jnp.pad(totals, ((0, 0), (16 - SUMM, 0), (0, 0)))
    return unpack(recv_back, fixed_out, tail)


def solution(mesh):
    specs = (P("seq", None, "head"),) * 4
    return jax.shard_map(shards, mesh=mesh, in_specs=specs, out_specs=specs, check_vma=False)
```

```python
import jax
import jax.numpy as jnp
from jax import lax
from jax.experimental import pallas as pl
from jax.experimental.pallas import tpu as pltpu
from jax.sharding import PartitionSpec as P

BLOCK = 512
SUMM = 4
HD = 128
COLS = 1024
NB = 128
HEADS = 4
OFFS = 4
WIDTH = HEADS * HD
PARTS = (8, 2, 4, 2)
VMEM3, VMEM4, VMEM6 = 32, 32, 32

epsilon = 1e-06
scale = HD ** (-0.5)
F32 = jnp.float32
BF16 = jnp.bfloat16


def iotas(shape):
    return (
        lax.broadcasted_iota(jnp.int32, shape, 0),
        lax.broadcasted_iota(jnp.int32, shape, 1),
    )


def one_hot(hit):
    return jnp.where(hit, 1.0, 0.0).astype(BF16)


def dot(a, b):
    return jnp.dot(a, b, preferred_element_type=F32)


def dot_nt(a, b):
    return lax.dot_general(a, b, (((1,), (1,)), ((), ())), preferred_element_type=F32)


def dot_tn(a, b):
    return lax.dot_general(a, b, (((0,), (0,)), ((), ())), preferred_element_type=F32)


def batch_dot(a, b, left, right):
    return lax.dot_general(
        a, b, (((left,), (right,)), ((0,), (0,))), preferred_element_type=F32
    )


def flat(array):
    split = array.reshape(BLOCK, 2, HEADS, HD).transpose(0, 2, 1, 3)
    return split.reshape(BLOCK * HEADS * 2, HD)


def unflat(rows):
    return rows.reshape(BLOCK, HEADS, 2, HD).transpose(0, 2, 1, 3).reshape(BLOCK, 2, WIDTH)


def call(kernel, grid, in_specs, out_specs, out_shape, flops, nbytes, scratch=(), vmem=60):
    return pl.pallas_call(
        kernel,
        grid=(grid,),
        in_specs=in_specs,
        out_specs=out_specs,
        out_shape=out_shape,
        scratch_shapes=list(scratch),
        compiler_params=pltpu.CompilerParams(vmem_limit_bytes=vmem * 2**20),
        cost_estimate=pl.CostEstimate(flops=flops, bytes_accessed=nbytes, transcendentals=0),
    )


IN_HBM = pl.BlockSpec(memory_space=pltpu.HBM)


def in_hbm(array):
    return pltpu.with_memory_space_constraint(array, pltpu.HBM)


def copy_all(pairs, sems):
    copies = [
        pltpu.make_async_copy(source, target, sems.at[n]) for n, (source, target) in enumerate(pairs)
    ]
    for copy in copies:
        copy.start()
    return copies


def spec(block, *index):
    return pl.BlockSpec(block, lambda i: tuple(i if at == "i" else at for at in index))


def pack_strided_kernel(q_ref, k_ref, v_ref, c_ref, send_ref, rows_ref, out_ref, in_sem, out_sem):
    parts = 4
    size = BLOCK * 8 // parts
    copies = copy_all(
        [
            (ref.at[pl.ds(part * size, size)], rows_ref.at[array, pl.ds(part * size, size)])
            for part in range(parts)
            for array, ref in enumerate((q_ref, k_ref, v_ref, c_ref))
        ],
        in_sem,
    )
    row, col = iotas((128, 256))
    home, head, array, offset = row >> 6, (row >> 4) & 3, (row >> 2) & 3, row & 3
    pick = one_hot(col == array * 64 + ((home * OFFS + offset) * HEADS + head) * 2)
    sent = []
    for part in range(parts):
        for copy in copies[4 * part : 4 * part + 4]:
            copy.wait()
        for at in range(part * 64 // parts, (part + 1) * 64 // parts, 2):
            pair = [
                jnp.concatenate(
                    [rows_ref[array, 64 * n : 64 * (n + 1)] for n in (at, at + 1)], 1
                )
                for array in range(4)
            ]
            picked = dot(pick, jnp.concatenate(pair, 0)).astype(BF16)
            for n in range(2):
                for home in range(2):
                    for head in range(HEADS):
                        row = home * 64 + head * 16
                        out_ref[2 * (at + n) + home, :, head * HD : (head + 1) * HD] = picked[
                            row : row + 16, n * HD : (n + 1) * HD
                        ]
        where = pl.ds(part * NB // parts, NB // parts)
        copy = pltpu.make_async_copy(out_ref.at[where], send_ref.at[where], out_sem.at[part])
        copy.start()
        sent.append(copy)
    for copy in sent:
        copy.wait()


def pack_strided(arrays):
    return call(
        pack_strided_kernel,
        1,
        [IN_HBM] * 4,
        IN_HBM,
        jax.ShapeDtypeStruct((NB, 16, WIDTH), BF16),
        10**9,
        6 * 2**20,
        [
            pltpu.VMEM((4, BLOCK * 8, HD), BF16),
            pltpu.VMEM((NB, 16, WIDTH), BF16),
            pltpu.SemaphoreType.DMA((16,)),
            pltpu.SemaphoreType.DMA((4,)),
        ],
    )(*arrays)


def pack_fixed_kernel(q_ref, k_ref, v_ref, c_ref, out_ref):
    row, col = iotas((64, 128))
    pick = one_hot(col == ((row & 15) * HEADS + (row >> 4)) * 2 + 1)
    for at in range(16):
        rows = [ref[128 * at : 128 * (at + 1)] for ref in (q_ref, k_ref, v_ref, c_ref)]
        picked = dot(pick, jnp.concatenate(rows, 1)).astype(BF16)
        for array in range(4):
            for head in range(HEADS):
                out_ref[array, 16 * at : 16 * (at + 1), head * HD : (head + 1) * HD] = picked[
                    16 * head : 16 * (head + 1), array * HD : (array + 1) * HD
                ]


def pack_fixed(arrays):
    return call(
        pack_fixed_kernel,
        2,
        [spec((2048, HD), "i", 0)] * 4,
        spec((4, BLOCK // 2, WIDTH), 0, "i", 0),
        jax.ShapeDtypeStruct((4, BLOCK, WIDTH), BF16),
        10**9,
        6 * 2**20,
    )(*arrays)


def fixed_probabilities(query, key, summ_key, seen):
    row, col = iotas((BLOCK, BLOCK))
    own = jnp.where(col <= row, dot_nt(query, key) * scale, -jnp.inf)
    far = jnp.where(seen > 0, dot_nt(query, summ_key) * scale, -jnp.inf)
    top = jnp.maximum(
        jnp.max(own, axis=-1, keepdims=True), jnp.max(far, axis=-1, keepdims=True)
    )
    own = jnp.exp(own - top)
    far = jnp.exp(far - top)
    total = jnp.sum(own, axis=-1, keepdims=True) + jnp.sum(far, axis=-1, keepdims=True)
    inverse = 1.0 / total
    return own * inverse, far * inverse


def fixed_forward_kernel(rows_ref, summ_ref, seen_ref, attn_ref, sums_ref):
    own, far = fixed_probabilities(rows_ref[0], rows_ref[1], summ_ref[:, :HD], seen_ref[...])
    attn = (
        dot(own.astype(BF16), rows_ref[2]) + dot(far.astype(BF16), summ_ref[:, HD:])
    ).astype(BF16)
    attn_ref[...] = attn
    wide = attn.astype(F32)
    square = jnp.sum(wide * wide, axis=-1, keepdims=True)
    cross = jnp.sum(wide * rows_ref[3].astype(F32), axis=-1, keepdims=True)
    lane = lax.broadcasted_iota(jnp.int32, (BLOCK, 8), 1)
    part = jnp.where(lane == 0, square, jnp.where(lane == 1, cross, 0.0))

    @pl.when(pl.program_id(0) == 0)
    def _():
        sums_ref[...] = part

    @pl.when(pl.program_id(0) > 0)
    def _():
        sums_ref[...] += part


def fixed_forward(rows, summ, seen):
    return call(
        fixed_forward_kernel,
        HEADS,
        [
            spec((4, BLOCK, HD), 0, 0, "i"),
            spec((BLOCK, 2 * HD), 0, "i"),
            spec((1, BLOCK), 0, 0),
        ],
        [spec((BLOCK, HD), 0, "i"), spec((BLOCK, 8), 0, 0)],
        [
            jax.ShapeDtypeStruct((BLOCK, WIDTH), BF16),
            jax.ShapeDtypeStruct((BLOCK, 8), F32),
        ],
        4 * 10**9,
        4 * 2**20,
    )(rows, summ, seen)


def swap_matrix():
    row, col = iotas((256, 256))
    return one_hot(col == ((row & 15) << 4) + (row >> 4))


def strided_forward_kernel(
    recv_ref, fixed_ref, grp_out, attn_out, prob_out, sums_ref, send_ref,
    grp_ref, attn_ref, prob_ref, sem,
):
    swap = swap_matrix()
    for at in range(0, NB, 16):
        rows = dot(swap, recv_ref[at : at + 16].reshape(256, WIDTH)).astype(BF16)
        for head in range(HEADS):
            grp_ref[head, :, :, at : at + 16, :] = rows[:, head * HD : (head + 1) * HD].reshape(
                4, OFFS, 16, HD
            )
    copies = copy_all([(grp_ref, grp_out)], sem.at[0])
    row, col = iotas((NB, NB))
    square, cross = 0.0, 0.0
    for head in range(HEADS):
        scores = batch_dot(grp_ref[head, 0], grp_ref[head, 1], 2, 2) * scale
        scores = jnp.where((col <= row)[None], scores, -jnp.inf)
        expo = jnp.exp(scores - jnp.max(scores, axis=-1, keepdims=True))
        prob = expo * (1.0 / jnp.sum(expo, axis=-1, keepdims=True))
        attn = batch_dot(prob.astype(BF16), grp_ref[head, 2], 2, 1).astype(BF16)
        prob_ref[head] = prob
        attn_ref[head] = attn
        wide = attn.astype(F32)
        square += wide * wide
        cross += wide * grp_ref[head, 3].astype(F32)
        copies += copy_all(
            [(prob_ref.at[head], prob_out.at[head]), (attn_ref.at[head], attn_out.at[head])],
            sem.at[head + 1],
        )
    square = jnp.sum(square, axis=-1, keepdims=True)
    cross = jnp.sum(cross, axis=-1, keepdims=True)
    lane = lax.broadcasted_iota(jnp.int32, (NB, HD), 1)
    part = fixed_ref[...]
    for at in range(OFFS):
        part += jnp.where(lane == 8 + at, square[at], jnp.where(lane == 12 + at, cross[at], 0.0))
    sums_ref[...] = part
    for head in range(2):
        send_ref[head * NB : (head + 1) * NB] = part.reshape(NB, 1, HD)
    for copy in copies:
        copy.wait()


def strided_forward(recv, fixed_sums):
    return call(
        strided_forward_kernel,
        1,
        [spec((NB, 16, WIDTH), 0, 0, 0), spec((NB, HD), 0, 0)],
        [
            IN_HBM,
            IN_HBM,
            IN_HBM,
            spec((NB, HD), 0, 0),
            spec((2 * NB, 1, HD), 0, 0, 0),
        ],
        [
            pltpu.HBM((HEADS, 4, OFFS, NB, HD), BF16),
            pltpu.HBM((HEADS, OFFS, NB, HD), BF16),
            pltpu.HBM((HEADS, OFFS, NB, NB), F32),
            jax.ShapeDtypeStruct((NB, HD), F32),
            jax.ShapeDtypeStruct((2 * NB, 1, HD), F32),
        ],
        10**9,
        6 * 2**20,
        [
            pltpu.VMEM((HEADS, 4, OFFS, NB, HD), BF16),
            pltpu.VMEM((HEADS, OFFS, NB, HD), BF16),
            pltpu.VMEM((HEADS, OFFS, NB, NB), F32),
            pltpu.SemaphoreType.DMA((HEADS + 1, 2)),
        ],
        vmem=VMEM3,
    )(recv, fixed_sums)


def normalize(wide, cotangent, square, cross):
    scaling = lax.rsqrt(square / (2 * COLS) + epsilon)
    normed = (wide * scaling).astype(BF16)
    grad = (
        scaling * cotangent.astype(F32) - wide * (scaling * scaling * scaling * cross / (2 * COLS))
    ).astype(BF16)
    return normed, grad, jnp.sum(grad.astype(F32) * wide, axis=-1, keepdims=True)


def strided_backward_kernel(
    grp_in, attn_in, prob_in, sums_ref, other_ref, recv_ref, send_out, block_ref,
    grp_ref, attn_ref, prob_ref, out_ref, send_ref, in_sem, out_sem,
):
    copies = [
        copy_all(
            [
                (attn_in.at[head], attn_ref.at[head]),
                (grp_in.at[head], grp_ref.at[head]),
                (prob_in.at[head], prob_ref.at[head]),
            ],
            in_sem.at[head],
        )
        for head in range(HEADS)
    ]
    both = sums_ref[:, :16] + other_ref[...]
    moved = (recv_ref[:NB] + recv_ref[NB:]).reshape(NB, HD)
    block_ref[...] = both[:, :8] + moved[:, 8:16]
    total = both[:, 8:] + moved[:, :8]
    square = jnp.stack([total[:, at : at + 1] for at in range(OFFS)])
    cross = jnp.stack([total[:, OFFS + at : OFFS + at + 1] for at in range(OFFS)])
    for head in range(HEADS):
        for copy in copies[head]:
            copy.wait()
        wide = attn_ref[head].astype(F32)
        normed, grad, row_dot = normalize(wide, grp_ref[head, 3], square, cross)
        prob = prob_ref[head]
        grad_prob = batch_dot(grad, grp_ref[head, 2], 2, 2)
        grad_score = (prob * (grad_prob - row_dot) * scale).astype(BF16)
        out_ref[head, 0] = normed
        out_ref[head, 1] = batch_dot(grad_score, grp_ref[head, 1], 2, 1).astype(BF16)
        out_ref[head, 2] = batch_dot(grad_score, grp_ref[head, 0], 1, 1).astype(BF16)
        out_ref[head, 3] = batch_dot(prob.astype(BF16), grad, 1, 1).astype(BF16)
    swap = swap_matrix()
    copies = []
    for at in range(0, NB, 16):
        rows = [out_ref[head, :, :, at : at + 16, :].reshape(256, HD) for head in range(HEADS)]
        moved = dot(swap, jnp.concatenate(rows, 1)).astype(BF16)
        send_ref[at : at + 16] = moved.reshape(16, 16, WIDTH)
        where = pl.ds(at, 16)
        copies += copy_all([(send_ref.at[where], send_out.at[where])], out_sem.at[at // 16])
    for copy in copies:
        copy.wait()


def strided_backward(grp, attn, prob, sums, other, recv):
    return call(
        strided_backward_kernel,
        1,
        [
            IN_HBM,
            IN_HBM,
            IN_HBM,
            spec((NB, HD), 0, 0),
            spec((NB, 16), 0, 0),
            spec((2 * NB, 1, HD), 0, 0, 0),
        ],
        [IN_HBM, spec((NB, 8), 0, 0)],
        [
            pltpu.HBM((NB, 16, WIDTH), BF16),
            jax.ShapeDtypeStruct((NB, 8), F32),
        ],
        10**9,
        6 * 2**20,
        [
            pltpu.VMEM((HEADS, 4, OFFS, NB, HD), BF16),
            pltpu.VMEM((HEADS, OFFS, NB, HD), BF16),
            pltpu.VMEM((HEADS, OFFS, NB, NB), F32),
            pltpu.VMEM((HEADS, 4, OFFS, NB, HD), BF16),
            pltpu.VMEM((NB, 16, WIDTH), BF16),
            pltpu.SemaphoreType.DMA((HEADS, 3)),
            pltpu.SemaphoreType.DMA((NB // 16, 1)),
        ],
        vmem=VMEM4,
    )(*[in_hbm(array) for array in (grp, attn, prob)], sums, other, recv)


def fixed_backward_kernel(rows_ref, summ_ref, seen_ref, attn_ref, sums_ref, out_ref, part_ref):
    query, key, value = rows_ref[0], rows_ref[1], rows_ref[2]
    summ_key, summ_value = summ_ref[:, :HD], summ_ref[:, HD:]
    own, far = fixed_probabilities(query, key, summ_key, seen_ref[...])
    wide = attn_ref[...].astype(F32)
    normed, grad, row_dot = normalize(wide, rows_ref[3], sums_ref[:, 0:1], sums_ref[:, 1:2])
    out_ref[0] = normed
    own_score = (own * (dot_nt(grad, value) - row_dot) * scale).astype(BF16)
    far_score = (far * (dot_nt(grad, summ_value) - row_dot) * scale).astype(BF16)
    out_ref[1] = (dot(own_score, key) + dot(far_score, summ_key)).astype(BF16)
    grad_key = dot_tn(own_score, query)
    grad_value = dot_tn(own.astype(BF16), grad)
    out_ref[2] = grad_key.astype(BF16)
    out_ref[3] = grad_value.astype(BF16)
    part_ref[:, :HD] = dot_tn(far_score, query)
    part_ref[:, HD:] = dot_tn(far.astype(BF16), grad)
    row = lax.broadcasted_iota(jnp.int32, (8, HD), 0)
    for at, grads in ((0, grad_key), (HD, grad_value)):
        tail = pltpu.roll(grads[BLOCK - 8 :], SUMM, 0)
        part_ref[0:8, at : at + HD] += jnp.where(row < SUMM, tail, 0.0)


def fixed_backward(rows, summ, seen, attn, sums):
    return call(
        fixed_backward_kernel,
        HEADS,
        [
            spec((4, BLOCK, HD), 0, 0, "i"),
            spec((BLOCK, 2 * HD), 0, "i"),
            spec((1, BLOCK), 0, 0),
            spec((BLOCK, HD), 0, "i"),
            spec((BLOCK, 2), 0, 0),
        ],
        [spec((4, BLOCK, HD), 0, 0, "i"), spec((BLOCK, 2 * HD), 0, "i")],
        [
            pltpu.HBM((4, BLOCK, WIDTH), BF16),
            jax.ShapeDtypeStruct((BLOCK, 2 * WIDTH), F32),
        ],
        8 * 10**9,
        8 * 2**20,
    )(rows, summ, seen, attn, sums)


def unpack_kernel(recv_ref, fixed_in, tail_ref, *refs):
    outs, fixed_ref, out_ref, in_sem, out_sem = refs[:4], refs[4], refs[5], refs[6], refs[7]
    parts = 4
    size = BLOCK // parts
    copies = copy_all(
        [
            (fixed_in.at[:, pl.ds(part * size, size)], fixed_ref.at[:, pl.ds(part * size, size)])
            for part in range(parts)
        ],
        in_sem,
    )
    sent = []
    row, col = iotas((512, 256))
    array, token, head, kind = row >> 7, (row >> 3) & 15, (row >> 1) & 3, row & 1
    source = (token >> 2) * 64 + head * 16 + array * OFFS + (token & 3)
    strided_pick = one_hot((kind == 0) & (col == source))
    row, col = iotas((128, 64))
    token, head, kind = row >> 3, (row >> 1) & 3, row & 1
    own_pick = one_hot((kind == 1) & (col == head * 16 + token))
    end = lax.broadcasted_iota(jnp.int32, (16, WIDTH), 0) >= 16 - SUMM
    for at in range(0, 32, 2):
        if at * 16 % size == 0:
            copies[at * 16 // size].wait()
        rows = [
            jnp.concatenate(
                [
                    recv_ref[4 * n + home, :, head * HD : (head + 1) * HD]
                    for home in range(4)
                    for head in range(HEADS)
                ],
                0,
            )
            for n in (at, at + 1)
        ]
        strided = dot(strided_pick, jnp.concatenate(rows, 1))
        for n in range(2):
            tile = 16 * (at + n)
            fixed = [fixed_ref[array, tile : tile + 16] for array in range(4)]
            if tile == BLOCK - 16:
                for array in (2, 3):
                    fixed[array] = jnp.where(end, tail_ref[array - 2], fixed[array])
            rows = [
                jnp.concatenate([part[:, head * HD : (head + 1) * HD] for part in fixed], 1)
                for head in range(HEADS)
            ]
            own = dot(own_pick, jnp.concatenate(rows, 0))
            for array in range(4):
                out_ref[array, 8 * tile : 8 * tile + 128] = (
                    strided[array * 128 : (array + 1) * 128, n * HD : (n + 1) * HD]
                    + own[:, array * HD : (array + 1) * HD]
                ).astype(BF16)
        if (at + 2) * 16 % size == 0:
            part = at * 16 // size
            where = pl.ds(part * size * 8, size * 8)
            sent += copy_all(
                [(out_ref.at[array, where], outs[array].at[where]) for array in range(4)],
                out_sem.at[part],
            )
    for copy in sent:
        copy.wait()


def unpack(recv, fixed, tail):
    rows = call(
        unpack_kernel,
        1,
        [spec((NB, 16, WIDTH), 0, 0, 0), IN_HBM, spec((2, 16, WIDTH), 0, 0, 0)],
        [IN_HBM] * 4,
        [jax.ShapeDtypeStruct((BLOCK * 8, HD), BF16)] * 4,
        2 * 10**9,
        8 * 2**20,
        [
            pltpu.VMEM((4, BLOCK, WIDTH), BF16),
            pltpu.VMEM((4, BLOCK * 8, HD), BF16),
            pltpu.SemaphoreType.DMA((4,)),
            pltpu.SemaphoreType.DMA((4, 4)),
        ],
        vmem=VMEM6,
    )(recv, in_hbm(fixed), tail)
    return tuple(unflat(array) for array in rows)


def place(index):
    coords = []
    for size in PARTS[::-1]:
        coords.append(index % size)
        index = index // size
    return coords[::-1]


def joined(coords):
    index = 0
    for size, at in zip(PARTS, coords):
        index = index * size + at
    return index


def shift(array, part, step):
    perm = []
    for source in range(NB):
        coords = place(source)
        coords[part] = (coords[part] + step) % PARTS[part]
        perm.append((source, joined(coords)))
    return lax.ppermute(array, "seq", perm)


ROUNDS = (
    ((0, 1, 1),),
    ((0, 2, 2), (0, -2, 2), (0, 4, 2)),
    ((2, 1, 8), (2, -1, 8), (2, 2, 8)),
    ((1, 1, 32),),
    ((3, 1, 64),),
)


def gather_summaries(held, rounds):
    for steps in rounds:
        moved = [shift(held[: slots * SUMM], part, step) for part, step, slots in steps]
        held = jnp.concatenate([held] + moved, 0)
    return held


def scatter_summaries(parts):
    for steps in ROUNDS[::-1]:
        kept = parts.shape[0] - SUMM * sum(slots for _, _, slots in steps)
        total, at = parts[:kept], kept
        for part, step, slots in steps:
            rows = slots * SUMM
            moved = shift(parts[at : at + rows].astype(BF16), part, -step).astype(F32)
            total = total + jnp.pad(moved, ((0, kept - rows), (0, 0)))
            at += rows
        parts = total
    return parts


def slot_blocks(me):
    back = [(0,) * len(PARTS)]
    for steps in ROUNDS:
        back = back + [
            tuple(by + step * (at == part) for at, by in enumerate(slot))
            for part, step, slots in steps
            for slot in back[:slots]
        ]
    back = jnp.array(back, jnp.int32)
    coords = [(at - back[:, n]) % size for n, (at, size) in enumerate(zip(place(me), PARTS))]
    return joined(coords)


def shards(queries, key_rows, value_rows, cotangent):
    me = lax.axis_index("seq")
    arrays = tuple(flat(array) for array in (queries, key_rows, value_rows, cotangent))
    send = pack_strided(arrays)
    tails = [a[BLOCK - SUMM :, 1].reshape(SUMM, HEADS, 1, HD) for a in (key_rows, value_rows)]
    own_summ = jnp.concatenate(tails, 2).reshape(SUMM, 2 * WIDTH)
    summ = gather_summaries(own_summ, ROUNDS[:1])
    send, summ = lax.optimization_barrier((send, summ))
    summ = gather_summaries(summ, ROUNDS[1:2])
    send, summ = lax.optimization_barrier((send, summ))
    recv = lax.all_to_all(send, "seq", 0, 0, tiled=True)
    summ = gather_summaries(summ, ROUNDS[2:])
    seen = jnp.repeat((slot_blocks(me) < me).astype(jnp.int32), SUMM)[None]
    rows = pack_fixed(arrays)
    fixed_attn, fixed_sums = fixed_forward(rows, summ, seen)
    fixed_send = fixed_sums[:, :2].reshape(NB, OFFS, 2).transpose(0, 2, 1).reshape(NB, 8)
    fixed_send = jnp.pad(fixed_send, ((0, 0), (0, HD - 8)))
    grp, attn, prob, sums, sums_both = strided_forward(recv, fixed_send)
    sums_in = lax.all_to_all(sums_both, ("head", "seq"), 0, 0, tiled=True)
    sums_other = lax.ppermute(sums[:, :16], "head", [(0, 1), (1, 0)])
    send_back, block_sums = strided_backward(grp, attn, prob, sums, sums_other, sums_in)
    recv_back = lax.all_to_all(send_back, "seq", 0, 0, tiled=True)
    block_sums = block_sums.reshape(NB, 2, OFFS).transpose(0, 2, 1).reshape(BLOCK, 2)
    fixed_out, parts = fixed_backward(rows, summ, seen, fixed_attn, block_sums)
    totals = scatter_summaries(parts).astype(BF16).reshape(SUMM, HEADS, 2, HD)
    totals = totals.transpose(2, 0, 1, 3).reshape(2, SUMM, WIDTH)
    tail = jnp.pad(totals, ((0, 0), (16 - SUMM, 0), (0, 0)))
    return unpack(recv_back, fixed_out, tail)


def solution(mesh):
    specs = (P("seq", None, "head"),) * 4
    return jax.shard_map(shards, mesh=mesh, in_specs=specs, out_specs=specs, check_vma=False)
```

```python
import jax
import jax.numpy as jnp
from jax import lax
from jax.experimental import pallas as pl
from jax.experimental.pallas import tpu as pltpu
from jax.sharding import PartitionSpec as P

BLOCK = 512
SUMM = 4
HD = 128
COLS = 1024
NB = 128
HEADS = 4
OFFS = 4
WIDTH = HEADS * HD
PARTS = (8, 2, 4, 2)
VMEM3, VMEM4, VMEM6 = 32, 32, 32

epsilon = 1e-06
scale = HD ** (-0.5)
F32 = jnp.float32
BF16 = jnp.bfloat16


def iotas(shape):
    return (
        lax.broadcasted_iota(jnp.int32, shape, 0),
        lax.broadcasted_iota(jnp.int32, shape, 1),
    )


def one_hot(hit):
    return jnp.where(hit, 1.0, 0.0).astype(BF16)


def dot(a, b):
    return jnp.dot(a, b, preferred_element_type=F32)


def dot_nt(a, b):
    return lax.dot_general(a, b, (((1,), (1,)), ((), ())), preferred_element_type=F32)


def dot_tn(a, b):
    return lax.dot_general(a, b, (((0,), (0,)), ((), ())), preferred_element_type=F32)


def batch_dot(a, b, left, right):
    return lax.dot_general(
        a, b, (((left,), (right,)), ((0,), (0,))), preferred_element_type=F32
    )


def flat(array):
    split = array.reshape(BLOCK, 2, HEADS, HD).transpose(0, 2, 1, 3)
    return split.reshape(BLOCK * HEADS * 2, HD)


def unflat(rows):
    return rows.reshape(BLOCK, HEADS, 2, HD).transpose(0, 2, 1, 3).reshape(BLOCK, 2, WIDTH)


def call(kernel, grid, in_specs, out_specs, out_shape, flops, nbytes, scratch=(), vmem=60):
    return pl.pallas_call(
        kernel,
        grid=(grid,),
        in_specs=in_specs,
        out_specs=out_specs,
        out_shape=out_shape,
        scratch_shapes=list(scratch),
        compiler_params=pltpu.CompilerParams(vmem_limit_bytes=vmem * 2**20),
        cost_estimate=pl.CostEstimate(flops=flops, bytes_accessed=nbytes, transcendentals=0),
    )


IN_HBM = pl.BlockSpec(memory_space=pltpu.HBM)


def in_hbm(array):
    return pltpu.with_memory_space_constraint(array, pltpu.HBM)


def copy_all(pairs, sems):
    copies = [
        pltpu.make_async_copy(source, target, sems.at[n]) for n, (source, target) in enumerate(pairs)
    ]
    for copy in copies:
        copy.start()
    return copies


def spec(block, *index):
    return pl.BlockSpec(block, lambda i: tuple(i if at == "i" else at for at in index))


def pack_strided_kernel(q_ref, k_ref, v_ref, c_ref, send_ref, rows_ref, out_ref, in_sem, out_sem):
    parts = 4
    size = BLOCK * 8 // parts
    copies = copy_all(
        [
            (ref.at[pl.ds(part * size, size)], rows_ref.at[array, pl.ds(part * size, size)])
            for part in range(parts)
            for array, ref in enumerate((q_ref, k_ref, v_ref, c_ref))
        ],
        in_sem,
    )
    row, col = iotas((128, 256))
    home, head, array, offset = row >> 6, (row >> 4) & 3, (row >> 2) & 3, row & 3
    pick = one_hot(col == array * 64 + ((home * OFFS + offset) * HEADS + head) * 2)
    sent = []
    for part in range(parts):
        for copy in copies[4 * part : 4 * part + 4]:
            copy.wait()
        for at in range(part * 64 // parts, (part + 1) * 64 // parts, 2):
            pair = [
                jnp.concatenate(
                    [rows_ref[array, 64 * n : 64 * (n + 1)] for n in (at, at + 1)], 1
                )
                for array in range(4)
            ]
            picked = dot(pick, jnp.concatenate(pair, 0)).astype(BF16)
            for n in range(2):
                for home in range(2):
                    for head in range(HEADS):
                        row = home * 64 + head * 16
                        out_ref[2 * (at + n) + home, :, head * HD : (head + 1) * HD] = picked[
                            row : row + 16, n * HD : (n + 1) * HD
                        ]
        where = pl.ds(part * NB // parts, NB // parts)
        copy = pltpu.make_async_copy(out_ref.at[where], send_ref.at[where], out_sem.at[part])
        copy.start()
        sent.append(copy)
    for copy in sent:
        copy.wait()


def pack_strided(arrays):
    return call(
        pack_strided_kernel,
        1,
        [IN_HBM] * 4,
        IN_HBM,
        jax.ShapeDtypeStruct((NB, 16, WIDTH), BF16),
        10**9,
        6 * 2**20,
        [
            pltpu.VMEM((4, BLOCK * 8, HD), BF16),
            pltpu.VMEM((NB, 16, WIDTH), BF16),
            pltpu.SemaphoreType.DMA((16,)),
            pltpu.SemaphoreType.DMA((4,)),
        ],
    )(*arrays)


def pack_fixed_kernel(q_ref, k_ref, v_ref, c_ref, out_ref):
    row, col = iotas((64, 128))
    pick = one_hot(col == ((row & 15) * HEADS + (row >> 4)) * 2 + 1)
    for at in range(16):
        rows = [ref[128 * at : 128 * (at + 1)] for ref in (q_ref, k_ref, v_ref, c_ref)]
        picked = dot(pick, jnp.concatenate(rows, 1)).astype(BF16)
        for array in range(4):
            for head in range(HEADS):
                out_ref[array, 16 * at : 16 * (at + 1), head * HD : (head + 1) * HD] = picked[
                    16 * head : 16 * (head + 1), array * HD : (array + 1) * HD
                ]


def pack_fixed(arrays):
    return call(
        pack_fixed_kernel,
        2,
        [spec((2048, HD), "i", 0)] * 4,
        spec((4, BLOCK // 2, WIDTH), 0, "i", 0),
        jax.ShapeDtypeStruct((4, BLOCK, WIDTH), BF16),
        10**9,
        6 * 2**20,
    )(*arrays)


def fixed_probabilities(query, key, summ_key, seen):
    row, col = iotas((BLOCK, BLOCK))
    own = jnp.where(col <= row, dot_nt(query, key) * scale, -jnp.inf)
    far = jnp.where(seen > 0, dot_nt(query, summ_key) * scale, -jnp.inf)
    top = jnp.maximum(
        jnp.max(own, axis=-1, keepdims=True), jnp.max(far, axis=-1, keepdims=True)
    )
    own = jnp.exp(own - top)
    far = jnp.exp(far - top)
    total = jnp.sum(own, axis=-1, keepdims=True) + jnp.sum(far, axis=-1, keepdims=True)
    inverse = 1.0 / total
    return own * inverse, far * inverse


def fixed_forward_kernel(rows_ref, summ_ref, seen_ref, attn_ref, own_ref, far_ref, sums_ref):
    own, far = fixed_probabilities(rows_ref[0], rows_ref[1], summ_ref[:, :HD], seen_ref[...])
    own_ref[0] = own
    far_ref[0] = far
    attn = (
        dot(own.astype(BF16), rows_ref[2]) + dot(far.astype(BF16), summ_ref[:, HD:])
    ).astype(BF16)
    attn_ref[...] = attn
    wide = attn.astype(F32)
    square = jnp.sum(wide * wide, axis=-1, keepdims=True)
    cross = jnp.sum(wide * rows_ref[3].astype(F32), axis=-1, keepdims=True)
    lane = lax.broadcasted_iota(jnp.int32, (BLOCK, 8), 1)
    part = jnp.where(lane == 0, square, jnp.where(lane == 1, cross, 0.0))

    @pl.when(pl.program_id(0) == 0)
    def _():
        sums_ref[...] = part

    @pl.when(pl.program_id(0) > 0)
    def _():
        sums_ref[...] += part


def fixed_forward(rows, summ, seen):
    return call(
        fixed_forward_kernel,
        HEADS,
        [
            spec((4, BLOCK, HD), 0, 0, "i"),
            spec((BLOCK, 2 * HD), 0, "i"),
            spec((1, BLOCK), 0, 0),
        ],
        [
            spec((BLOCK, HD), 0, "i"),
            spec((1, BLOCK, BLOCK), "i", 0, 0),
            spec((1, BLOCK, BLOCK), "i", 0, 0),
            spec((BLOCK, 8), 0, 0),
        ],
        [
            jax.ShapeDtypeStruct((BLOCK, WIDTH), BF16),
            jax.ShapeDtypeStruct((HEADS, BLOCK, BLOCK), F32),
            jax.ShapeDtypeStruct((HEADS, BLOCK, BLOCK), F32),
            jax.ShapeDtypeStruct((BLOCK, 8), F32),
        ],
        4 * 10**9,
        4 * 2**20,
    )(rows, summ, seen)


def swap_matrix():
    row, col = iotas((256, 256))
    return one_hot(col == ((row & 15) << 4) + (row >> 4))


def strided_forward_kernel(
    recv_ref, fixed_ref, keys_out, prob_out, grp_ref, sums_ref, send_ref, keys_ref, prob_ref, sem
):
    swap = swap_matrix()
    for at in range(0, NB, 16):
        rows = dot(swap, recv_ref[at : at + 16].reshape(256, WIDTH)).astype(BF16)
        for head in range(HEADS):
            tiles = rows[:, head * HD : (head + 1) * HD].reshape(4, OFFS, 16, HD)
            keys_ref[head, :, :, at : at + 16, :] = tiles[:3]
            grp_ref[head, 0, :, at : at + 16, :] = tiles[3]
    copies = copy_all([(keys_ref, keys_out)], sem.at[0])
    row, col = iotas((NB, NB))
    square, cross = 0.0, 0.0
    for head in range(HEADS):
        scores = batch_dot(keys_ref[head, 0], keys_ref[head, 1], 2, 2) * scale
        scores = jnp.where((col <= row)[None], scores, -jnp.inf)
        expo = jnp.exp(scores - jnp.max(scores, axis=-1, keepdims=True))
        prob = expo * (1.0 / jnp.sum(expo, axis=-1, keepdims=True))
        attn = batch_dot(prob.astype(BF16), keys_ref[head, 2], 2, 1).astype(BF16)
        prob_ref[head] = prob
        wide = attn.astype(F32)
        square += wide * wide
        cross += wide * grp_ref[head, 0].astype(F32)
        grp_ref[head, 1] = attn
        copies += copy_all([(prob_ref.at[head], prob_out.at[head])], sem.at[head + 1])
    square = jnp.sum(square, axis=-1, keepdims=True)
    cross = jnp.sum(cross, axis=-1, keepdims=True)
    lane = lax.broadcasted_iota(jnp.int32, (NB, HD), 1)
    part = fixed_ref[...]
    for at in range(OFFS):
        part += jnp.where(lane == 8 + at, square[at], jnp.where(lane == 12 + at, cross[at], 0.0))
    sums_ref[...] = part
    send_ref[...] = part.reshape(NB, 1, HD)
    for copy in copies:
        copy.wait()


def strided_forward(recv, fixed_sums):
    return call(
        strided_forward_kernel,
        1,
        [spec((NB, 16, WIDTH), 0, 0, 0), spec((NB, HD), 0, 0)],
        [
            IN_HBM,
            IN_HBM,
            spec((HEADS, 2, OFFS, NB, HD), 0, 0, 0, 0, 0),
            spec((NB, HD), 0, 0),
            spec((NB, 1, HD), 0, 0, 0),
        ],
        [
            pltpu.HBM((HEADS, 3, OFFS, NB, HD), BF16),
            pltpu.HBM((HEADS, OFFS, NB, NB), F32),
            jax.ShapeDtypeStruct((HEADS, 2, OFFS, NB, HD), BF16),
            jax.ShapeDtypeStruct((NB, HD), F32),
            jax.ShapeDtypeStruct((NB, 1, HD), F32),
        ],
        10**9,
        6 * 2**20,
        [
            pltpu.VMEM((HEADS, 3, OFFS, NB, HD), BF16),
            pltpu.VMEM((HEADS, OFFS, NB, NB), F32),
            pltpu.SemaphoreType.DMA((HEADS + 1, 1)),
        ],
        vmem=VMEM3,
    )(recv, fixed_sums)


def normalize(wide, cotangent, square, cross):
    scaling = lax.rsqrt(square / (2 * COLS) + epsilon)
    normed = (wide * scaling).astype(BF16)
    grad = (
        scaling * cotangent.astype(F32) - wide * (scaling * scaling * scaling * cross / (2 * COLS))
    ).astype(BF16)
    return normed, grad, jnp.sum(grad.astype(F32) * wide, axis=-1, keepdims=True)


def strided_backward_kernel(
    keys_in, prob_in, grp_ref, sums_ref, other_ref, recv_ref, send_out, block_ref,
    keys_ref, prob_ref, out_ref, send_ref, in_sem, out_sem,
):
    fetched = [
        copy_all(
            [(keys_in.at[head], keys_ref.at[head]), (prob_in.at[head], prob_ref.at[head])],
            in_sem.at[head],
        )
        for head in range(HEADS)
    ]
    moved = recv_ref[...].reshape(NB, HD)
    block_ref[...] = moved[:, 8:16]
    total = sums_ref[:, 8:16] + other_ref[...] + moved[:, :8]
    square = jnp.stack([total[:, at : at + 1] for at in range(OFFS)])
    cross = jnp.stack([total[:, OFFS + at : OFFS + at + 1] for at in range(OFFS)])
    grads = []
    for head in range(HEADS):
        wide = grp_ref[head, 1].astype(F32)
        normed, grad, row_dot = normalize(wide, grp_ref[head, 0], square, cross)
        out_ref[head, 0] = normed
        grads.append((grad, row_dot))
    for head in range(HEADS):
        for copy in fetched[head]:
            copy.wait()
        grad, row_dot = grads[head]
        prob = prob_ref[head]
        grad_prob = batch_dot(grad, keys_ref[head, 2], 2, 2)
        grad_score = (prob * (grad_prob - row_dot) * scale).astype(BF16)
        out_ref[head, 1] = batch_dot(grad_score, keys_ref[head, 1], 2, 1).astype(BF16)
        out_ref[head, 2] = batch_dot(grad_score, keys_ref[head, 0], 1, 1).astype(BF16)
        out_ref[head, 3] = batch_dot(prob.astype(BF16), grad, 1, 1).astype(BF16)
    swap = swap_matrix()
    copies = []
    for at in range(0, NB, 16):
        rows = [out_ref[head, :, :, at : at + 16, :].reshape(256, HD) for head in range(HEADS)]
        moved = dot(swap, jnp.concatenate(rows, 1)).astype(BF16)
        send_ref[at : at + 16] = moved.reshape(16, 16, WIDTH)
        where = pl.ds(at, 16)
        copies += copy_all([(send_ref.at[where], send_out.at[where])], out_sem.at[at // 16])
    for copy in copies:
        copy.wait()


def strided_backward(keys, prob, grp, sums, other, recv):
    return call(
        strided_backward_kernel,
        1,
        [
            IN_HBM,
            IN_HBM,
            spec((HEADS, 2, OFFS, NB, HD), 0, 0, 0, 0, 0),
            spec((NB, HD), 0, 0),
            spec((NB, 8), 0, 0),
            spec((NB, 1, HD), 0, 0, 0),
        ],
        [IN_HBM, spec((NB, 8), 0, 0)],
        [
            pltpu.HBM((NB, 16, WIDTH), BF16),
            jax.ShapeDtypeStruct((NB, 8), F32),
        ],
        10**9,
        6 * 2**20,
        [
            pltpu.VMEM((HEADS, 3, OFFS, NB, HD), BF16),
            pltpu.VMEM((HEADS, OFFS, NB, NB), F32),
            pltpu.VMEM((HEADS, 4, OFFS, NB, HD), BF16),
            pltpu.VMEM((NB, 16, WIDTH), BF16),
            pltpu.SemaphoreType.DMA((HEADS, 2)),
            pltpu.SemaphoreType.DMA((NB // 16, 1)),
        ],
        vmem=VMEM4,
    )(in_hbm(keys), in_hbm(prob), grp, sums, other, recv)


def fixed_backward_kernel(
    rows_ref, summ_ref, own_ref, far_ref, attn_ref, sums_ref, out_ref, keep_ref, send_ref
):
    query, key, value = rows_ref[0], rows_ref[1], rows_ref[2]
    summ_key, summ_value = summ_ref[:, :HD], summ_ref[:, HD:]
    own, far = own_ref[0], far_ref[0]
    wide = attn_ref[...].astype(F32)
    normed, grad, row_dot = normalize(wide, rows_ref[3], sums_ref[:, 0:1], sums_ref[:, 1:2])
    out_ref[0] = normed
    own_score = (own * (dot_nt(grad, value) - row_dot) * scale).astype(BF16)
    far_score = (far * (dot_nt(grad, summ_value) - row_dot) * scale).astype(BF16)
    out_ref[1] = (dot(own_score, key) + dot(far_score, summ_key)).astype(BF16)
    grad_key = dot_tn(own_score, query)
    grad_value = dot_tn(own.astype(BF16), grad)
    out_ref[2] = grad_key.astype(BF16)
    out_ref[3] = grad_value.astype(BF16)
    far_key = dot_tn(far_score, query)
    far_value = dot_tn(far.astype(BF16), grad)
    half = BLOCK // 2
    send_ref[:, :HD] = far_key[half:].astype(BF16)
    send_ref[:, HD:] = far_value[half:].astype(BF16)
    keep_ref[:, :HD] = far_key[:half]
    keep_ref[:, HD:] = far_value[:half]
    row = lax.broadcasted_iota(jnp.int32, (8, HD), 0)
    for at, grads in ((0, grad_key), (HD, grad_value)):
        tail = pltpu.roll(grads[BLOCK - 8 :], SUMM, 0)
        keep_ref[0:8, at : at + HD] += jnp.where(row < SUMM, tail, 0.0)


def fixed_backward(rows, summ, own, far, attn, sums):
    return call(
        fixed_backward_kernel,
        HEADS,
        [
            spec((4, BLOCK, HD), 0, 0, "i"),
            spec((BLOCK, 2 * HD), 0, "i"),
            spec((1, BLOCK, BLOCK), "i", 0, 0),
            spec((1, BLOCK, BLOCK), "i", 0, 0),
            spec((BLOCK, HD), 0, "i"),
            spec((BLOCK, 2), 0, 0),
        ],
        [
            spec((4, BLOCK, HD), 0, 0, "i"),
            spec((BLOCK // 2, 2 * HD), 0, "i"),
            spec((BLOCK // 2, 2 * HD), 0, "i"),
        ],
        [
            pltpu.HBM((4, BLOCK, WIDTH), BF16),
            jax.ShapeDtypeStruct((BLOCK // 2, 2 * WIDTH), F32),
            jax.ShapeDtypeStruct((BLOCK // 2, 2 * WIDTH), BF16),
        ],
        8 * 10**9,
        8 * 2**20,
    )(rows, summ, own, far, attn, sums)


def unpack_kernel(recv_ref, fixed_in, tail_ref, *refs):
    outs, fixed_ref, out_ref, in_sem, out_sem = refs[:4], refs[4], refs[5], refs[6], refs[7]
    parts = 4
    size = BLOCK // parts
    copies = copy_all(
        [
            (fixed_in.at[:, pl.ds(part * size, size)], fixed_ref.at[:, pl.ds(part * size, size)])
            for part in range(parts)
        ],
        in_sem,
    )
    sent = []
    row, col = iotas((512, 256))
    array, token, head, kind = row >> 7, (row >> 3) & 15, (row >> 1) & 3, row & 1
    source = (token >> 2) * 64 + head * 16 + array * OFFS + (token & 3)
    strided_pick = one_hot((kind == 0) & (col == source))
    row, col = iotas((128, 64))
    token, head, kind = row >> 3, (row >> 1) & 3, row & 1
    own_pick = one_hot((kind == 1) & (col == head * 16 + token))
    end = lax.broadcasted_iota(jnp.int32, (16, WIDTH), 0) >= 16 - SUMM
    for at in range(0, 32, 2):
        if at * 16 % size == 0:
            copies[at * 16 // size].wait()
        rows = [
            jnp.concatenate(
                [
                    recv_ref[4 * n + home, :, head * HD : (head + 1) * HD]
                    for home in range(4)
                    for head in range(HEADS)
                ],
                0,
            )
            for n in (at, at + 1)
        ]
        strided = dot(strided_pick, jnp.concatenate(rows, 1))
        for n in range(2):
            tile = 16 * (at + n)
            fixed = [fixed_ref[array, tile : tile + 16] for array in range(4)]
            if tile == BLOCK - 16:
                for array in (2, 3):
                    fixed[array] = jnp.where(end, tail_ref[array - 2], fixed[array])
            rows = [
                jnp.concatenate([part[:, head * HD : (head + 1) * HD] for part in fixed], 1)
                for head in range(HEADS)
            ]
            own = dot(own_pick, jnp.concatenate(rows, 0))
            for array in range(4):
                out_ref[array, 8 * tile : 8 * tile + 128] = (
                    strided[array * 128 : (array + 1) * 128, n * HD : (n + 1) * HD]
                    + own[:, array * HD : (array + 1) * HD]
                ).astype(BF16)
        if (at + 2) * 16 % size == 0:
            part = at * 16 // size
            where = pl.ds(part * size * 8, size * 8)
            sent += copy_all(
                [(out_ref.at[array, where], outs[array].at[where]) for array in range(4)],
                out_sem.at[part],
            )
    for copy in sent:
        copy.wait()


def unpack(recv, fixed, tail):
    rows = call(
        unpack_kernel,
        1,
        [spec((NB, 16, WIDTH), 0, 0, 0), IN_HBM, spec((2, 16, WIDTH), 0, 0, 0)],
        [IN_HBM] * 4,
        [jax.ShapeDtypeStruct((BLOCK * 8, HD), BF16)] * 4,
        2 * 10**9,
        8 * 2**20,
        [
            pltpu.VMEM((4, BLOCK, WIDTH), BF16),
            pltpu.VMEM((4, BLOCK * 8, HD), BF16),
            pltpu.SemaphoreType.DMA((4,)),
            pltpu.SemaphoreType.DMA((4, 4)),
        ],
        vmem=VMEM6,
    )(recv, in_hbm(fixed), tail)
    return tuple(unflat(array) for array in rows)


def place(index):
    coords = []
    for size in PARTS[::-1]:
        coords.append(index % size)
        index = index // size
    return coords[::-1]


def joined(coords):
    index = 0
    for size, at in zip(PARTS, coords):
        index = index * size + at
    return index


def shift(array, part, step):
    perm = []
    for source in range(NB):
        coords = place(source)
        coords[part] = (coords[part] + step) % PARTS[part]
        perm.append((source, joined(coords)))
    return lax.ppermute(array, "seq", perm)


def other_head(array):
    return lax.ppermute(array, "head", [(0, 1), (1, 0)])


ROUNDS = (
    ((0, -1, 1),),
    ((0, -2, 2), (0, -4, 2), (0, 2, 2)),
    ((1, 1, 8),),
    ((2, 1, 16), (2, -1, 16), (2, 2, 16)),
    ((3, 1, 64),),
)


def gather_along_z(own, me):
    size = PARTS[0]
    step = NB // size
    groups = [[at + step * z for z in range(size)] for at in range(step)]
    sent = jnp.broadcast_to(own[None], (size,) + own.shape)
    held = lax.all_to_all(sent, "seq", 0, 0, axis_index_groups=groups, tiled=True)
    held = jnp.concatenate([held, held], 0)
    held = lax.dynamic_slice_in_dim(held, me // step, size, 0)
    return held.reshape(size * SUMM, 2 * WIDTH)


def gather_summaries(held):
    for steps in ROUNDS[2:]:
        moved = [shift(held[: slots * SUMM], part, step) for part, step, slots in steps]
        held = jnp.concatenate([held] + moved, 0)
    return held


def scatter_summaries(total, sent):
    (part, step, _), = ROUNDS[-1]
    parts = total + shift(sent, part, -step).astype(F32)
    for steps in ROUNDS[-2::-1]:
        kept = parts.shape[0] - SUMM * sum(slots for _, _, slots in steps)
        total, at = parts[:kept], kept
        for part, step, slots in steps:
            rows = slots * SUMM
            moved = shift(parts[at : at + rows].astype(BF16), part, -step).astype(F32)
            total = total + jnp.pad(moved, ((0, kept - rows), (0, 0)))
            at += rows
        parts = total
    return parts


def slot_blocks(me):
    back = [(0,) * len(PARTS)]
    for steps in ROUNDS:
        back = back + [
            tuple(by + step * (at == part) for at, by in enumerate(slot))
            for part, step, slots in steps
            for slot in back[:slots]
        ]
    back = jnp.array(back, jnp.int32)
    coords = [(at - back[:, n]) % size for n, (at, size) in enumerate(zip(place(me), PARTS))]
    return joined(coords)


def shards(queries, key_rows, value_rows, cotangent):
    me = lax.axis_index("seq")
    arrays = tuple(flat(array) for array in (queries, key_rows, value_rows, cotangent))
    send = pack_strided(arrays)
    tails = [a[BLOCK - SUMM :, 1].reshape(SUMM, HEADS, 1, HD) for a in (key_rows, value_rows)]
    own_summ = jnp.concatenate(tails, 2).reshape(SUMM, 2 * WIDTH)
    summ = gather_along_z(own_summ, me)
    send, summ = lax.optimization_barrier((send, summ))
    recv = lax.all_to_all(send, "seq", 0, 0, tiled=True)
    summ = gather_summaries(summ)
    seen = jnp.repeat((slot_blocks(me) < me).astype(jnp.int32), SUMM)[None]
    rows = pack_fixed(arrays)
    fixed_attn, own_prob, far_prob, fixed_sums = fixed_forward(rows, summ, seen)
    fixed_send = fixed_sums[:, :2].reshape(NB, OFFS, 2).transpose(0, 2, 1).reshape(NB, 8)
    fixed_both = fixed_send + other_head(fixed_send)
    keys, prob, grp, sums, sums_send = strided_forward(recv, jnp.pad(fixed_both, ((0, 0), (0, HD - 8))))
    sums_in = lax.all_to_all(sums_send, "seq", 0, 0, tiled=True)
    sums_other = other_head(sums[:, 8:16])
    send_back, block_sums = strided_backward(keys, prob, grp, sums, sums_other, sums_in)
    block_sums = fixed_both + block_sums + other_head(block_sums)
    recv_back = lax.all_to_all(send_back, "seq", 0, 0, tiled=True)
    block_sums = block_sums.reshape(NB, 2, OFFS).transpose(0, 2, 1).reshape(BLOCK, 2)
    fixed_out, kept, sent = fixed_backward(rows, summ, own_prob, far_prob, fixed_attn, block_sums)
    totals = scatter_summaries(kept, sent).astype(BF16).reshape(SUMM, HEADS, 2, HD)
    totals = totals.transpose(2, 0, 1, 3).reshape(2, SUMM, WIDTH)
    tail = jnp.pad(totals, ((0, 0), (16 - SUMM, 0), (0, 0)))
    return unpack(recv_back, fixed_out, tail)


def solution(mesh):
    specs = (P("seq", None, "head"),) * 4
    return jax.shard_map(shards, mesh=mesh, in_specs=specs, out_specs=specs, check_vma=False)
```

```python
import jax
import jax.numpy as jnp
from jax import lax
from jax.experimental import pallas as pl
from jax.experimental.pallas import tpu as pltpu
from jax.sharding import PartitionSpec as P

BLOCK = 512
SUMM = 4
HD = 128
COLS = 1024
NB = 128
HEADS = 4
OFFS = 4
WIDTH = HEADS * HD
PARTS = (8, 2, 4, 2)
VMEM3, VMEM4, VMEM6 = 32, 32, 32

epsilon = 1e-06
scale = HD ** (-0.5)
F32 = jnp.float32
BF16 = jnp.bfloat16


def iotas(shape):
    return (
        lax.broadcasted_iota(jnp.int32, shape, 0),
        lax.broadcasted_iota(jnp.int32, shape, 1),
    )


def one_hot(hit):
    return jnp.where(hit, 1.0, 0.0).astype(BF16)


def dot(a, b):
    return jnp.dot(a, b, preferred_element_type=F32)


def dot_nt(a, b):
    return lax.dot_general(a, b, (((1,), (1,)), ((), ())), preferred_element_type=F32)


def dot_tn(a, b):
    return lax.dot_general(a, b, (((0,), (0,)), ((), ())), preferred_element_type=F32)


def dot_rows(a, b):
    return dot_tn(b, a).T


def batch_dot(a, b, left, right):
    return lax.dot_general(
        a, b, (((left,), (right,)), ((0,), (0,))), preferred_element_type=F32
    )


def flat(array):
    split = array.reshape(BLOCK, 2, HEADS, HD).transpose(0, 2, 1, 3)
    return split.reshape(BLOCK * HEADS * 2, HD)


def unflat(rows):
    return rows.reshape(BLOCK, HEADS, 2, HD).transpose(0, 2, 1, 3).reshape(BLOCK, 2, WIDTH)


def call(kernel, grid, in_specs, out_specs, out_shape, flops, nbytes, scratch=(), vmem=60):
    return pl.pallas_call(
        kernel,
        grid=(grid,),
        in_specs=in_specs,
        out_specs=out_specs,
        out_shape=out_shape,
        scratch_shapes=list(scratch),
        compiler_params=pltpu.CompilerParams(vmem_limit_bytes=vmem * 2**20),
        cost_estimate=pl.CostEstimate(flops=flops, bytes_accessed=nbytes, transcendentals=0),
    )


IN_HBM = pl.BlockSpec(memory_space=pltpu.HBM)


def in_hbm(array):
    return pltpu.with_memory_space_constraint(array, pltpu.HBM)


def copy_all(pairs, sems):
    copies = [
        pltpu.make_async_copy(source, target, sems.at[n]) for n, (source, target) in enumerate(pairs)
    ]
    for copy in copies:
        copy.start()
    return copies


def spec(block, *index):
    return pl.BlockSpec(block, lambda i: tuple(i if at == "i" else at for at in index))


def pack_strided_kernel(q_ref, k_ref, v_ref, c_ref, send_ref, rows_ref, out_ref, in_sem, out_sem):
    parts = 4
    size = BLOCK * 8 // parts
    copies = copy_all(
        [
            (ref.at[pl.ds(part * size, size)], rows_ref.at[array, pl.ds(part * size, size)])
            for part in range(parts)
            for array, ref in enumerate((q_ref, k_ref, v_ref, c_ref))
        ],
        in_sem,
    )
    row, col = iotas((128, 256))
    home, head, array, offset = row >> 6, (row >> 4) & 3, (row >> 2) & 3, row & 3
    pick = one_hot(col == array * 64 + ((home * OFFS + offset) * HEADS + head) * 2)
    sent = []
    for part in range(parts):
        for copy in copies[4 * part : 4 * part + 4]:
            copy.wait()
        for at in range(part * 64 // parts, (part + 1) * 64 // parts, 2):
            pair = [
                jnp.concatenate(
                    [rows_ref[array, 64 * n : 64 * (n + 1)] for n in (at, at + 1)], 1
                )
                for array in range(4)
            ]
            picked = dot(pick, jnp.concatenate(pair, 0)).astype(BF16)
            for n in range(2):
                for home in range(2):
                    for head in range(HEADS):
                        row = home * 64 + head * 16
                        out_ref[2 * (at + n) + home, :, head * HD : (head + 1) * HD] = picked[
                            row : row + 16, n * HD : (n + 1) * HD
                        ]
        where = pl.ds(part * NB // parts, NB // parts)
        copy = pltpu.make_async_copy(out_ref.at[where], send_ref.at[where], out_sem.at[part])
        copy.start()
        sent.append(copy)
    for copy in sent:
        copy.wait()


def pack_strided(arrays):
    return call(
        pack_strided_kernel,
        1,
        [IN_HBM] * 4,
        IN_HBM,
        jax.ShapeDtypeStruct((NB, 16, WIDTH), BF16),
        10**9,
        6 * 2**20,
        [
            pltpu.VMEM((4, BLOCK * 8, HD), BF16),
            pltpu.VMEM((NB, 16, WIDTH), BF16),
            pltpu.SemaphoreType.DMA((16,)),
            pltpu.SemaphoreType.DMA((4,)),
        ],
    )(*arrays)


def pack_fixed_kernel(q_ref, k_ref, v_ref, c_ref, out_ref):
    row, col = iotas((64, 128))
    pick = one_hot(col == ((row & 15) * HEADS + (row >> 4)) * 2 + 1)
    for at in range(16):
        rows = [ref[128 * at : 128 * (at + 1)] for ref in (q_ref, k_ref, v_ref, c_ref)]
        picked = dot(pick, jnp.concatenate(rows, 1)).astype(BF16)
        for array in range(4):
            for head in range(HEADS):
                out_ref[array, 16 * at : 16 * (at + 1), head * HD : (head + 1) * HD] = picked[
                    16 * head : 16 * (head + 1), array * HD : (array + 1) * HD
                ]


def pack_fixed(arrays):
    return call(
        pack_fixed_kernel,
        2,
        [spec((2048, HD), "i", 0)] * 4,
        spec((4, BLOCK // 2, WIDTH), 0, "i", 0),
        jax.ShapeDtypeStruct((4, BLOCK, WIDTH), BF16),
        10**9,
        6 * 2**20,
    )(*arrays)


def fixed_probabilities(query, key, summ_key, seen):
    row, col = iotas((BLOCK, BLOCK))
    own = jnp.where(col <= row, dot_nt(query, key) * scale, -jnp.inf)
    far = jnp.where(seen > 0, dot_nt(query, summ_key) * scale, -jnp.inf)
    top = jnp.maximum(
        jnp.max(own, axis=-1, keepdims=True), jnp.max(far, axis=-1, keepdims=True)
    )
    own = jnp.exp(own - top)
    far = jnp.exp(far - top)
    total = jnp.sum(own, axis=-1, keepdims=True) + jnp.sum(far, axis=-1, keepdims=True)
    inverse = 1.0 / total
    return own * inverse, far * inverse


def fixed_forward_kernel(rows_ref, summ_ref, seen_ref, attn_ref, own_ref, far_ref, sums_ref):
    own, far = fixed_probabilities(rows_ref[0], rows_ref[1], summ_ref[:, :HD], seen_ref[...])
    own_ref[0] = own
    far_ref[0] = far
    attn = (
        dot(own.astype(BF16), rows_ref[2]) + dot(far.astype(BF16), summ_ref[:, HD:])
    ).astype(BF16)
    attn_ref[...] = attn
    wide = attn.astype(F32)
    square = jnp.sum(wide * wide, axis=-1, keepdims=True)
    cross = jnp.sum(wide * rows_ref[3].astype(F32), axis=-1, keepdims=True)
    lane = lax.broadcasted_iota(jnp.int32, (BLOCK, 8), 1)
    part = jnp.where(lane == 0, square, jnp.where(lane == 1, cross, 0.0))

    @pl.when(pl.program_id(0) == 0)
    def _():
        sums_ref[...] = part

    @pl.when(pl.program_id(0) > 0)
    def _():
        sums_ref[...] += part


def fixed_forward(rows, summ, seen):
    return call(
        fixed_forward_kernel,
        HEADS,
        [
            spec((4, BLOCK, HD), 0, 0, "i"),
            spec((BLOCK, 2 * HD), 0, "i"),
            spec((1, BLOCK), 0, 0),
        ],
        [
            spec((BLOCK, HD), 0, "i"),
            spec((1, BLOCK, BLOCK), "i", 0, 0),
            spec((1, BLOCK, BLOCK), "i", 0, 0),
            spec((BLOCK, 8), 0, 0),
        ],
        [
            jax.ShapeDtypeStruct((BLOCK, WIDTH), BF16),
            jax.ShapeDtypeStruct((HEADS, BLOCK, BLOCK), F32),
            jax.ShapeDtypeStruct((HEADS, BLOCK, BLOCK), F32),
            jax.ShapeDtypeStruct((BLOCK, 8), F32),
        ],
        4 * 10**9,
        4 * 2**20,
    )(rows, summ, seen)


def swap_matrix():
    row, col = iotas((256, 256))
    return one_hot(col == ((row & 15) << 4) + (row >> 4))


def strided_forward_kernel(
    recv_ref, fixed_ref, keys_out, prob_out, grp_ref, sums_ref, send_ref, keys_ref, prob_ref, sem
):
    swap = swap_matrix()
    for at in range(0, NB, 16):
        rows = dot(swap, recv_ref[at : at + 16].reshape(256, WIDTH)).astype(BF16)
        for head in range(HEADS):
            tiles = rows[:, head * HD : (head + 1) * HD].reshape(4, OFFS, 16, HD)
            keys_ref[head, :, :, at : at + 16, :] = tiles[:3]
            grp_ref[head, 0, :, at : at + 16, :] = tiles[3]
    copies = copy_all([(keys_ref, keys_out)], sem.at[0])
    row, col = iotas((NB, NB))
    square, cross = 0.0, 0.0
    for head in range(HEADS):
        scores = batch_dot(keys_ref[head, 0], keys_ref[head, 1], 2, 2) * scale
        scores = jnp.where((col <= row)[None], scores, -jnp.inf)
        expo = jnp.exp(scores - jnp.max(scores, axis=-1, keepdims=True))
        prob = expo * (1.0 / jnp.sum(expo, axis=-1, keepdims=True))
        attn = batch_dot(prob.astype(BF16), keys_ref[head, 2], 2, 1).astype(BF16)
        prob_ref[head] = prob
        wide = attn.astype(F32)
        square += wide * wide
        cross += wide * grp_ref[head, 0].astype(F32)
        grp_ref[head, 1] = attn
        copies += copy_all([(prob_ref.at[head], prob_out.at[head])], sem.at[head + 1])
    square = jnp.sum(square, axis=-1, keepdims=True)
    cross = jnp.sum(cross, axis=-1, keepdims=True)
    lane = lax.broadcasted_iota(jnp.int32, (NB, HD), 1)
    part = fixed_ref[...]
    for at in range(OFFS):
        part += jnp.where(lane == 8 + at, square[at], jnp.where(lane == 12 + at, cross[at], 0.0))
    sums_ref[...] = part
    send_ref[...] = part.reshape(NB, 1, HD)
    for copy in copies:
        copy.wait()


def strided_forward(recv, fixed_sums):
    return call(
        strided_forward_kernel,
        1,
        [spec((NB, 16, WIDTH), 0, 0, 0), spec((NB, HD), 0, 0)],
        [
            IN_HBM,
            IN_HBM,
            spec((HEADS, 2, OFFS, NB, HD), 0, 0, 0, 0, 0),
            spec((NB, HD), 0, 0),
            spec((NB, 1, HD), 0, 0, 0),
        ],
        [
            pltpu.HBM((HEADS, 3, OFFS, NB, HD), BF16),
            pltpu.HBM((HEADS, OFFS, NB, NB), F32),
            jax.ShapeDtypeStruct((HEADS, 2, OFFS, NB, HD), BF16),
            jax.ShapeDtypeStruct((NB, HD), F32),
            jax.ShapeDtypeStruct((NB, 1, HD), F32),
        ],
        10**9,
        6 * 2**20,
        [
            pltpu.VMEM((HEADS, 3, OFFS, NB, HD), BF16),
            pltpu.VMEM((HEADS, OFFS, NB, NB), F32),
            pltpu.SemaphoreType.DMA((HEADS + 1, 1)),
        ],
        vmem=VMEM3,
    )(recv, fixed_sums)


def normalize(wide, cotangent, square, cross):
    scaling = lax.rsqrt(square / (2 * COLS) + epsilon)
    normed = (wide * scaling).astype(BF16)
    grad = (
        scaling * cotangent.astype(F32) - wide * (scaling * scaling * scaling * cross / (2 * COLS))
    ).astype(BF16)
    return normed, grad, jnp.sum(grad.astype(F32) * wide, axis=-1, keepdims=True)


def strided_backward_kernel(
    keys_in, prob_in, grp_ref, sums_ref, other_ref, recv_ref, send_out,
    keys_ref, prob_ref, out_ref, send_ref, in_sem, out_sem,
):
    fetched = [
        copy_all(
            [(keys_in.at[head], keys_ref.at[head]), (prob_in.at[head], prob_ref.at[head])],
            in_sem.at[head],
        )
        for head in range(HEADS)
    ]
    moved = recv_ref[...].reshape(NB, HD)
    total = sums_ref[:, 8:16] + other_ref[...] + moved[:, :8]
    square = jnp.stack([total[:, at : at + 1] for at in range(OFFS)])
    cross = jnp.stack([total[:, OFFS + at : OFFS + at + 1] for at in range(OFFS)])
    grads = []
    for head in range(HEADS):
        wide = grp_ref[head, 1].astype(F32)
        normed, grad, row_dot = normalize(wide, grp_ref[head, 0], square, cross)
        out_ref[head, 0] = normed
        grads.append((grad, row_dot))
    for head in range(HEADS):
        for copy in fetched[head]:
            copy.wait()
        grad, row_dot = grads[head]
        prob = prob_ref[head]
        grad_prob = batch_dot(grad, keys_ref[head, 2], 2, 2)
        grad_score = (prob * (grad_prob - row_dot) * scale).astype(BF16)
        out_ref[head, 1] = batch_dot(grad_score, keys_ref[head, 1], 2, 1).astype(BF16)
        out_ref[head, 2] = batch_dot(grad_score, keys_ref[head, 0], 1, 1).astype(BF16)
        out_ref[head, 3] = batch_dot(prob.astype(BF16), grad, 1, 1).astype(BF16)
    swap = swap_matrix()
    copies = []
    for at in range(0, NB, 16):
        rows = [out_ref[head, :, :, at : at + 16, :].reshape(256, HD) for head in range(HEADS)]
        moved = dot(swap, jnp.concatenate(rows, 1)).astype(BF16)
        send_ref[at : at + 16] = moved.reshape(16, 16, WIDTH)
        where = pl.ds(at, 16)
        copies += copy_all([(send_ref.at[where], send_out.at[where])], out_sem.at[at // 16])
    for copy in copies:
        copy.wait()


def strided_backward(keys, prob, grp, sums, other, recv):
    return call(
        strided_backward_kernel,
        1,
        [
            IN_HBM,
            IN_HBM,
            spec((HEADS, 2, OFFS, NB, HD), 0, 0, 0, 0, 0),
            spec((NB, HD), 0, 0),
            spec((NB, 8), 0, 0),
            spec((NB, 1, HD), 0, 0, 0),
        ],
        IN_HBM,
        pltpu.HBM((NB, 16, WIDTH), BF16),
        10**9,
        6 * 2**20,
        [
            pltpu.VMEM((HEADS, 3, OFFS, NB, HD), BF16),
            pltpu.VMEM((HEADS, OFFS, NB, NB), F32),
            pltpu.VMEM((HEADS, 4, OFFS, NB, HD), BF16),
            pltpu.VMEM((NB, 16, WIDTH), BF16),
            pltpu.SemaphoreType.DMA((HEADS, 2)),
            pltpu.SemaphoreType.DMA((NB // 16, 1)),
        ],
        vmem=VMEM4,
    )(in_hbm(keys), in_hbm(prob), grp, sums, other, recv)


def summary_backward_kernel(
    rows_ref, summ_ref, far_ref, attn_ref, sums_ref, query_ref, keep_ref, send_ref
):
    wide = attn_ref[...].astype(F32)
    _, grad, row_dot = normalize(wide, rows_ref[3], sums_ref[:, 0:1], sums_ref[:, 1:2])
    far = far_ref[0]
    score = (far * (dot_nt(grad, summ_ref[:, HD:]) - row_dot) * scale).astype(BF16)
    query_ref[...] = dot(score, summ_ref[:, :HD])
    key = dot_rows(score, rows_ref[0])
    value = dot_rows(far.astype(BF16), grad)
    half = BLOCK // 2
    send_ref[:, :HD] = key[half:].astype(BF16)
    send_ref[:, HD:] = value[half:].astype(BF16)
    keep_ref[:, :HD] = key[:half]
    keep_ref[:, HD:] = value[:half]


def summary_backward(rows, summ, far, attn, sums):
    return call(
        summary_backward_kernel,
        HEADS,
        [
            spec((4, BLOCK, HD), 0, 0, "i"),
            spec((BLOCK, 2 * HD), 0, "i"),
            spec((1, BLOCK, BLOCK), "i", 0, 0),
            spec((BLOCK, HD), 0, "i"),
            spec((BLOCK, 2), 0, 0),
        ],
        [
            spec((BLOCK, HD), 0, "i"),
            spec((BLOCK // 2, 2 * HD), 0, "i"),
            spec((BLOCK // 2, 2 * HD), 0, "i"),
        ],
        [
            jax.ShapeDtypeStruct((BLOCK, WIDTH), F32),
            jax.ShapeDtypeStruct((BLOCK // 2, 2 * WIDTH), F32),
            jax.ShapeDtypeStruct((BLOCK // 2, 2 * WIDTH), BF16),
        ],
        3 * 10**9,
        8 * 2**20,
    )(rows, summ, far, attn, sums)


def fixed_backward_kernel(rows_ref, own_ref, attn_ref, sums_ref, query_ref, out_ref, tail_ref):
    query, key, value = rows_ref[0], rows_ref[1], rows_ref[2]
    own = own_ref[0]
    wide = attn_ref[...].astype(F32)
    normed, grad, row_dot = normalize(wide, rows_ref[3], sums_ref[:, 0:1], sums_ref[:, 1:2])
    out_ref[0] = normed
    score = (own * (dot_nt(grad, value) - row_dot) * scale).astype(BF16)
    out_ref[1] = (dot(score, key) + query_ref[...]).astype(BF16)
    for at, grads in enumerate((dot_rows(score, query), dot_rows(own.astype(BF16), grad))):
        out_ref[2 + at] = grads.astype(BF16)
        tail_ref[at] = grads[BLOCK - 8 :]


def fixed_backward(rows, own, attn, sums, far_query):
    return call(
        fixed_backward_kernel,
        HEADS,
        [
            spec((4, BLOCK, HD), 0, 0, "i"),
            spec((1, BLOCK, BLOCK), "i", 0, 0),
            spec((BLOCK, HD), 0, "i"),
            spec((BLOCK, 2), 0, 0),
            spec((BLOCK, HD), 0, "i"),
        ],
        [spec((4, BLOCK, HD), 0, 0, "i"), spec((2, 8, HD), 0, 0, "i")],
        [
            pltpu.HBM((4, BLOCK, WIDTH), BF16),
            jax.ShapeDtypeStruct((2, 8, WIDTH), F32),
        ],
        5 * 10**9,
        8 * 2**20,
    )(rows, own, attn, sums, far_query)


def unpack_kernel(recv_ref, fixed_in, tail_ref, *refs):
    outs, fixed_ref, out_ref, in_sem, out_sem = refs[:4], refs[4], refs[5], refs[6], refs[7]
    parts = 4
    size = BLOCK // parts
    copies = copy_all(
        [
            (fixed_in.at[:, pl.ds(part * size, size)], fixed_ref.at[:, pl.ds(part * size, size)])
            for part in range(parts)
        ],
        in_sem,
    )
    sent = []
    row, col = iotas((512, 256))
    array, token, head, kind = row >> 7, (row >> 3) & 15, (row >> 1) & 3, row & 1
    source = (token >> 2) * 64 + head * 16 + array * OFFS + (token & 3)
    strided_pick = one_hot((kind == 0) & (col == source))
    row, col = iotas((128, 64))
    token, head, kind = row >> 3, (row >> 1) & 3, row & 1
    own_pick = one_hot((kind == 1) & (col == head * 16 + token))
    end = lax.broadcasted_iota(jnp.int32, (16, WIDTH), 0) >= 16 - SUMM
    for at in range(0, 32, 2):
        if at * 16 % size == 0:
            copies[at * 16 // size].wait()
        rows = [
            jnp.concatenate(
                [
                    recv_ref[4 * n + home, :, head * HD : (head + 1) * HD]
                    for home in range(4)
                    for head in range(HEADS)
                ],
                0,
            )
            for n in (at, at + 1)
        ]
        strided = dot(strided_pick, jnp.concatenate(rows, 1))
        for n in range(2):
            tile = 16 * (at + n)
            fixed = [fixed_ref[array, tile : tile + 16] for array in range(4)]
            if tile == BLOCK - 16:
                for array in (2, 3):
                    fixed[array] = jnp.where(end, tail_ref[array - 2], fixed[array])
            rows = [
                jnp.concatenate([part[:, head * HD : (head + 1) * HD] for part in fixed], 1)
                for head in range(HEADS)
            ]
            own = dot(own_pick, jnp.concatenate(rows, 0))
            for array in range(4):
                out_ref[array, 8 * tile : 8 * tile + 128] = (
                    strided[array * 128 : (array + 1) * 128, n * HD : (n + 1) * HD]
                    + own[:, array * HD : (array + 1) * HD]
                ).astype(BF16)
        if (at + 2) * 16 % size == 0:
            part = at * 16 // size
            where = pl.ds(part * size * 8, size * 8)
            sent += copy_all(
                [(out_ref.at[array, where], outs[array].at[where]) for array in range(4)],
                out_sem.at[part],
            )
    for copy in sent:
        copy.wait()


def unpack(recv, fixed, tail):
    rows = call(
        unpack_kernel,
        1,
        [spec((NB, 16, WIDTH), 0, 0, 0), IN_HBM, spec((2, 16, WIDTH), 0, 0, 0)],
        [IN_HBM] * 4,
        [jax.ShapeDtypeStruct((BLOCK * 8, HD), BF16)] * 4,
        2 * 10**9,
        8 * 2**20,
        [
            pltpu.VMEM((4, BLOCK, WIDTH), BF16),
            pltpu.VMEM((4, BLOCK * 8, HD), BF16),
            pltpu.SemaphoreType.DMA((4,)),
            pltpu.SemaphoreType.DMA((4, 4)),
        ],
        vmem=VMEM6,
    )(recv, in_hbm(fixed), tail)
    return tuple(unflat(array) for array in rows)


def place(index):
    coords = []
    for size in PARTS[::-1]:
        coords.append(index % size)
        index = index // size
    return coords[::-1]


def joined(coords):
    index = 0
    for size, at in zip(PARTS, coords):
        index = index * size + at
    return index


def shift(array, part, step):
    perm = []
    for source in range(NB):
        coords = place(source)
        coords[part] = (coords[part] + step) % PARTS[part]
        perm.append((source, joined(coords)))
    return lax.ppermute(array, "seq", perm)


def other_head(array):
    return lax.ppermute(array, "head", [(0, 1), (1, 0)])


ROUNDS = (
    ((0, -1, 1),),
    ((0, -2, 2), (0, -4, 2), (0, 2, 2)),
    ((1, 1, 8),),
    ((2, 1, 16), (2, -1, 16), (2, 2, 16)),
    ((3, 1, 64),),
)


def gather_along_z(own, me):
    size = PARTS[0]
    step = NB // size
    groups = [[at + step * z for z in range(size)] for at in range(step)]
    sent = jnp.broadcast_to(own[None], (size,) + own.shape)
    held = lax.all_to_all(sent, "seq", 0, 0, axis_index_groups=groups, tiled=True)
    held = jnp.concatenate([held, held], 0)
    held = lax.dynamic_slice_in_dim(held, me // step, size, 0)
    return held.reshape(size * SUMM, 2 * WIDTH)


def gather_summaries(held):
    for steps in ROUNDS[2:]:
        moved = [shift(held[: slots * SUMM], part, step) for part, step, slots in steps]
        held = jnp.concatenate([held] + moved, 0)
    return held


def scatter_first(total, sent):
    ((part, step, _),) = ROUNDS[-1]
    return total + shift(sent, part, -step).astype(F32)


def scatter_summaries(parts, rounds):
    for steps in rounds[::-1]:
        kept = parts.shape[0] - SUMM * sum(slots for _, _, slots in steps)
        total, at = parts[:kept], kept
        for part, step, slots in steps:
            rows = slots * SUMM
            moved = shift(parts[at : at + rows].astype(BF16), part, -step).astype(F32)
            total = total + jnp.pad(moved, ((0, kept - rows), (0, 0)))
            at += rows
        parts = total
    return parts


def slot_blocks(me):
    back = [(0,) * len(PARTS)]
    for steps in ROUNDS:
        back = back + [
            tuple(by + step * (at == part) for at, by in enumerate(slot))
            for part, step, slots in steps
            for slot in back[:slots]
        ]
    back = jnp.array(back, jnp.int32)
    coords = [(at - back[:, n]) % size for n, (at, size) in enumerate(zip(place(me), PARTS))]
    return joined(coords)


def shards(queries, key_rows, value_rows, cotangent):
    me = lax.axis_index("seq")
    arrays = tuple(flat(array) for array in (queries, key_rows, value_rows, cotangent))
    send = pack_strided(arrays)
    tails = [a[BLOCK - SUMM :, 1].reshape(SUMM, HEADS, 1, HD) for a in (key_rows, value_rows)]
    own_summ = jnp.concatenate(tails, 2).reshape(SUMM, 2 * WIDTH)
    summ = gather_along_z(own_summ, me)
    send, summ = lax.optimization_barrier((send, summ))
    recv = lax.all_to_all(send, "seq", 0, 0, tiled=True)
    summ = gather_summaries(summ)
    seen = jnp.repeat((slot_blocks(me) < me).astype(jnp.int32), SUMM)[None]
    rows = pack_fixed(arrays)
    fixed_attn, own_prob, far_prob, fixed_sums = fixed_forward(rows, summ, seen)
    fixed_send = fixed_sums[:, :2].reshape(NB, OFFS, 2).transpose(0, 2, 1).reshape(NB, 8)
    fixed_both = fixed_send + other_head(fixed_send)
    keys, prob, grp, sums, sums_send = strided_forward(recv, jnp.pad(fixed_both, ((0, 0), (0, HD - 8))))
    sums_in = lax.all_to_all(sums_send, "seq", 0, 0, tiled=True)
    sums_other = other_head(sums[:, 8:16])
    own_sums = sums_in[:, 0, 8:16]
    block_sums = fixed_both + own_sums + other_head(own_sums)
    send_back = strided_backward(keys, prob, grp, sums, sums_other, sums_in)
    send_back, block_sums = lax.optimization_barrier((send_back, block_sums))
    recv_back = lax.all_to_all(send_back, "seq", 0, 0, tiled=True)
    block_sums = block_sums.reshape(NB, 2, OFFS).transpose(0, 2, 1).reshape(BLOCK, 2)
    far_query, kept, sent = summary_backward(rows, summ, far_prob, fixed_attn, block_sums)
    fixed_out, tails = fixed_backward(rows, own_prob, fixed_attn, block_sums, far_query)
    parts = scatter_summaries(scatter_first(kept, sent), ROUNDS[3:4])
    parts, fixed_out, tails = lax.optimization_barrier((parts, fixed_out, tails))
    totals = scatter_summaries(parts, ROUNDS[:3]).reshape(SUMM, HEADS, 2, HD)
    totals = totals.transpose(2, 0, 1, 3).reshape(2, SUMM, WIDTH)
    totals = (tails[:, 8 - SUMM :] + totals).astype(BF16)
    tail = jnp.pad(totals, ((0, 0), (16 - SUMM, 0), (0, 0)))
    return unpack(recv_back, fixed_out, tail)


def solution(mesh):
    specs = (P("seq", None, "head"),) * 4
    return jax.shard_map(shards, mesh=mesh, in_specs=specs, out_specs=specs, check_vma=False)
```

```python
import jax
import jax.numpy as jnp
from jax import lax
from jax.experimental import pallas as pl
from jax.experimental.pallas import tpu as pltpu
from jax.sharding import PartitionSpec as P

BLOCK = 512
SUMM = 4
HD = 128
COLS = 1024
NB = 128
HEADS = 4
OFFS = 4
WIDTH = HEADS * HD
PARTS = (8, 2, 4, 2)
VMEM3, VMEM4, VMEM5, VMEM6 = 32, 32, 48, 32

epsilon = 1e-06
scale = HD ** (-0.5)
F32 = jnp.float32
BF16 = jnp.bfloat16


def iotas(shape):
    return (
        lax.broadcasted_iota(jnp.int32, shape, 0),
        lax.broadcasted_iota(jnp.int32, shape, 1),
    )


def one_hot(hit):
    return jnp.where(hit, 1.0, 0.0).astype(BF16)


def dot(a, b):
    return jnp.dot(a, b, preferred_element_type=F32)


def dot_nt(a, b):
    return lax.dot_general(a, b, (((1,), (1,)), ((), ())), preferred_element_type=F32)


def dot_tn(a, b):
    return lax.dot_general(a, b, (((0,), (0,)), ((), ())), preferred_element_type=F32)


def dot_rows(a, b):
    return dot_tn(b, a).T


def batch_dot(a, b, left, right):
    return lax.dot_general(
        a, b, (((left,), (right,)), ((0,), (0,))), preferred_element_type=F32
    )


def flat(array):
    split = array.reshape(BLOCK, 2, HEADS, HD).transpose(0, 2, 1, 3)
    return split.reshape(BLOCK * HEADS * 2, HD)


def unflat(rows):
    return rows.reshape(BLOCK, HEADS, 2, HD).transpose(0, 2, 1, 3).reshape(BLOCK, 2, WIDTH)


def call(kernel, grid, in_specs, out_specs, out_shape, flops, nbytes, scratch=(), vmem=60):
    return pl.pallas_call(
        kernel,
        grid=(grid,),
        in_specs=in_specs,
        out_specs=out_specs,
        out_shape=out_shape,
        scratch_shapes=list(scratch),
        compiler_params=pltpu.CompilerParams(vmem_limit_bytes=vmem * 2**20),
        cost_estimate=pl.CostEstimate(flops=flops, bytes_accessed=nbytes, transcendentals=0),
    )


IN_HBM = pl.BlockSpec(memory_space=pltpu.HBM)


def in_hbm(array):
    return pltpu.with_memory_space_constraint(array, pltpu.HBM)


def copy_all(pairs, sems):
    copies = [
        pltpu.make_async_copy(source, target, sems.at[n]) for n, (source, target) in enumerate(pairs)
    ]
    for copy in copies:
        copy.start()
    return copies


def spec(block, *index):
    return pl.BlockSpec(block, lambda i: tuple(i if at == "i" else at for at in index))


def pack_strided_kernel(q_ref, k_ref, v_ref, c_ref, send_ref, rows_ref, out_ref, in_sem, out_sem):
    parts = 4
    size = BLOCK * 8 // parts
    copies = copy_all(
        [
            (ref.at[pl.ds(part * size, size)], rows_ref.at[array, pl.ds(part * size, size)])
            for part in range(parts)
            for array, ref in enumerate((q_ref, k_ref, v_ref, c_ref))
        ],
        in_sem,
    )
    row, col = iotas((128, 256))
    home, head, array, offset = row >> 6, (row >> 4) & 3, (row >> 2) & 3, row & 3
    pick = one_hot(col == array * 64 + ((home * OFFS + offset) * HEADS + head) * 2)
    sent = []
    for part in range(parts):
        for copy in copies[4 * part : 4 * part + 4]:
            copy.wait()
        for at in range(part * 64 // parts, (part + 1) * 64 // parts, 2):
            pair = [
                jnp.concatenate(
                    [rows_ref[array, 64 * n : 64 * (n + 1)] for n in (at, at + 1)], 1
                )
                for array in range(4)
            ]
            picked = dot(pick, jnp.concatenate(pair, 0)).astype(BF16)
            for n in range(2):
                for home in range(2):
                    for head in range(HEADS):
                        row = home * 64 + head * 16
                        out_ref[2 * (at + n) + home, :, head * HD : (head + 1) * HD] = picked[
                            row : row + 16, n * HD : (n + 1) * HD
                        ]
        where = pl.ds(part * NB // parts, NB // parts)
        copy = pltpu.make_async_copy(out_ref.at[where], send_ref.at[where], out_sem.at[part])
        copy.start()
        sent.append(copy)
    for copy in sent:
        copy.wait()


def pack_strided(arrays):
    return call(
        pack_strided_kernel,
        1,
        [IN_HBM] * 4,
        IN_HBM,
        jax.ShapeDtypeStruct((NB, 16, WIDTH), BF16),
        10**9,
        6 * 2**20,
        [
            pltpu.VMEM((4, BLOCK * 8, HD), BF16),
            pltpu.VMEM((NB, 16, WIDTH), BF16),
            pltpu.SemaphoreType.DMA((16,)),
            pltpu.SemaphoreType.DMA((4,)),
        ],
    )(*arrays)


def pack_fixed_kernel(q_ref, k_ref, v_ref, c_ref, out_ref):
    row, col = iotas((64, 128))
    pick = one_hot(col == ((row & 15) * HEADS + (row >> 4)) * 2 + 1)
    for at in range(16):
        rows = [ref[128 * at : 128 * (at + 1)] for ref in (q_ref, k_ref, v_ref, c_ref)]
        picked = dot(pick, jnp.concatenate(rows, 1)).astype(BF16)
        for array in range(4):
            for head in range(HEADS):
                out_ref[array, 16 * at : 16 * (at + 1), head * HD : (head + 1) * HD] = picked[
                    16 * head : 16 * (head + 1), array * HD : (array + 1) * HD
                ]


def pack_fixed(arrays):
    return call(
        pack_fixed_kernel,
        2,
        [spec((2048, HD), "i", 0)] * 4,
        spec((4, BLOCK // 2, WIDTH), 0, "i", 0),
        jax.ShapeDtypeStruct((4, BLOCK, WIDTH), BF16),
        10**9,
        6 * 2**20,
    )(*arrays)


def fixed_probabilities(query, key, summ_key, seen):
    row, col = iotas((BLOCK, BLOCK))
    own = jnp.where(col <= row, dot_nt(query, key) * scale, -jnp.inf)
    far = jnp.where(seen > 0, dot_nt(query, summ_key) * scale, -jnp.inf)
    top = jnp.maximum(
        jnp.max(own, axis=-1, keepdims=True), jnp.max(far, axis=-1, keepdims=True)
    )
    own = jnp.exp(own - top)
    far = jnp.exp(far - top)
    total = jnp.sum(own, axis=-1, keepdims=True) + jnp.sum(far, axis=-1, keepdims=True)
    inverse = 1.0 / total
    return own * inverse, far * inverse


def fixed_forward_kernel(rows_ref, summ_ref, seen_ref, attn_ref, own_ref, far_ref, sums_ref):
    own, far = fixed_probabilities(rows_ref[0], rows_ref[1], summ_ref[:, :HD], seen_ref[...])
    own_ref[0] = own.astype(BF16)
    far_ref[0] = far.astype(BF16)
    attn = (dot(own_ref[0], rows_ref[2]) + dot(far_ref[0], summ_ref[:, HD:])).astype(BF16)
    attn_ref[...] = attn
    wide = attn.astype(F32)
    square = jnp.sum(wide * wide, axis=-1, keepdims=True)
    cross = jnp.sum(wide * rows_ref[3].astype(F32), axis=-1, keepdims=True)
    lane = lax.broadcasted_iota(jnp.int32, (BLOCK, 8), 1)
    part = jnp.where(lane == 0, square, jnp.where(lane == 1, cross, 0.0))

    @pl.when(pl.program_id(0) == 0)
    def _():
        sums_ref[...] = part

    @pl.when(pl.program_id(0) > 0)
    def _():
        sums_ref[...] += part


def fixed_forward(rows, summ, seen):
    return call(
        fixed_forward_kernel,
        HEADS,
        [
            spec((4, BLOCK, HD), 0, 0, "i"),
            spec((BLOCK, 2 * HD), 0, "i"),
            spec((1, BLOCK), 0, 0),
        ],
        [
            spec((BLOCK, HD), 0, "i"),
            spec((1, BLOCK, BLOCK), "i", 0, 0),
            spec((1, BLOCK, BLOCK), "i", 0, 0),
            spec((BLOCK, 8), 0, 0),
        ],
        [
            jax.ShapeDtypeStruct((BLOCK, WIDTH), BF16),
            pltpu.HBM((HEADS, BLOCK, BLOCK), BF16),
            pltpu.HBM((HEADS, BLOCK, BLOCK), BF16),
            jax.ShapeDtypeStruct((BLOCK, 8), F32),
        ],
        4 * 10**9,
        4 * 2**20,
    )(rows, summ, seen)


def swap_matrix():
    row, col = iotas((256, 256))
    return one_hot(col == ((row & 15) << 4) + (row >> 4))


def strided_forward_kernel(
    recv_ref, fixed_ref, keys_out, prob_out, grp_ref, sums_ref, send_ref, keys_ref, prob_ref, sem
):
    swap = swap_matrix()
    for at in range(0, NB, 16):
        rows = dot(swap, recv_ref[at : at + 16].reshape(256, WIDTH)).astype(BF16)
        for head in range(HEADS):
            tiles = rows[:, head * HD : (head + 1) * HD].reshape(4, OFFS, 16, HD)
            keys_ref[head, :, :, at : at + 16, :] = tiles[:3]
            grp_ref[head, 0, :, at : at + 16, :] = tiles[3]
    copies = copy_all([(keys_ref, keys_out)], sem.at[0])
    row, col = iotas((NB, NB))
    square, cross = 0.0, 0.0
    for head in range(HEADS):
        scores = batch_dot(keys_ref[head, 0], keys_ref[head, 1], 2, 2) * scale
        scores = jnp.where((col <= row)[None], scores, -jnp.inf)
        expo = jnp.exp(scores - jnp.max(scores, axis=-1, keepdims=True))
        prob = (expo * (1.0 / jnp.sum(expo, axis=-1, keepdims=True))).astype(BF16)
        attn = batch_dot(prob, keys_ref[head, 2], 2, 1).astype(BF16)
        prob_ref[head] = prob
        copies += copy_all([(prob_ref.at[head], prob_out.at[head])], sem.at[head + 1])
        wide = attn.astype(F32)
        square += wide * wide
        cross += wide * grp_ref[head, 0].astype(F32)
        grp_ref[head, 1] = attn
    square = jnp.sum(square, axis=-1, keepdims=True)
    cross = jnp.sum(cross, axis=-1, keepdims=True)
    lane = lax.broadcasted_iota(jnp.int32, (NB, HD), 1)
    part = fixed_ref[...]
    for at in range(OFFS):
        part += jnp.where(lane == 8 + at, square[at], jnp.where(lane == 12 + at, cross[at], 0.0))
    sums_ref[...] = part
    send_ref[...] = part.reshape(NB, 1, HD)
    for copy in copies:
        copy.wait()


def strided_forward(recv, fixed_sums):
    return call(
        strided_forward_kernel,
        1,
        [spec((NB, 16, WIDTH), 0, 0, 0), spec((NB, HD), 0, 0)],
        [
            IN_HBM,
            IN_HBM,
            spec((HEADS, 2, OFFS, NB, HD), 0, 0, 0, 0, 0),
            spec((NB, HD), 0, 0),
            spec((NB, 1, HD), 0, 0, 0),
        ],
        [
            pltpu.HBM((HEADS, 3, OFFS, NB, HD), BF16),
            pltpu.HBM((HEADS, OFFS, NB, NB), BF16),
            jax.ShapeDtypeStruct((HEADS, 2, OFFS, NB, HD), BF16),
            jax.ShapeDtypeStruct((NB, HD), F32),
            jax.ShapeDtypeStruct((NB, 1, HD), F32),
        ],
        10**9,
        6 * 2**20,
        [
            pltpu.VMEM((HEADS, 3, OFFS, NB, HD), BF16),
            pltpu.VMEM((HEADS, OFFS, NB, NB), BF16),
            pltpu.SemaphoreType.DMA((HEADS + 1, 1)),
        ],
        vmem=VMEM3,
    )(recv, fixed_sums)


def normalize(wide, cotangent, square, cross):
    scaling = lax.rsqrt(square / (2 * COLS) + epsilon)
    normed = (wide * scaling).astype(BF16)
    grad = (
        scaling * cotangent.astype(F32) - wide * (scaling * scaling * scaling * cross / (2 * COLS))
    ).astype(BF16)
    return normed, grad, jnp.sum(grad.astype(F32) * wide, axis=-1, keepdims=True)


def strided_backward_kernel(
    keys_in, prob_in, grp_ref, sums_ref, other_ref, recv_ref, send_out,
    keys_ref, prob_ref, out_ref, send_ref, in_sem, out_sem,
):
    fetched = [
        copy_all(
            [(keys_in.at[head], keys_ref.at[head]), (prob_in.at[head], prob_ref.at[head])],
            in_sem.at[head],
        )
        for head in range(HEADS)
    ]
    moved = recv_ref[...].reshape(NB, HD)
    total = sums_ref[:, 8:16] + other_ref[...] + moved[:, :8]
    square = jnp.stack([total[:, at : at + 1] for at in range(OFFS)])
    cross = jnp.stack([total[:, OFFS + at : OFFS + at + 1] for at in range(OFFS)])
    grads = []
    for head in range(HEADS):
        wide = grp_ref[head, 1].astype(F32)
        normed, grad, row_dot = normalize(wide, grp_ref[head, 0], square, cross)
        out_ref[head, 0] = normed
        grads.append((grad, row_dot))
    for head in range(HEADS):
        for copy in fetched[head]:
            copy.wait()
        grad, row_dot = grads[head]
        prob = prob_ref[head]
        grad_prob = batch_dot(grad, keys_ref[head, 2], 2, 2)
        grad_score = (prob.astype(F32) * (grad_prob - row_dot) * scale).astype(BF16)
        out_ref[head, 1] = batch_dot(grad_score, keys_ref[head, 1], 2, 1).astype(BF16)
        out_ref[head, 2] = batch_dot(grad_score, keys_ref[head, 0], 1, 1).astype(BF16)
        out_ref[head, 3] = batch_dot(prob, grad, 1, 1).astype(BF16)
    swap = swap_matrix()
    copies = []
    for at in range(0, NB, 16):
        rows = [out_ref[head, :, :, at : at + 16, :].reshape(256, HD) for head in range(HEADS)]
        moved = dot(swap, jnp.concatenate(rows, 1)).astype(BF16)
        send_ref[at : at + 16] = moved.reshape(16, 16, WIDTH)
        where = pl.ds(at, 16)
        copies += copy_all([(send_ref.at[where], send_out.at[where])], out_sem.at[at // 16])
    for copy in copies:
        copy.wait()


def strided_backward(keys, prob, grp, sums, other, recv):
    return call(
        strided_backward_kernel,
        1,
        [
            IN_HBM,
            IN_HBM,
            spec((HEADS, 2, OFFS, NB, HD), 0, 0, 0, 0, 0),
            spec((NB, HD), 0, 0),
            spec((NB, 8), 0, 0),
            spec((NB, 1, HD), 0, 0, 0),
        ],
        IN_HBM,
        pltpu.HBM((NB, 16, WIDTH), BF16),
        10**9,
        6 * 2**20,
        [
            pltpu.VMEM((HEADS, 3, OFFS, NB, HD), BF16),
            pltpu.VMEM((HEADS, OFFS, NB, NB), BF16),
            pltpu.VMEM((HEADS, 4, OFFS, NB, HD), BF16),
            pltpu.VMEM((NB, 16, WIDTH), BF16),
            pltpu.SemaphoreType.DMA((HEADS, 2)),
            pltpu.SemaphoreType.DMA((NB // 16, 1)),
        ],
        vmem=VMEM4,
    )(in_hbm(keys), in_hbm(prob), grp, sums, other, recv)


def summary_backward_kernel(
    rows_in, summ_in, far_in, attn_in, sums_ref, query_ref, keep_ref, send_ref,
    attn_ref, cot_ref, summ_ref, rows_ref, far_ref, sem,
):
    copies = copy_all(
        [
            (attn_in, attn_ref),
            (rows_in.at[3], cot_ref),
            (summ_in, summ_ref),
            (rows_in.at[0], rows_ref),
        ]
        + [(far_in.at[head], far_ref.at[head]) for head in range(HEADS)],
        sem,
    )
    for copy in copies[:4]:
        copy.wait()
    for head in range(HEADS):
        copies[4 + head].wait()
        at = slice(head * HD, (head + 1) * HD)
        to_key = slice(2 * head * HD, (2 * head + 1) * HD)
        to_value = slice((2 * head + 1) * HD, (2 * head + 2) * HD)
        _, grad, row_dot = normalize(
            attn_ref[:, at].astype(F32), cot_ref[:, at], sums_ref[:, 0:1], sums_ref[:, 1:2]
        )
        far = far_ref[head]
        score = far.astype(F32) * (dot_nt(grad, summ_ref[:, to_value]) - row_dot) * scale
        score = score.astype(BF16)
        query_ref[:, at] = dot(score, summ_ref[:, to_key])
        for to, grads in ((to_key, dot_rows(score, rows_ref[:, at])), (to_value, dot_rows(far, grad))):
            grads = grads.reshape(2, 8, 2, 16, HD)
            keep = jnp.stack([grads[0, :, 0], grads[1, :, 1]], 1)
            send = jnp.stack([grads[1, :, 0], grads[0, :, 1]], 1)
            keep_ref[:, to] = keep.reshape(BLOCK // 2, HD)
            send_ref[:, to] = send.reshape(BLOCK // 2, HD).astype(BF16)


def summary_backward(rows, summ, far, attn, sums):
    return call(
        summary_backward_kernel,
        1,
        [IN_HBM] * 4 + [spec((BLOCK, 2), 0, 0)],
        [
            spec((BLOCK, WIDTH), 0, 0),
            spec((BLOCK // 2, 2 * WIDTH), 0, 0),
            spec((BLOCK // 2, 2 * WIDTH), 0, 0),
        ],
        [
            pltpu.HBM((BLOCK, WIDTH), F32),
            jax.ShapeDtypeStruct((BLOCK // 2, 2 * WIDTH), F32),
            jax.ShapeDtypeStruct((BLOCK // 2, 2 * WIDTH), BF16),
        ],
        3 * 10**9,
        8 * 2**20,
        [
            pltpu.VMEM((BLOCK, WIDTH), BF16),
            pltpu.VMEM((BLOCK, WIDTH), BF16),
            pltpu.VMEM((BLOCK, 2 * WIDTH), BF16),
            pltpu.VMEM((BLOCK, WIDTH), BF16),
            pltpu.VMEM((HEADS, BLOCK, BLOCK), BF16),
            pltpu.SemaphoreType.DMA((8,)),
        ],
        vmem=VMEM5,
    )(*[in_hbm(array) for array in (rows, summ, far, attn)], sums)


def fixed_backward_kernel(rows_ref, own_ref, attn_ref, sums_ref, query_ref, out_ref, tail_ref):
    query, key, value = rows_ref[0], rows_ref[1], rows_ref[2]
    own = own_ref[0]
    wide = attn_ref[...].astype(F32)
    normed, grad, row_dot = normalize(wide, rows_ref[3], sums_ref[:, 0:1], sums_ref[:, 1:2])
    out_ref[0] = normed
    score = (own.astype(F32) * (dot_nt(grad, value) - row_dot) * scale).astype(BF16)
    out_ref[1] = (dot(score, key) + query_ref[...]).astype(BF16)
    for at, grads in enumerate((dot_rows(score, query), dot_rows(own, grad))):
        out_ref[2 + at] = grads.astype(BF16)
        tail_ref[at] = grads[BLOCK - 8 :]


def fixed_backward(rows, own, attn, sums, far_query):
    return call(
        fixed_backward_kernel,
        HEADS,
        [
            spec((4, BLOCK, HD), 0, 0, "i"),
            spec((1, BLOCK, BLOCK), "i", 0, 0),
            spec((BLOCK, HD), 0, "i"),
            spec((BLOCK, 2), 0, 0),
            spec((BLOCK, HD), 0, "i"),
        ],
        [spec((4, BLOCK, HD), 0, 0, "i"), spec((2, 8, HD), 0, 0, "i")],
        [
            pltpu.HBM((4, BLOCK, WIDTH), BF16),
            jax.ShapeDtypeStruct((2, 8, WIDTH), F32),
        ],
        5 * 10**9,
        8 * 2**20,
    )(rows, own, attn, sums, far_query)


def unpack_kernel(recv_ref, fixed_in, tail_ref, *refs):
    outs, fixed_ref, out_ref, in_sem, out_sem = refs[:4], refs[4], refs[5], refs[6], refs[7]
    parts = 4
    size = BLOCK // parts
    copies = copy_all(
        [
            (fixed_in.at[:, pl.ds(part * size, size)], fixed_ref.at[:, pl.ds(part * size, size)])
            for part in range(parts)
        ],
        in_sem,
    )
    sent = []
    row, col = iotas((512, 256))
    array, token, head, kind = row >> 7, (row >> 3) & 15, (row >> 1) & 3, row & 1
    source = (token >> 2) * 64 + head * 16 + array * OFFS + (token & 3)
    strided_pick = one_hot((kind == 0) & (col == source))
    row, col = iotas((128, 64))
    token, head, kind = row >> 3, (row >> 1) & 3, row & 1
    own_pick = one_hot((kind == 1) & (col == head * 16 + token))
    end = lax.broadcasted_iota(jnp.int32, (16, WIDTH), 0) >= 16 - SUMM
    for at in range(0, 32, 2):
        if at * 16 % size == 0:
            copies[at * 16 // size].wait()
        rows = [
            jnp.concatenate(
                [
                    recv_ref[4 * n + home, :, head * HD : (head + 1) * HD]
                    for home in range(4)
                    for head in range(HEADS)
                ],
                0,
            )
            for n in (at, at + 1)
        ]
        strided = dot(strided_pick, jnp.concatenate(rows, 1))
        for n in range(2):
            tile = 16 * (at + n)
            fixed = [fixed_ref[array, tile : tile + 16] for array in range(4)]
            if tile == BLOCK - 16:
                for array in (2, 3):
                    fixed[array] = jnp.where(end, tail_ref[array - 2], fixed[array])
            rows = [
                jnp.concatenate([part[:, head * HD : (head + 1) * HD] for part in fixed], 1)
                for head in range(HEADS)
            ]
            own = dot(own_pick, jnp.concatenate(rows, 0))
            for array in range(4):
                out_ref[array, 8 * tile : 8 * tile + 128] = (
                    strided[array * 128 : (array + 1) * 128, n * HD : (n + 1) * HD]
                    + own[:, array * HD : (array + 1) * HD]
                ).astype(BF16)
        if (at + 2) * 16 % size == 0:
            part = at * 16 // size
            where = pl.ds(part * size * 8, size * 8)
            sent += copy_all(
                [(out_ref.at[array, where], outs[array].at[where]) for array in range(4)],
                out_sem.at[part],
            )
    for copy in sent:
        copy.wait()


def unpack(recv, fixed, tail):
    rows = call(
        unpack_kernel,
        1,
        [spec((NB, 16, WIDTH), 0, 0, 0), IN_HBM, spec((2, 16, WIDTH), 0, 0, 0)],
        [IN_HBM] * 4,
        [jax.ShapeDtypeStruct((BLOCK * 8, HD), BF16)] * 4,
        2 * 10**9,
        8 * 2**20,
        [
            pltpu.VMEM((4, BLOCK, WIDTH), BF16),
            pltpu.VMEM((4, BLOCK * 8, HD), BF16),
            pltpu.SemaphoreType.DMA((4,)),
            pltpu.SemaphoreType.DMA((4, 4)),
        ],
        vmem=VMEM6,
    )(recv, in_hbm(fixed), tail)
    return tuple(unflat(array) for array in rows)


def place(index):
    coords = []
    for size in PARTS[::-1]:
        coords.append(index % size)
        index = index // size
    return coords[::-1]


def joined(coords):
    index = 0
    for size, at in zip(PARTS, coords):
        index = index * size + at
    return index


def shift(array, part, step):
    perm = []
    for source in range(NB):
        coords = place(source)
        coords[part] = (coords[part] + step) % PARTS[part]
        perm.append((source, joined(coords)))
    return lax.ppermute(array, "seq", perm)


def other_head(array):
    return lax.ppermute(array, "head", [(0, 1), (1, 0)])


Z, X, Y, CORE = range(4)
Y_BACK = (0, 1, -1, 2)
SLAB = 2 * WIDTH


def gather_along_z(own, me):
    size = PARTS[Z]
    step = NB // size
    groups = [[at + step * z for z in range(size)] for at in range(step)]
    sent = jnp.broadcast_to(own[None], (size,) + own.shape)
    held = lax.all_to_all(sent, "seq", 0, 0, axis_index_groups=groups, tiled=True)
    held = jnp.concatenate([held, held], 0)
    first = (me // step + 4 * (me % 2)) % size
    return lax.dynamic_slice_in_dim(held, first, size, 0).reshape(size * SUMM, SLAB)


def gather_summaries(held):
    held = jnp.concatenate([held, shift(held, X, 1)], 0)
    held = jnp.concatenate([held] + [shift(held, Y, back) for back in Y_BACK[1:]], 0)
    return jnp.concatenate([held, shift(held, CORE, 1)], 0)


def add_up(own, moved):
    return sum((part.astype(F32) for part in moved), own)


def scatter_along_core(kept, sent):
    return add_up(kept, [shift(sent, CORE, 1)])


def scatter_along_y(parts):
    parts = parts.reshape(4, -1, SLAB)
    sent = parts.astype(BF16)
    return add_up(parts[0], [shift(sent[n], Y, -Y_BACK[n]) for n in range(1, 4)])


def scatter_summaries(parts):
    parts = parts.reshape(2, -1, SLAB)
    parts = add_up(parts[0], [shift(parts[1].astype(BF16), X, -1)])
    sent = parts.astype(BF16).reshape(2, 4, SUMM, SLAB)
    moved = []
    for n in range(4):
        perm = []
        for source in range(NB):
            coords = place(source)
            coords[Z] = (coords[Z] + 4 * coords[CORE] + n) % PARTS[Z]
            perm.append((source, joined(coords)))
        moved.append(lax.ppermute(sent[:, n].reshape(2 * SUMM, SLAB), "seq", perm))
    parts = add_up(0.0, moved)
    return add_up(parts[:SUMM], [shift(parts[SUMM:].astype(BF16), CORE, 1)])


def slot_blocks(me):
    slots = jnp.arange(NB, dtype=jnp.int32)
    z, x, y, core = place(me)
    core_of = (core - (slots >> 6)) % 2
    y_of = (y - jnp.array(Y_BACK, jnp.int32)[(slots >> 4) & 3]) % PARTS[Y]
    x_of = (x - ((slots >> 3) & 1)) % PARTS[X]
    z_of = (z + 4 * core_of + (slots & 7)) % PARTS[Z]
    return joined((z_of, x_of, y_of, core_of))


def shards(queries, key_rows, value_rows, cotangent):
    me = lax.axis_index("seq")
    arrays = tuple(flat(array) for array in (queries, key_rows, value_rows, cotangent))
    send = pack_strided(arrays)
    tails = [a[BLOCK - SUMM :, 1].reshape(SUMM, HEADS, 1, HD) for a in (key_rows, value_rows)]
    own_summ = jnp.concatenate(tails, 2).reshape(SUMM, 2 * WIDTH)
    summ = gather_along_z(own_summ, me)
    send, summ = lax.optimization_barrier((send, summ))
    recv = lax.all_to_all(send, "seq", 0, 0, tiled=True)
    summ = gather_summaries(summ)
    seen = jnp.repeat((slot_blocks(me) < me).astype(jnp.int32), SUMM)[None]
    rows = pack_fixed(arrays)
    fixed_attn, own_prob, far_prob, fixed_sums = fixed_forward(rows, summ, seen)
    fixed_send = fixed_sums[:, :2].reshape(NB, OFFS, 2).transpose(0, 2, 1).reshape(NB, 8)
    fixed_both = fixed_send + other_head(fixed_send)
    keys, prob, grp, sums, sums_send = strided_forward(recv, jnp.pad(fixed_both, ((0, 0), (0, HD - 8))))
    sums_in = lax.all_to_all(sums_send, "seq", 0, 0, tiled=True)
    sums_other = other_head(sums[:, 8:16])
    own_sums = sums_in[:, 0, 8:16]
    block_sums = fixed_both + own_sums + other_head(own_sums)
    send_back = strided_backward(keys, prob, grp, sums, sums_other, sums_in)
    send_back, block_sums = lax.optimization_barrier((send_back, block_sums))
    recv_back = lax.all_to_all(send_back, "seq", 0, 0, tiled=True)
    block_sums = block_sums.reshape(NB, 2, OFFS).transpose(0, 2, 1).reshape(BLOCK, 2)
    far_query, kept, sent = summary_backward(rows, summ, far_prob, fixed_attn, block_sums)
    fixed_out, tails = fixed_backward(rows, own_prob, fixed_attn, block_sums, far_query)
    parts = scatter_along_y(scatter_along_core(kept, sent))
    parts, fixed_out, tails = lax.optimization_barrier((parts, fixed_out, tails))
    totals = scatter_summaries(parts).reshape(SUMM, HEADS, 2, HD)
    totals = totals.transpose(2, 0, 1, 3).reshape(2, SUMM, WIDTH)
    totals = (tails[:, 8 - SUMM :] + totals).astype(BF16)
    tail = jnp.pad(totals, ((0, 0), (16 - SUMM, 0), (0, 0)))
    return unpack(recv_back, fixed_out, tail)


def solution(mesh):
    specs = (P("seq", None, "head"),) * 4
    return jax.shard_map(shards, mesh=mesh, in_specs=specs, out_specs=specs, check_vma=False)
```

```python
import jax
import jax.numpy as jnp
from jax import lax
from jax.experimental import pallas as pl
from jax.experimental.pallas import tpu as pltpu
from jax.sharding import PartitionSpec as P

BLOCK = 512
SUMM = 4
HD = 128
COLS = 1024
NB = 128
HEADS = 4
OFFS = 4
WIDTH = HEADS * HD
PARTS = (8, 2, 4, 2)
VMEM3, VMEM4, VMEM5, VMEM6 = 32, 32, 48, 32

epsilon = 1e-06
scale = HD ** (-0.5)
F32 = jnp.float32
BF16 = jnp.bfloat16


def iotas(shape):
    return (
        lax.broadcasted_iota(jnp.int32, shape, 0),
        lax.broadcasted_iota(jnp.int32, shape, 1),
    )


def one_hot(hit):
    return jnp.where(hit, 1.0, 0.0).astype(BF16)


def dot(a, b):
    return jnp.dot(a, b, preferred_element_type=F32)


def dot_nt(a, b):
    return lax.dot_general(a, b, (((1,), (1,)), ((), ())), preferred_element_type=F32)


def dot_tn(a, b):
    return lax.dot_general(a, b, (((0,), (0,)), ((), ())), preferred_element_type=F32)


def dot_rows(a, b):
    return dot_tn(b, a).T


def batch_dot(a, b, left, right):
    return lax.dot_general(
        a, b, (((left,), (right,)), ((0,), (0,))), preferred_element_type=F32
    )


def flat(array):
    split = array.reshape(BLOCK, 2, HEADS, HD).transpose(0, 2, 1, 3)
    return split.reshape(BLOCK * HEADS * 2, HD)


def unflat(rows):
    return rows.reshape(BLOCK, HEADS, 2, HD).transpose(0, 2, 1, 3).reshape(BLOCK, 2, WIDTH)


def call(kernel, grid, in_specs, out_specs, out_shape, flops, nbytes, scratch=(), vmem=60):
    return pl.pallas_call(
        kernel,
        grid=(grid,),
        in_specs=in_specs,
        out_specs=out_specs,
        out_shape=out_shape,
        scratch_shapes=list(scratch),
        compiler_params=pltpu.CompilerParams(vmem_limit_bytes=vmem * 2**20),
        cost_estimate=pl.CostEstimate(flops=flops, bytes_accessed=nbytes, transcendentals=0),
    )


IN_HBM = pl.BlockSpec(memory_space=pltpu.HBM)


def in_hbm(array):
    return pltpu.with_memory_space_constraint(array, pltpu.HBM)


def copy_all(pairs, sems):
    copies = [
        pltpu.make_async_copy(source, target, sems.at[n]) for n, (source, target) in enumerate(pairs)
    ]
    for copy in copies:
        copy.start()
    return copies


def spec(block, *index):
    return pl.BlockSpec(block, lambda i: tuple(i if at == "i" else at for at in index))


def pack_strided_kernel(q_ref, k_ref, v_ref, c_ref, send_ref, rows_ref, out_ref, in_sem, out_sem):
    parts = 4
    size = BLOCK * 8 // parts
    copies = copy_all(
        [
            (ref.at[pl.ds(part * size, size)], rows_ref.at[array, pl.ds(part * size, size)])
            for part in range(parts)
            for array, ref in enumerate((q_ref, k_ref, v_ref, c_ref))
        ],
        in_sem,
    )
    row, col = iotas((128, 256))
    home, head, array, offset = row >> 6, (row >> 4) & 3, (row >> 2) & 3, row & 3
    pick = one_hot(col == array * 64 + ((home * OFFS + offset) * HEADS + head) * 2)
    sent = []
    for part in range(parts):
        for copy in copies[4 * part : 4 * part + 4]:
            copy.wait()
        for at in range(part * 64 // parts, (part + 1) * 64 // parts, 2):
            pair = [
                jnp.concatenate(
                    [rows_ref[array, 64 * n : 64 * (n + 1)] for n in (at, at + 1)], 1
                )
                for array in range(4)
            ]
            picked = dot(pick, jnp.concatenate(pair, 0)).astype(BF16)
            for n in range(2):
                for home in range(2):
                    for head in range(HEADS):
                        row = home * 64 + head * 16
                        out_ref[2 * (at + n) + home, :, head * HD : (head + 1) * HD] = picked[
                            row : row + 16, n * HD : (n + 1) * HD
                        ]
        where = pl.ds(part * NB // parts, NB // parts)
        copy = pltpu.make_async_copy(out_ref.at[where], send_ref.at[where], out_sem.at[part])
        copy.start()
        sent.append(copy)
    for copy in sent:
        copy.wait()


def pack_strided(arrays):
    return call(
        pack_strided_kernel,
        1,
        [IN_HBM] * 4,
        IN_HBM,
        jax.ShapeDtypeStruct((NB, 16, WIDTH), BF16),
        10**9,
        6 * 2**20,
        [
            pltpu.VMEM((4, BLOCK * 8, HD), BF16),
            pltpu.VMEM((NB, 16, WIDTH), BF16),
            pltpu.SemaphoreType.DMA((16,)),
            pltpu.SemaphoreType.DMA((4,)),
        ],
    )(*arrays)


def pack_fixed_kernel(q_ref, k_ref, v_ref, c_ref, out_ref):
    row, col = iotas((64, 128))
    pick = one_hot(col == ((row & 15) * HEADS + (row >> 4)) * 2 + 1)
    for at in range(16):
        rows = [ref[128 * at : 128 * (at + 1)] for ref in (q_ref, k_ref, v_ref, c_ref)]
        picked = dot(pick, jnp.concatenate(rows, 1)).astype(BF16)
        for array in range(4):
            for head in range(HEADS):
                out_ref[array, 16 * at : 16 * (at + 1), head * HD : (head + 1) * HD] = picked[
                    16 * head : 16 * (head + 1), array * HD : (array + 1) * HD
                ]


def pack_fixed(arrays):
    return call(
        pack_fixed_kernel,
        2,
        [spec((2048, HD), "i", 0)] * 4,
        spec((4, BLOCK // 2, WIDTH), 0, "i", 0),
        jax.ShapeDtypeStruct((4, BLOCK, WIDTH), BF16),
        10**9,
        6 * 2**20,
    )(*arrays)


def fixed_probabilities(query, key, summ_key, seen):
    row, col = iotas((BLOCK, BLOCK))
    own = jnp.where(col <= row, dot_nt(query, key) * scale, -jnp.inf)
    far = jnp.where(seen > 0, dot_nt(query, summ_key) * scale, -jnp.inf)
    top = jnp.maximum(
        jnp.max(own, axis=-1, keepdims=True), jnp.max(far, axis=-1, keepdims=True)
    )
    own = jnp.exp(own - top)
    far = jnp.exp(far - top)
    total = jnp.sum(own, axis=-1, keepdims=True) + jnp.sum(far, axis=-1, keepdims=True)
    inverse = 1.0 / total
    return own * inverse, far * inverse


def fixed_forward_kernel(rows_ref, summ_ref, seen_ref, attn_ref, own_ref, far_ref, sums_ref):
    own, far = fixed_probabilities(rows_ref[0], rows_ref[1], summ_ref[:, :HD], seen_ref[...])
    own_ref[0] = own.astype(BF16)
    far_ref[0] = far.astype(BF16)
    attn = (dot(own_ref[0], rows_ref[2]) + dot(far_ref[0], summ_ref[:, HD:])).astype(BF16)
    attn_ref[...] = attn
    wide = attn.astype(F32)
    square = jnp.sum(wide * wide, axis=-1, keepdims=True)
    cross = jnp.sum(wide * rows_ref[3].astype(F32), axis=-1, keepdims=True)
    lane = lax.broadcasted_iota(jnp.int32, (BLOCK, 8), 1)
    part = jnp.where(lane == 0, square, jnp.where(lane == 1, cross, 0.0))

    @pl.when(pl.program_id(0) == 0)
    def _():
        sums_ref[...] = part

    @pl.when(pl.program_id(0) > 0)
    def _():
        sums_ref[...] += part


def fixed_forward(rows, summ, seen):
    return call(
        fixed_forward_kernel,
        HEADS,
        [
            spec((4, BLOCK, HD), 0, 0, "i"),
            spec((BLOCK, 2 * HD), 0, "i"),
            spec((1, BLOCK), 0, 0),
        ],
        [
            spec((BLOCK, HD), 0, "i"),
            spec((1, BLOCK, BLOCK), "i", 0, 0),
            spec((1, BLOCK, BLOCK), "i", 0, 0),
            spec((BLOCK, 8), 0, 0),
        ],
        [
            jax.ShapeDtypeStruct((BLOCK, WIDTH), BF16),
            pltpu.HBM((HEADS, BLOCK, BLOCK), BF16),
            pltpu.HBM((HEADS, BLOCK, BLOCK), BF16),
            jax.ShapeDtypeStruct((BLOCK, 8), F32),
        ],
        4 * 10**9,
        4 * 2**20,
    )(rows, summ, seen)


def swap_matrix():
    row, col = iotas((256, 256))
    return one_hot(col == ((row & 15) << 4) + (row >> 4))


def strided_forward_kernel(
    recv_ref, fixed_ref, keys_out, prob_out, grp_ref, sums_ref, send_ref, keys_ref, prob_ref, sem
):
    swap = swap_matrix()
    for at in range(0, NB, 16):
        rows = dot(swap, recv_ref[at : at + 16].reshape(256, WIDTH)).astype(BF16)
        for head in range(HEADS):
            tiles = rows[:, head * HD : (head + 1) * HD].reshape(4, OFFS, 16, HD)
            keys_ref[head, :, :, at : at + 16, :] = tiles[:3]
            grp_ref[head, 0, :, at : at + 16, :] = tiles[3]
    copies = copy_all([(keys_ref, keys_out)], sem.at[0])
    row, col = iotas((NB, NB))
    heads = range(HEADS)
    scores = [batch_dot(keys_ref[head, 0], keys_ref[head, 1], 2, 2) * scale for head in heads]
    scores = [jnp.where((col <= row)[None], score, -jnp.inf) for score in scores]
    expos = [jnp.exp(score - jnp.max(score, axis=-1, keepdims=True)) for score in scores]
    probs = [
        (expo * (1.0 / jnp.sum(expo, axis=-1, keepdims=True))).astype(BF16) for expo in expos
    ]
    attns = [batch_dot(probs[head], keys_ref[head, 2], 2, 1).astype(BF16) for head in heads]
    square, cross = 0.0, 0.0
    for head in heads:
        prob_ref[head] = probs[head]
        copies += copy_all([(prob_ref.at[head], prob_out.at[head])], sem.at[head + 1])
        wide = attns[head].astype(F32)
        square += wide * wide
        cross += wide * grp_ref[head, 0].astype(F32)
        grp_ref[head, 1] = attns[head]
    square = jnp.sum(square, axis=-1, keepdims=True)
    cross = jnp.sum(cross, axis=-1, keepdims=True)
    lane = lax.broadcasted_iota(jnp.int32, (NB, HD), 1)
    part = fixed_ref[...]
    for at in range(OFFS):
        part += jnp.where(lane == 8 + at, square[at], jnp.where(lane == 12 + at, cross[at], 0.0))
    sums_ref[...] = part
    send_ref[...] = part.reshape(NB, 1, HD)
    for copy in copies:
        copy.wait()


def strided_forward(recv, fixed_sums):
    return call(
        strided_forward_kernel,
        1,
        [spec((NB, 16, WIDTH), 0, 0, 0), spec((NB, HD), 0, 0)],
        [
            IN_HBM,
            IN_HBM,
            spec((HEADS, 2, OFFS, NB, HD), 0, 0, 0, 0, 0),
            spec((NB, HD), 0, 0),
            spec((NB, 1, HD), 0, 0, 0),
        ],
        [
            pltpu.HBM((HEADS, 3, OFFS, NB, HD), BF16),
            pltpu.HBM((HEADS, OFFS, NB, NB), BF16),
            jax.ShapeDtypeStruct((HEADS, 2, OFFS, NB, HD), BF16),
            jax.ShapeDtypeStruct((NB, HD), F32),
            jax.ShapeDtypeStruct((NB, 1, HD), F32),
        ],
        10**9,
        6 * 2**20,
        [
            pltpu.VMEM((HEADS, 3, OFFS, NB, HD), BF16),
            pltpu.VMEM((HEADS, OFFS, NB, NB), BF16),
            pltpu.SemaphoreType.DMA((HEADS + 1, 1)),
        ],
        vmem=VMEM3,
    )(recv, fixed_sums)


def normalize(wide, cotangent, square, cross):
    scaling = lax.rsqrt(square / (2 * COLS) + epsilon)
    normed = (wide * scaling).astype(BF16)
    grad = (
        scaling * cotangent.astype(F32) - wide * (scaling * scaling * scaling * cross / (2 * COLS))
    ).astype(BF16)
    return normed, grad, jnp.sum(grad.astype(F32) * wide, axis=-1, keepdims=True)


def strided_backward_kernel(
    keys_in, prob_in, grp_ref, sums_ref, other_ref, recv_ref, send_out,
    keys_ref, prob_ref, out_ref, send_ref, in_sem, out_sem,
):
    fetched = [
        copy_all(
            [(keys_in.at[head], keys_ref.at[head]), (prob_in.at[head], prob_ref.at[head])],
            in_sem.at[head],
        )
        for head in range(HEADS)
    ]
    moved = recv_ref[...].reshape(NB, HD)
    total = sums_ref[:, 8:16] + other_ref[...] + moved[:, :8]
    square = jnp.stack([total[:, at : at + 1] for at in range(OFFS)])
    cross = jnp.stack([total[:, OFFS + at : OFFS + at + 1] for at in range(OFFS)])
    grads = []
    for head in range(HEADS):
        wide = grp_ref[head, 1].astype(F32)
        normed, grad, row_dot = normalize(wide, grp_ref[head, 0], square, cross)
        out_ref[head, 0] = normed
        grads.append((grad, row_dot))
    heads = range(HEADS)
    for head in heads:
        for copy in fetched[head]:
            copy.wait()
    probs = [prob_ref[head] for head in heads]
    grad_probs = [batch_dot(grads[head][0], keys_ref[head, 2], 2, 2) for head in heads]
    scores = [
        (probs[head].astype(F32) * (grad_probs[head] - grads[head][1]) * scale).astype(BF16)
        for head in heads
    ]
    for head in heads:
        out_ref[head, 3] = batch_dot(probs[head], grads[head][0], 1, 1).astype(BF16)
    for head in heads:
        out_ref[head, 1] = batch_dot(scores[head], keys_ref[head, 1], 2, 1).astype(BF16)
    for head in heads:
        out_ref[head, 2] = batch_dot(scores[head], keys_ref[head, 0], 1, 1).astype(BF16)
    swap = swap_matrix()
    copies = []
    for at in range(0, NB, 16):
        rows = [out_ref[head, :, :, at : at + 16, :].reshape(256, HD) for head in range(HEADS)]
        moved = dot(swap, jnp.concatenate(rows, 1)).astype(BF16)
        send_ref[at : at + 16] = moved.reshape(16, 16, WIDTH)
        where = pl.ds(at, 16)
        copies += copy_all([(send_ref.at[where], send_out.at[where])], out_sem.at[at // 16])
    for copy in copies:
        copy.wait()


def strided_backward(keys, prob, grp, sums, other, recv):
    return call(
        strided_backward_kernel,
        1,
        [
            IN_HBM,
            IN_HBM,
            spec((HEADS, 2, OFFS, NB, HD), 0, 0, 0, 0, 0),
            spec((NB, HD), 0, 0),
            spec((NB, 8), 0, 0),
            spec((NB, 1, HD), 0, 0, 0),
        ],
        IN_HBM,
        pltpu.HBM((NB, 16, WIDTH), BF16),
        10**9,
        6 * 2**20,
        [
            pltpu.VMEM((HEADS, 3, OFFS, NB, HD), BF16),
            pltpu.VMEM((HEADS, OFFS, NB, NB), BF16),
            pltpu.VMEM((HEADS, 4, OFFS, NB, HD), BF16),
            pltpu.VMEM((NB, 16, WIDTH), BF16),
            pltpu.SemaphoreType.DMA((HEADS, 2)),
            pltpu.SemaphoreType.DMA((NB // 16, 1)),
        ],
        vmem=VMEM4,
    )(in_hbm(keys), in_hbm(prob), grp, sums, other, recv)


def summary_backward_kernel(
    rows_in, summ_in, far_in, attn_in, sums_ref, query_ref, keep_ref, send_ref,
    attn_ref, cot_ref, summ_ref, rows_ref, far_ref, sem,
):
    copies = copy_all(
        [
            (attn_in, attn_ref),
            (rows_in.at[3], cot_ref),
            (summ_in, summ_ref),
            (rows_in.at[0], rows_ref),
        ]
        + [(far_in.at[head], far_ref.at[head]) for head in range(HEADS)],
        sem,
    )
    for copy in copies[:4]:
        copy.wait()
    for head in range(HEADS):
        copies[4 + head].wait()
        at = slice(head * HD, (head + 1) * HD)
        to_key = slice(2 * head * HD, (2 * head + 1) * HD)
        to_value = slice((2 * head + 1) * HD, (2 * head + 2) * HD)
        _, grad, row_dot = normalize(
            attn_ref[:, at].astype(F32), cot_ref[:, at], sums_ref[:, 0:1], sums_ref[:, 1:2]
        )
        far = far_ref[head]
        score = far.astype(F32) * (dot_nt(grad, summ_ref[:, to_value]) - row_dot) * scale
        score = score.astype(BF16)
        query_ref[:, at] = dot(score, summ_ref[:, to_key])
        for to, grads in ((to_key, dot_rows(score, rows_ref[:, at])), (to_value, dot_rows(far, grad))):
            grads = grads.reshape(2, 8, 2, 16, HD)
            keep = jnp.stack([grads[0, :, 0], grads[1, :, 1]], 1)
            send = jnp.stack([grads[1, :, 0], grads[0, :, 1]], 1)
            keep_ref[:, to] = keep.reshape(BLOCK // 2, HD)
            send_ref[:, to] = send.reshape(BLOCK // 2, HD).astype(BF16)


def summary_backward(rows, summ, far, attn, sums):
    return call(
        summary_backward_kernel,
        1,
        [IN_HBM] * 4 + [spec((BLOCK, 2), 0, 0)],
        [
            spec((BLOCK, WIDTH), 0, 0),
            spec((BLOCK // 2, 2 * WIDTH), 0, 0),
            spec((BLOCK // 2, 2 * WIDTH), 0, 0),
        ],
        [
            pltpu.HBM((BLOCK, WIDTH), F32),
            jax.ShapeDtypeStruct((BLOCK // 2, 2 * WIDTH), F32),
            jax.ShapeDtypeStruct((BLOCK // 2, 2 * WIDTH), BF16),
        ],
        3 * 10**9,
        8 * 2**20,
        [
            pltpu.VMEM((BLOCK, WIDTH), BF16),
            pltpu.VMEM((BLOCK, WIDTH), BF16),
            pltpu.VMEM((BLOCK, 2 * WIDTH), BF16),
            pltpu.VMEM((BLOCK, WIDTH), BF16),
            pltpu.VMEM((HEADS, BLOCK, BLOCK), BF16),
            pltpu.SemaphoreType.DMA((8,)),
        ],
        vmem=VMEM5,
    )(*[in_hbm(array) for array in (rows, summ, far, attn)], sums)


def fixed_backward_kernel(rows_ref, own_ref, attn_ref, sums_ref, query_ref, out_ref, tail_ref):
    query, key, value = rows_ref[0], rows_ref[1], rows_ref[2]
    own = own_ref[0]
    wide = attn_ref[...].astype(F32)
    normed, grad, row_dot = normalize(wide, rows_ref[3], sums_ref[:, 0:1], sums_ref[:, 1:2])
    out_ref[0] = normed
    score = (own.astype(F32) * (dot_nt(grad, value) - row_dot) * scale).astype(BF16)
    out_ref[1] = (dot(score, key) + query_ref[...]).astype(BF16)
    for at, grads in enumerate((dot_rows(score, query), dot_rows(own, grad))):
        out_ref[2 + at] = grads.astype(BF16)
        tail_ref[at] = grads[BLOCK - 8 :]


def fixed_backward(rows, own, attn, sums, far_query):
    return call(
        fixed_backward_kernel,
        HEADS,
        [
            spec((4, BLOCK, HD), 0, 0, "i"),
            spec((1, BLOCK, BLOCK), "i", 0, 0),
            spec((BLOCK, HD), 0, "i"),
            spec((BLOCK, 2), 0, 0),
            spec((BLOCK, HD), 0, "i"),
        ],
        [spec((4, BLOCK, HD), 0, 0, "i"), spec((2, 8, HD), 0, 0, "i")],
        [
            pltpu.HBM((4, BLOCK, WIDTH), BF16),
            jax.ShapeDtypeStruct((2, 8, WIDTH), F32),
        ],
        5 * 10**9,
        8 * 2**20,
    )(rows, own, attn, sums, far_query)


def unpack_kernel(recv_ref, fixed_in, tail_ref, *refs):
    outs, fixed_ref, out_ref, in_sem, out_sem = refs[:4], refs[4], refs[5], refs[6], refs[7]
    parts = 4
    size = BLOCK // parts
    copies = copy_all(
        [
            (fixed_in.at[:, pl.ds(part * size, size)], fixed_ref.at[:, pl.ds(part * size, size)])
            for part in range(parts)
        ],
        in_sem,
    )
    sent = []
    row, col = iotas((512, 256))
    array, token, head, kind = row >> 7, (row >> 3) & 15, (row >> 1) & 3, row & 1
    source = (token >> 2) * 64 + head * 16 + array * OFFS + (token & 3)
    strided_pick = one_hot((kind == 0) & (col == source))
    row, col = iotas((128, 64))
    token, head, kind = row >> 3, (row >> 1) & 3, row & 1
    own_pick = one_hot((kind == 1) & (col == head * 16 + token))
    end = lax.broadcasted_iota(jnp.int32, (16, WIDTH), 0) >= 16 - SUMM
    for at in range(0, 32, 2):
        if at * 16 % size == 0:
            copies[at * 16 // size].wait()
        rows = [
            jnp.concatenate(
                [
                    recv_ref[4 * n + home, :, head * HD : (head + 1) * HD]
                    for home in range(4)
                    for head in range(HEADS)
                ],
                0,
            )
            for n in (at, at + 1)
        ]
        strided = dot(strided_pick, jnp.concatenate(rows, 1))
        for n in range(2):
            tile = 16 * (at + n)
            fixed = [fixed_ref[array, tile : tile + 16] for array in range(4)]
            if tile == BLOCK - 16:
                for array in (2, 3):
                    fixed[array] = jnp.where(end, tail_ref[array - 2], fixed[array])
            rows = [
                jnp.concatenate([part[:, head * HD : (head + 1) * HD] for part in fixed], 1)
                for head in range(HEADS)
            ]
            own = dot(own_pick, jnp.concatenate(rows, 0))
            for array in range(4):
                out_ref[array, 8 * tile : 8 * tile + 128] = (
                    strided[array * 128 : (array + 1) * 128, n * HD : (n + 1) * HD]
                    + own[:, array * HD : (array + 1) * HD]
                ).astype(BF16)
        if (at + 2) * 16 % size == 0:
            part = at * 16 // size
            where = pl.ds(part * size * 8, size * 8)
            sent += copy_all(
                [(out_ref.at[array, where], outs[array].at[where]) for array in range(4)],
                out_sem.at[part],
            )
    for copy in sent:
        copy.wait()


def unpack(recv, fixed, tail):
    rows = call(
        unpack_kernel,
        1,
        [spec((NB, 16, WIDTH), 0, 0, 0), IN_HBM, spec((2, 16, WIDTH), 0, 0, 0)],
        [IN_HBM] * 4,
        [jax.ShapeDtypeStruct((BLOCK * 8, HD), BF16)] * 4,
        2 * 10**9,
        8 * 2**20,
        [
            pltpu.VMEM((4, BLOCK, WIDTH), BF16),
            pltpu.VMEM((4, BLOCK * 8, HD), BF16),
            pltpu.SemaphoreType.DMA((4,)),
            pltpu.SemaphoreType.DMA((4, 4)),
        ],
        vmem=VMEM6,
    )(recv, in_hbm(fixed), tail)
    return tuple(unflat(array) for array in rows)


def place(index):
    coords = []
    for size in PARTS[::-1]:
        coords.append(index % size)
        index = index // size
    return coords[::-1]


def joined(coords):
    index = 0
    for size, at in zip(PARTS, coords):
        index = index * size + at
    return index


def shift(array, part, step):
    perm = []
    for source in range(NB):
        coords = place(source)
        coords[part] = (coords[part] + step) % PARTS[part]
        perm.append((source, joined(coords)))
    return lax.ppermute(array, "seq", perm)


def other_head(array):
    return lax.ppermute(array, "head", [(0, 1), (1, 0)])


Z, X, Y, CORE = range(4)
Y_BACK = (0, 1, -1, 2)
SLAB = 2 * WIDTH


def gather_along_z(own, me):
    size = PARTS[Z]
    step = NB // size
    groups = [[at + step * z for z in range(size)] for at in range(step)]
    sent = jnp.broadcast_to(own[None], (size,) + own.shape)
    held = lax.all_to_all(sent, "seq", 0, 0, axis_index_groups=groups, tiled=True)
    held = jnp.concatenate([held, held], 0)
    first = (me // step + 4 * (me % 2)) % size
    return lax.dynamic_slice_in_dim(held, first, size, 0).reshape(size * SUMM, SLAB)


def gather_summaries(held):
    held = jnp.concatenate([held, shift(held, X, 1)], 0)
    held = jnp.concatenate([held] + [shift(held, Y, back) for back in Y_BACK[1:]], 0)
    return jnp.concatenate([held, shift(held, CORE, 1)], 0)


def add_up(own, moved):
    return sum((part.astype(F32) for part in moved), own)


def scatter_along_core(kept, sent):
    return add_up(kept, [shift(sent, CORE, 1)])


def scatter_along_y(parts):
    parts = parts.reshape(4, -1, SLAB)
    sent = parts.astype(BF16)
    return add_up(parts[0], [shift(sent[n], Y, -Y_BACK[n]) for n in range(1, 4)])


def scatter_summaries(parts):
    parts = parts.reshape(2, -1, SLAB)
    parts = add_up(parts[0], [shift(parts[1].astype(BF16), X, -1)])
    sent = parts.astype(BF16).reshape(2, 4, SUMM, SLAB)
    moved = []
    for n in range(4):
        perm = []
        for source in range(NB):
            coords = place(source)
            coords[Z] = (coords[Z] + 4 * coords[CORE] + n) % PARTS[Z]
            perm.append((source, joined(coords)))
        moved.append(lax.ppermute(sent[:, n].reshape(2 * SUMM, SLAB), "seq", perm))
    parts = add_up(0.0, moved)
    return add_up(parts[:SUMM], [shift(parts[SUMM:].astype(BF16), CORE, 1)])


def slot_blocks(me):
    slots = jnp.arange(NB, dtype=jnp.int32)
    z, x, y, core = place(me)
    core_of = (core - (slots >> 6)) % 2
    y_of = (y - jnp.array(Y_BACK, jnp.int32)[(slots >> 4) & 3]) % PARTS[Y]
    x_of = (x - ((slots >> 3) & 1)) % PARTS[X]
    z_of = (z + 4 * core_of + (slots & 7)) % PARTS[Z]
    return joined((z_of, x_of, y_of, core_of))


def shards(queries, key_rows, value_rows, cotangent):
    me = lax.axis_index("seq")
    arrays = tuple(flat(array) for array in (queries, key_rows, value_rows, cotangent))
    send = pack_strided(arrays)
    tails = [a[BLOCK - SUMM :, 1].reshape(SUMM, HEADS, 1, HD) for a in (key_rows, value_rows)]
    own_summ = jnp.concatenate(tails, 2).reshape(SUMM, 2 * WIDTH)
    summ = gather_along_z(own_summ, me)
    send, summ = lax.optimization_barrier((send, summ))
    recv = lax.all_to_all(send, "seq", 0, 0, tiled=True)
    summ = gather_summaries(summ)
    seen = jnp.repeat((slot_blocks(me) < me).astype(jnp.int32), SUMM)[None]
    rows = pack_fixed(arrays)
    fixed_attn, own_prob, far_prob, fixed_sums = fixed_forward(rows, summ, seen)
    fixed_send = fixed_sums[:, :2].reshape(NB, OFFS, 2).transpose(0, 2, 1).reshape(NB, 8)
    fixed_both = fixed_send + other_head(fixed_send)
    keys, prob, grp, sums, sums_send = strided_forward(recv, jnp.pad(fixed_both, ((0, 0), (0, HD - 8))))
    sums_in = lax.all_to_all(sums_send, "seq", 0, 0, tiled=True)
    sums_other = other_head(sums[:, 8:16])
    own_sums = sums_in[:, 0, 8:16]
    block_sums = fixed_both + own_sums + other_head(own_sums)
    send_back = strided_backward(keys, prob, grp, sums, sums_other, sums_in)
    recv_back = lax.all_to_all(send_back, "seq", 0, 0, tiled=True)
    block_sums = block_sums.reshape(NB, 2, OFFS).transpose(0, 2, 1).reshape(BLOCK, 2)
    far_query, kept, sent = summary_backward(rows, summ, far_prob, fixed_attn, block_sums)
    fixed_out, tails = fixed_backward(rows, own_prob, fixed_attn, block_sums, far_query)
    parts = scatter_along_y(scatter_along_core(kept, sent))
    parts, fixed_out, tails = lax.optimization_barrier((parts, fixed_out, tails))
    totals = scatter_summaries(parts).reshape(SUMM, HEADS, 2, HD)
    totals = totals.transpose(2, 0, 1, 3).reshape(2, SUMM, WIDTH)
    totals = (tails[:, 8 - SUMM :] + totals).astype(BF16)
    tail = jnp.pad(totals, ((0, 0), (16 - SUMM, 0), (0, 0)))
    return unpack(recv_back, fixed_out, tail)


def solution(mesh):
    specs = (P("seq", None, "head"),) * 4
    return jax.shard_map(shards, mesh=mesh, in_specs=specs, out_specs=specs, check_vma=False)
```

```python
import jax
import jax.numpy as jnp
from jax import lax
from jax.experimental import pallas as pl
from jax.experimental.pallas import tpu as pltpu
from jax.sharding import PartitionSpec as P

BLOCK = 512
SUMM = 4
HD = 128
COLS = 1024
NB = 128
HEADS = 4
OFFS = 4
WIDTH = HEADS * HD
PARTS = (8, 2, 4, 2)
VMEM3, VMEM4, VMEM5, VMEM6 = 32, 32, 48, 32

epsilon = 1e-06
scale = HD ** (-0.5)
F32 = jnp.float32
BF16 = jnp.bfloat16


def iotas(shape):
    return (
        lax.broadcasted_iota(jnp.int32, shape, 0),
        lax.broadcasted_iota(jnp.int32, shape, 1),
    )


def one_hot(hit):
    return jnp.where(hit, 1.0, 0.0).astype(BF16)


def dot(a, b):
    return jnp.dot(a, b, preferred_element_type=F32)


def dot_nt(a, b):
    return lax.dot_general(a, b, (((1,), (1,)), ((), ())), preferred_element_type=F32)


def dot_tn(a, b):
    return lax.dot_general(a, b, (((0,), (0,)), ((), ())), preferred_element_type=F32)


def batch_dot(a, b, left, right):
    return lax.dot_general(
        a, b, (((left,), (right,)), ((0,), (0,))), preferred_element_type=F32
    )


def flat(array):
    split = array.reshape(BLOCK, 2, HEADS, HD).transpose(0, 2, 1, 3)
    return split.reshape(BLOCK * HEADS * 2, HD)


def unflat(rows):
    return rows.reshape(BLOCK, HEADS, 2, HD).transpose(0, 2, 1, 3).reshape(BLOCK, 2, WIDTH)


def call(kernel, grid, in_specs, out_specs, out_shape, flops, nbytes, scratch=(), vmem=60):
    return pl.pallas_call(
        kernel,
        grid=(grid,),
        in_specs=in_specs,
        out_specs=out_specs,
        out_shape=out_shape,
        scratch_shapes=list(scratch),
        compiler_params=pltpu.CompilerParams(vmem_limit_bytes=vmem * 2**20),
        cost_estimate=pl.CostEstimate(flops=flops, bytes_accessed=nbytes, transcendentals=0),
    )


IN_HBM = pl.BlockSpec(memory_space=pltpu.HBM)


def in_hbm(array):
    return pltpu.with_memory_space_constraint(array, pltpu.HBM)


def copy_all(pairs, sems):
    copies = [
        pltpu.make_async_copy(source, target, sems.at[n]) for n, (source, target) in enumerate(pairs)
    ]
    for copy in copies:
        copy.start()
    return copies


def spec(block, *index):
    return pl.BlockSpec(block, lambda i: tuple(i if at == "i" else at for at in index))


def pack_strided_kernel(q_ref, k_ref, v_ref, c_ref, send_ref, rows_ref, out_ref, in_sem, out_sem):
    parts = 4
    size = BLOCK * 8 // parts
    copies = copy_all(
        [
            (ref.at[pl.ds(part * size, size)], rows_ref.at[array, pl.ds(part * size, size)])
            for part in range(parts)
            for array, ref in enumerate((q_ref, k_ref, v_ref, c_ref))
        ],
        in_sem,
    )
    row, col = iotas((128, 256))
    home, head, array, offset = row >> 6, (row >> 4) & 3, (row >> 2) & 3, row & 3
    pick = one_hot(col == array * 64 + ((home * OFFS + offset) * HEADS + head) * 2)
    sent = []
    for part in range(parts):
        for copy in copies[4 * part : 4 * part + 4]:
            copy.wait()
        for at in range(part * 64 // parts, (part + 1) * 64 // parts, 2):
            pair = [
                jnp.concatenate(
                    [rows_ref[array, 64 * n : 64 * (n + 1)] for n in (at, at + 1)], 1
                )
                for array in range(4)
            ]
            picked = dot(pick, jnp.concatenate(pair, 0)).astype(BF16)
            for n in range(2):
                for home in range(2):
                    for head in range(HEADS):
                        row = home * 64 + head * 16
                        out_ref[2 * (at + n) + home, :, head * HD : (head + 1) * HD] = picked[
                            row : row + 16, n * HD : (n + 1) * HD
                        ]
        where = pl.ds(part * NB // parts, NB // parts)
        copy = pltpu.make_async_copy(out_ref.at[where], send_ref.at[where], out_sem.at[part])
        copy.start()
        sent.append(copy)
    for copy in sent:
        copy.wait()


def pack_strided(arrays):
    return call(
        pack_strided_kernel,
        1,
        [IN_HBM] * 4,
        IN_HBM,
        jax.ShapeDtypeStruct((NB, 16, WIDTH), BF16),
        10**9,
        6 * 2**20,
        [
            pltpu.VMEM((4, BLOCK * 8, HD), BF16),
            pltpu.VMEM((NB, 16, WIDTH), BF16),
            pltpu.SemaphoreType.DMA((16,)),
            pltpu.SemaphoreType.DMA((4,)),
        ],
    )(*arrays)


def pack_fixed_kernel(q_ref, k_ref, v_ref, c_ref, out_ref):
    row, col = iotas((64, 128))
    pick = one_hot(col == ((row & 15) * HEADS + (row >> 4)) * 2 + 1)
    for at in range(16):
        rows = [ref[128 * at : 128 * (at + 1)] for ref in (q_ref, k_ref, v_ref, c_ref)]
        picked = dot(pick, jnp.concatenate(rows, 1)).astype(BF16)
        for array in range(4):
            for head in range(HEADS):
                out_ref[array, 16 * at : 16 * (at + 1), head * HD : (head + 1) * HD] = picked[
                    16 * head : 16 * (head + 1), array * HD : (array + 1) * HD
                ]


def pack_fixed(arrays):
    return call(
        pack_fixed_kernel,
        2,
        [spec((2048, HD), "i", 0)] * 4,
        spec((4, BLOCK // 2, WIDTH), 0, "i", 0),
        jax.ShapeDtypeStruct((4, BLOCK, WIDTH), BF16),
        10**9,
        6 * 2**20,
    )(*arrays)


def fixed_probabilities(query, key, summ_key, seen):
    row, col = iotas((BLOCK, BLOCK))
    own = jnp.where(col <= row, dot_nt(query, key) * scale, -jnp.inf)
    far = jnp.where(seen > 0, dot_nt(query, summ_key) * scale, -jnp.inf)
    top = jnp.maximum(
        jnp.max(own, axis=-1, keepdims=True), jnp.max(far, axis=-1, keepdims=True)
    )
    own = jnp.exp(own - top)
    far = jnp.exp(far - top)
    total = jnp.sum(own, axis=-1, keepdims=True) + jnp.sum(far, axis=-1, keepdims=True)
    inverse = 1.0 / total
    return own * inverse, far * inverse


def fixed_forward_kernel(rows_ref, summ_ref, seen_ref, attn_ref, own_ref, far_ref, sums_ref):
    own, far = fixed_probabilities(rows_ref[0], rows_ref[1], summ_ref[:, :HD], seen_ref[...])
    own_ref[0] = own.astype(BF16)
    far_ref[0] = far.astype(BF16)
    attn = (dot(own_ref[0], rows_ref[2]) + dot(far_ref[0], summ_ref[:, HD:])).astype(BF16)
    attn_ref[...] = attn
    wide = attn.astype(F32)
    square = jnp.sum(wide * wide, axis=-1, keepdims=True)
    cross = jnp.sum(wide * rows_ref[3].astype(F32), axis=-1, keepdims=True)
    lane = lax.broadcasted_iota(jnp.int32, (BLOCK, 8), 1)
    part = jnp.where(lane == 0, square, jnp.where(lane == 1, cross, 0.0))

    @pl.when(pl.program_id(0) == 0)
    def _():
        sums_ref[...] = part

    @pl.when(pl.program_id(0) > 0)
    def _():
        sums_ref[...] += part


def fixed_forward(rows, summ, seen):
    return call(
        fixed_forward_kernel,
        HEADS,
        [
            spec((4, BLOCK, HD), 0, 0, "i"),
            spec((BLOCK, 2 * HD), 0, "i"),
            spec((1, BLOCK), 0, 0),
        ],
        [
            spec((BLOCK, HD), 0, "i"),
            spec((1, BLOCK, BLOCK), "i", 0, 0),
            spec((1, BLOCK, BLOCK), "i", 0, 0),
            spec((BLOCK, 8), 0, 0),
        ],
        [
            jax.ShapeDtypeStruct((BLOCK, WIDTH), BF16),
            pltpu.HBM((HEADS, BLOCK, BLOCK), BF16),
            pltpu.HBM((HEADS, BLOCK, BLOCK), BF16),
            jax.ShapeDtypeStruct((BLOCK, 8), F32),
        ],
        4 * 10**9,
        4 * 2**20,
    )(rows, summ, seen)


def swap_matrix():
    row, col = iotas((256, 256))
    return one_hot(col == ((row & 15) << 4) + (row >> 4))


def strided_forward_kernel(
    recv_ref, fixed_ref, keys_out, prob_out, grp_ref, sums_ref, send_ref, keys_ref, prob_ref, sem
):
    swap = swap_matrix()
    for at in range(0, NB, 16):
        rows = dot(swap, recv_ref[at : at + 16].reshape(256, WIDTH)).astype(BF16)
        for head in range(HEADS):
            tiles = rows[:, head * HD : (head + 1) * HD].reshape(4, OFFS, 16, HD)
            keys_ref[head, :, :, at : at + 16, :] = tiles[:3]
            grp_ref[head, 0, :, at : at + 16, :] = tiles[3]
    copies = copy_all([(keys_ref, keys_out)], sem.at[0])
    row, col = iotas((NB, NB))
    heads = range(HEADS)
    scores = [batch_dot(keys_ref[head, 0], keys_ref[head, 1], 2, 2) * scale for head in heads]
    scores = [jnp.where((col <= row)[None], score, -jnp.inf) for score in scores]
    expos = [jnp.exp(score - jnp.max(score, axis=-1, keepdims=True)) for score in scores]
    probs = [
        (expo * (1.0 / jnp.sum(expo, axis=-1, keepdims=True))).astype(BF16) for expo in expos
    ]
    attns = [batch_dot(probs[head], keys_ref[head, 2], 2, 1).astype(BF16) for head in heads]
    square, cross = 0.0, 0.0
    for head in heads:
        prob_ref[head] = probs[head]
        copies += copy_all([(prob_ref.at[head], prob_out.at[head])], sem.at[head + 1])
        wide = attns[head].astype(F32)
        square += wide * wide
        cross += wide * grp_ref[head, 0].astype(F32)
        grp_ref[head, 1] = attns[head]
    square = jnp.sum(square, axis=-1, keepdims=True)
    cross = jnp.sum(cross, axis=-1, keepdims=True)
    lane = lax.broadcasted_iota(jnp.int32, (NB, HD), 1)
    part = fixed_ref[...]
    for at in range(OFFS):
        part += jnp.where(lane == 8 + at, square[at], jnp.where(lane == 12 + at, cross[at], 0.0))
    sums_ref[...] = part
    send_ref[...] = part.reshape(NB, 1, HD)
    for copy in copies:
        copy.wait()


def strided_forward(recv, fixed_sums):
    return call(
        strided_forward_kernel,
        1,
        [spec((NB, 16, WIDTH), 0, 0, 0), spec((NB, HD), 0, 0)],
        [
            IN_HBM,
            IN_HBM,
            spec((HEADS, 2, OFFS, NB, HD), 0, 0, 0, 0, 0),
            spec((NB, HD), 0, 0),
            spec((NB, 1, HD), 0, 0, 0),
        ],
        [
            pltpu.HBM((HEADS, 3, OFFS, NB, HD), BF16),
            pltpu.HBM((HEADS, OFFS, NB, NB), BF16),
            jax.ShapeDtypeStruct((HEADS, 2, OFFS, NB, HD), BF16),
            jax.ShapeDtypeStruct((NB, HD), F32),
            jax.ShapeDtypeStruct((NB, 1, HD), F32),
        ],
        10**9,
        6 * 2**20,
        [
            pltpu.VMEM((HEADS, 3, OFFS, NB, HD), BF16),
            pltpu.VMEM((HEADS, OFFS, NB, NB), BF16),
            pltpu.SemaphoreType.DMA((HEADS + 1, 1)),
        ],
        vmem=VMEM3,
    )(recv, fixed_sums)


def normalize(wide, cotangent, square, cross):
    scaling = lax.rsqrt(square / (2 * COLS) + epsilon)
    normed = (wide * scaling).astype(BF16)
    grad = (
        scaling * cotangent.astype(F32) - wide * (scaling * scaling * scaling * cross / (2 * COLS))
    ).astype(BF16)
    return normed, grad, jnp.sum(grad.astype(F32) * wide, axis=-1, keepdims=True)


def factors(sums_ref):
    row, col = iotas((BLOCK, NB))
    spread = one_hot(col == row >> 2)
    rest, columns = sums_ref[...], 0.0
    for _ in range(3):
        part = rest.astype(BF16)
        rest = rest - part.astype(F32)
        columns += dot_nt(spread, part)
    row, col = iotas((BLOCK, 8))
    square, cross = (
        jnp.sum(jnp.where(col == (row & 3) + at, columns, 0.0), axis=-1, keepdims=True)
        for at in (0, OFFS)
    )
    scaling = lax.rsqrt(square / (2 * COLS) + epsilon)
    other = scaling * scaling * scaling * cross / (2 * COLS)
    return jnp.broadcast_to(scaling, (BLOCK, HD)), jnp.broadcast_to(other, (BLOCK, HD))


def gradient(wide, cotangent, scaling, other):
    grad = (scaling * cotangent.astype(F32) - wide * other).astype(BF16)
    return grad, jnp.sum(grad.astype(F32) * wide, axis=-1, keepdims=True)


def strided_backward_kernel(
    keys_in, prob_in, grp_ref, sums_ref, other_ref, recv_ref, send_out,
    keys_ref, prob_ref, out_ref, send_ref, in_sem, out_sem,
):
    fetched = [
        copy_all(
            [(keys_in.at[head], keys_ref.at[head]), (prob_in.at[head], prob_ref.at[head])],
            in_sem.at[head],
        )
        for head in range(HEADS)
    ]
    moved = recv_ref[...].reshape(NB, HD)
    total = sums_ref[:, 8:16] + other_ref[...] + moved[:, :8]
    square = jnp.stack([total[:, at : at + 1] for at in range(OFFS)])
    cross = jnp.stack([total[:, OFFS + at : OFFS + at + 1] for at in range(OFFS)])
    grads = []
    for head in range(HEADS):
        wide = grp_ref[head, 1].astype(F32)
        normed, grad, row_dot = normalize(wide, grp_ref[head, 0], square, cross)
        out_ref[head, 0] = normed
        grads.append((grad, row_dot))
    heads = range(HEADS)
    for head in heads:
        for copy in fetched[head]:
            copy.wait()
    probs = [prob_ref[head] for head in heads]
    grad_probs = [batch_dot(grads[head][0], keys_ref[head, 2], 2, 2) for head in heads]
    scores = [
        (probs[head].astype(F32) * (grad_probs[head] - grads[head][1]) * scale).astype(BF16)
        for head in heads
    ]
    for head in heads:
        out_ref[head, 3] = batch_dot(probs[head], grads[head][0], 1, 1).astype(BF16)
    for head in heads:
        out_ref[head, 1] = batch_dot(scores[head], keys_ref[head, 1], 2, 1).astype(BF16)
    for head in heads:
        out_ref[head, 2] = batch_dot(scores[head], keys_ref[head, 0], 1, 1).astype(BF16)
    swap = swap_matrix()
    copies = []
    for at in range(0, NB, 16):
        rows = [out_ref[head, :, :, at : at + 16, :].reshape(256, HD) for head in range(HEADS)]
        moved = dot(swap, jnp.concatenate(rows, 1)).astype(BF16)
        send_ref[at : at + 16] = moved.reshape(16, 16, WIDTH)
        where = pl.ds(at, 16)
        copies += copy_all([(send_ref.at[where], send_out.at[where])], out_sem.at[at // 16])
    for copy in copies:
        copy.wait()


def strided_backward(keys, prob, grp, sums, other, recv):
    return call(
        strided_backward_kernel,
        1,
        [
            IN_HBM,
            IN_HBM,
            spec((HEADS, 2, OFFS, NB, HD), 0, 0, 0, 0, 0),
            spec((NB, HD), 0, 0),
            spec((NB, 8), 0, 0),
            spec((NB, 1, HD), 0, 0, 0),
        ],
        IN_HBM,
        pltpu.HBM((NB, 16, WIDTH), BF16),
        10**9,
        6 * 2**20,
        [
            pltpu.VMEM((HEADS, 3, OFFS, NB, HD), BF16),
            pltpu.VMEM((HEADS, OFFS, NB, NB), BF16),
            pltpu.VMEM((HEADS, 4, OFFS, NB, HD), BF16),
            pltpu.VMEM((NB, 16, WIDTH), BF16),
            pltpu.SemaphoreType.DMA((HEADS, 2)),
            pltpu.SemaphoreType.DMA((NB // 16, 1)),
        ],
        vmem=VMEM4,
    )(in_hbm(keys), in_hbm(prob), grp, sums, other, recv)


def summary_backward_kernel(
    rows_in, summ_in, far_in, attn_in, sums_ref, query_ref, keep_ref, send_ref,
    attn_ref, cot_ref, summ_ref, rows_ref, far_ref, sem,
):
    copies = copy_all(
        [
            (attn_in, attn_ref),
            (rows_in.at[3], cot_ref),
            (summ_in, summ_ref),
        ]
        + [(far_in.at[head], far_ref.at[head]) for head in range(HEADS)]
        + [(rows_in.at[0], rows_ref)],
        sem,
    )
    heads = range(HEADS)
    at = [slice(head * HD, (head + 1) * HD) for head in heads]
    to_key = [slice(2 * head * HD, (2 * head + 1) * HD) for head in heads]
    to_value = [slice((2 * head + 1) * HD, (2 * head + 2) * HD) for head in heads]
    scaling, other = factors(sums_ref)
    copies[0].wait()
    copies[1].wait()
    grads = [
        gradient(attn_ref[:, at[head]].astype(F32), cot_ref[:, at[head]], scaling, other)
        for head in heads
    ]
    scores = []
    copies[2].wait()
    for head in heads:
        copies[3 + head].wait()
        grad, row_dot = grads[head]
        grad_prob = dot_nt(grad, summ_ref[:, to_value[head]])
        score = far_ref[head].astype(F32) * (grad_prob - row_dot) * scale
        scores.append(score.astype(BF16))

    def put(to, grads):
        grads = grads.reshape(2, 8, 2, 16, HD)
        keep = jnp.stack([grads[0, :, 0], grads[1, :, 1]], 1)
        send = jnp.stack([grads[1, :, 0], grads[0, :, 1]], 1)
        keep_ref[:, to] = keep.reshape(BLOCK // 2, HD)
        send_ref[:, to] = send.reshape(BLOCK // 2, HD).astype(BF16)

    for head in heads:
        put(to_value[head], dot_tn(far_ref[head], grads[head][0]))
    copies[3 + HEADS].wait()
    for head in heads:
        put(to_key[head], dot_tn(scores[head], rows_ref[:, at[head]]))
    for head in heads:
        query_ref[:, at[head]] = dot(scores[head], summ_ref[:, to_key[head]])


def summary_backward(rows, summ, far, attn, sums):
    return call(
        summary_backward_kernel,
        1,
        [IN_HBM] * 4 + [spec((8, NB), 0, 0)],
        [
            spec((BLOCK, WIDTH), 0, 0),
            spec((BLOCK // 2, 2 * WIDTH), 0, 0),
            spec((BLOCK // 2, 2 * WIDTH), 0, 0),
        ],
        [
            pltpu.HBM((BLOCK, WIDTH), F32),
            jax.ShapeDtypeStruct((BLOCK // 2, 2 * WIDTH), F32),
            jax.ShapeDtypeStruct((BLOCK // 2, 2 * WIDTH), BF16),
        ],
        3 * 10**9,
        8 * 2**20,
        [
            pltpu.VMEM((BLOCK, WIDTH), BF16),
            pltpu.VMEM((BLOCK, WIDTH), BF16),
            pltpu.VMEM((BLOCK, 2 * WIDTH), BF16),
            pltpu.VMEM((BLOCK, WIDTH), BF16),
            pltpu.VMEM((HEADS, BLOCK, BLOCK), BF16),
            pltpu.SemaphoreType.DMA((8,)),
        ],
        vmem=VMEM5,
    )(*[in_hbm(array) for array in (rows, summ, far, attn)], sums)


def fixed_backward_kernel(
    rows_in, own_in, attn_in, sums_ref, query_in, out_out, tail_ref,
    rows_ref, own_ref, attn_ref, query_ref, out_ref, sem, out_sem,
):
    copies = copy_all(
        [(attn_in, attn_ref)]
        + [(rows_in.at[array], rows_ref.at[array]) for array in (3, 2)]
        + [(own_in.at[head], own_ref.at[head]) for head in range(HEADS)]
        + [(rows_in.at[array], rows_ref.at[array]) for array in (0, 1)]
        + [(query_in, query_ref)],
        sem,
    )
    heads = range(HEADS)
    at = [slice(head * HD, (head + 1) * HD) for head in heads]
    low, high = slice(0, BLOCK // 2), slice(BLOCK // 2, BLOCK)
    scaling, other = factors(sums_ref)
    copies[0].wait()
    copies[1].wait()
    grads = []
    for head in heads:
        wide = attn_ref[:, at[head]].astype(F32)
        out_ref[0, :, at[head]] = (wide * scaling).astype(BF16)
        grads.append(gradient(wide, rows_ref[3, :, at[head]], scaling, other))
    sent = copy_all([(out_ref.at[0], out_out.at[0])], out_sem.at[0])
    scores = []
    copies[2].wait()
    for head in heads:
        copies[3 + head].wait()
        grad, row_dot = grads[head]
        first = dot_nt(grad[low], rows_ref[2, low, at[head]]) - row_dot[low]
        second = dot_nt(grad[high], rows_ref[2, :, at[head]]) - row_dot[high]
        first = (own_ref[head, low, low].astype(F32) * first * scale).astype(BF16)
        second = (own_ref[head, high, :].astype(F32) * second * scale).astype(BF16)
        scores.append((first, second))

    def put(array, head, first, second, b):
        grads_low = dot_tn(first, b[low]) + dot_tn(second[:, low], b[high])
        grads_high = dot_tn(second[:, high], b[high])
        out_ref[array, low, at[head]] = grads_low.astype(BF16)
        out_ref[array, high, at[head]] = grads_high.astype(BF16)
        tail_ref[array - 2, :, at[head]] = grads_high[BLOCK // 2 - 8 :]

    for head in heads:
        put(3, head, own_ref[head, low, low], own_ref[head, high, :], grads[head][0])
    sent += copy_all([(out_ref.at[3], out_out.at[3])], out_sem.at[3])
    copies[3 + HEADS].wait()
    for head in heads:
        put(2, head, *scores[head], rows_ref[0, :, at[head]])
    sent += copy_all([(out_ref.at[2], out_out.at[2])], out_sem.at[2])
    copies[4 + HEADS].wait()
    copies[5 + HEADS].wait()
    for head in heads:
        first, second = scores[head]
        out_ref[1, low, at[head]] = (
            dot(first, rows_ref[1, low, at[head]]) + query_ref[low, at[head]]
        ).astype(BF16)
        out_ref[1, high, at[head]] = (
            dot(second, rows_ref[1, :, at[head]]) + query_ref[high, at[head]]
        ).astype(BF16)
    sent += copy_all([(out_ref.at[1], out_out.at[1])], out_sem.at[1])
    for copy in sent:
        copy.wait()


def fixed_backward(rows, own, attn, sums, far_query):
    return call(
        fixed_backward_kernel,
        1,
        [IN_HBM, IN_HBM, IN_HBM, spec((8, NB), 0, 0), IN_HBM],
        [IN_HBM, spec((2, 8, WIDTH), 0, 0, 0)],
        [
            pltpu.HBM((4, BLOCK, WIDTH), BF16),
            jax.ShapeDtypeStruct((2, 8, WIDTH), F32),
        ],
        5 * 10**9,
        8 * 2**20,
        [
            pltpu.VMEM((4, BLOCK, WIDTH), BF16),
            pltpu.VMEM((HEADS, BLOCK, BLOCK), BF16),
            pltpu.VMEM((BLOCK, WIDTH), BF16),
            pltpu.VMEM((BLOCK, WIDTH), F32),
            pltpu.VMEM((4, BLOCK, WIDTH), BF16),
            pltpu.SemaphoreType.DMA((HEADS + 6,)),
            pltpu.SemaphoreType.DMA((4, 1)),
        ],
        vmem=VMEM5,
    )(*[in_hbm(array) for array in (rows, own, attn)], sums, in_hbm(far_query))


def unpack_kernel(recv_ref, fixed_in, tail_ref, *refs):
    outs, fixed_ref, out_ref, in_sem, out_sem = refs[:4], refs[4], refs[5], refs[6], refs[7]
    parts = 4
    size = BLOCK // parts
    copies = copy_all(
        [
            (fixed_in.at[:, pl.ds(part * size, size)], fixed_ref.at[:, pl.ds(part * size, size)])
            for part in range(parts)
        ],
        in_sem,
    )
    sent = []
    row, col = iotas((512, 512))
    array, token, head, kind = row >> 7, (row >> 3) & 15, (row >> 1) & 3, row & 1
    strided = (token >> 2) * 64 + head * 16 + array * OFFS + (token & 3)
    fixed = 256 + array * 64 + head * 16 + token
    pick = one_hot(col == jnp.where(kind == 0, strided, fixed))
    end = lax.broadcasted_iota(jnp.int32, (16, WIDTH), 0) >= 16 - SUMM
    for at in range(0, 32, 2):
        if at * 16 % size == 0:
            copies[at * 16 // size].wait()
        pair = []
        for n in (at, at + 1):
            tile = 16 * n
            fixed = [fixed_ref[array, tile : tile + 16] for array in range(4)]
            if tile == BLOCK - 16:
                for array in (2, 3):
                    fixed[array] = jnp.where(end, tail_ref[array - 2], fixed[array])
            heads = [slice(head * HD, (head + 1) * HD) for head in range(HEADS)]
            rows = [recv_ref[4 * n + home, :, head] for home in range(4) for head in heads]
            rows += [part[:, head] for part in fixed for head in heads]
            pair.append(jnp.concatenate(rows, 0))
        picked = dot(pick, jnp.concatenate(pair, 1)).astype(BF16)
        for n in range(2):
            for array in range(4):
                out_ref[array, 128 * (at + n) : 128 * (at + n + 1)] = picked[
                    array * 128 : (array + 1) * 128, n * HD : (n + 1) * HD
                ]
        if (at + 2) * 16 % size == 0:
            part = at * 16 // size
            where = pl.ds(part * size * 8, size * 8)
            sent += copy_all(
                [(out_ref.at[array, where], outs[array].at[where]) for array in range(4)],
                out_sem.at[part],
            )
    for copy in sent:
        copy.wait()


def unpack(recv, fixed, tail):
    rows = call(
        unpack_kernel,
        1,
        [spec((NB, 16, WIDTH), 0, 0, 0), IN_HBM, spec((2, 16, WIDTH), 0, 0, 0)],
        [IN_HBM] * 4,
        [jax.ShapeDtypeStruct((BLOCK * 8, HD), BF16)] * 4,
        2 * 10**9,
        8 * 2**20,
        [
            pltpu.VMEM((4, BLOCK, WIDTH), BF16),
            pltpu.VMEM((4, BLOCK * 8, HD), BF16),
            pltpu.SemaphoreType.DMA((4,)),
            pltpu.SemaphoreType.DMA((4, 4)),
        ],
        vmem=VMEM6,
    )(recv, in_hbm(fixed), tail)
    return tuple(unflat(array) for array in rows)


def place(index):
    coords = []
    for size in PARTS[::-1]:
        coords.append(index % size)
        index = index // size
    return coords[::-1]


def joined(coords):
    index = 0
    for size, at in zip(PARTS, coords):
        index = index * size + at
    return index


def shift(array, part, step):
    perm = []
    for source in range(NB):
        coords = place(source)
        coords[part] = (coords[part] + step) % PARTS[part]
        perm.append((source, joined(coords)))
    return lax.ppermute(array, "seq", perm)


def other_head(array):
    return lax.ppermute(array, "head", [(0, 1), (1, 0)])


Z, X, Y, CORE = range(4)
Y_BACK = (0, 1, -1, 2)
SLAB = 2 * WIDTH


def gather_along_z(own, me):
    size = PARTS[Z]
    step = NB // size
    groups = [[at + step * z for z in range(size)] for at in range(step)]
    sent = jnp.broadcast_to(own[None], (size,) + own.shape)
    held = lax.all_to_all(sent, "seq", 0, 0, axis_index_groups=groups, tiled=True)
    held = jnp.concatenate([held, held], 0)
    first = (me // step + 4 * (me % 2)) % size
    return lax.dynamic_slice_in_dim(held, first, size, 0).reshape(size * SUMM, SLAB)


def gather_summaries(held):
    held = jnp.concatenate([held, shift(held, X, 1)], 0)
    held = jnp.concatenate([held] + [shift(held, Y, back) for back in Y_BACK[1:]], 0)
    return jnp.concatenate([held, shift(held, CORE, 1)], 0)


def add_up(own, moved):
    return sum((part.astype(F32) for part in moved), own)


def scatter_along_core(kept, sent):
    return add_up(kept, [shift(sent, CORE, 1)])


def scatter_along_y(parts):
    parts = parts.reshape(4, -1, SLAB)
    sent = parts.astype(BF16)
    return add_up(parts[0], [shift(sent[n], Y, -Y_BACK[n]) for n in range(1, 4)])


def scatter_summaries(parts):
    parts = parts.reshape(2, -1, SLAB)
    parts = add_up(parts[0], [shift(parts[1].astype(BF16), X, -1)])
    sent = parts.astype(BF16).reshape(2, 4, SUMM, SLAB)
    moved = []
    for n in range(4):
        perm = []
        for source in range(NB):
            coords = place(source)
            coords[Z] = (coords[Z] + 4 * coords[CORE] + n) % PARTS[Z]
            perm.append((source, joined(coords)))
        moved.append(lax.ppermute(sent[:, n].reshape(2 * SUMM, SLAB), "seq", perm))
    parts = add_up(0.0, moved)
    return add_up(parts[:SUMM], [shift(parts[SUMM:].astype(BF16), CORE, 1)])


def slot_blocks(me):
    slots = jnp.arange(NB, dtype=jnp.int32)
    z, x, y, core = place(me)
    core_of = (core - (slots >> 6)) % 2
    y_of = (y - jnp.array(Y_BACK, jnp.int32)[(slots >> 4) & 3]) % PARTS[Y]
    x_of = (x - ((slots >> 3) & 1)) % PARTS[X]
    z_of = (z + 4 * core_of + (slots & 7)) % PARTS[Z]
    return joined((z_of, x_of, y_of, core_of))


def shards(queries, key_rows, value_rows, cotangent):
    me = lax.axis_index("seq")
    arrays = tuple(flat(array) for array in (queries, key_rows, value_rows, cotangent))
    send = pack_strided(arrays)
    tails = [a[BLOCK - SUMM :, 1].reshape(SUMM, HEADS, 1, HD) for a in (key_rows, value_rows)]
    own_summ = jnp.concatenate(tails, 2).reshape(SUMM, 2 * WIDTH)
    summ = gather_along_z(own_summ, me)
    send, summ = lax.optimization_barrier((send, summ))
    recv = lax.all_to_all(send, "seq", 0, 0, tiled=True)
    summ = gather_summaries(summ)
    seen = jnp.repeat((slot_blocks(me) < me).astype(jnp.int32), SUMM)[None]
    rows = pack_fixed(arrays)
    fixed_attn, own_prob, far_prob, fixed_sums = fixed_forward(rows, summ, seen)
    fixed_send = fixed_sums[:, :2].reshape(NB, OFFS, 2).transpose(0, 2, 1).reshape(NB, 8)
    fixed_both = fixed_send + other_head(fixed_send)
    keys, prob, grp, sums, sums_send = strided_forward(recv, jnp.pad(fixed_both, ((0, 0), (0, HD - 8))))
    sums_in = lax.all_to_all(sums_send, "seq", 0, 0, tiled=True)
    sums_other = other_head(sums[:, 8:16])
    own_sums = sums_in[:, 0, 8:16].T
    block_sums = fixed_both.T + own_sums + other_head(own_sums)
    send_back = strided_backward(keys, prob, grp, sums, sums_other, sums_in)
    recv_back = lax.all_to_all(send_back, "seq", 0, 0, tiled=True)
    far_query, kept, sent = summary_backward(rows, summ, far_prob, fixed_attn, block_sums)
    fixed_out, tails = fixed_backward(rows, own_prob, fixed_attn, block_sums, far_query)
    parts = scatter_along_y(scatter_along_core(kept, sent))
    parts, fixed_out, tails = lax.optimization_barrier((parts, fixed_out, tails))
    totals = scatter_summaries(parts).reshape(SUMM, HEADS, 2, HD)
    totals = totals.transpose(2, 0, 1, 3).reshape(2, SUMM, WIDTH)
    totals = (tails[:, 8 - SUMM :] + totals).astype(BF16)
    tail = jnp.pad(totals, ((0, 0), (16 - SUMM, 0), (0, 0)))
    return unpack(recv_back, fixed_out, tail)


def solution(mesh):
    specs = (P("seq", None, "head"),) * 4
    return jax.shard_map(shards, mesh=mesh, in_specs=specs, out_specs=specs, check_vma=False)
```

```python
import jax
import jax.numpy as jnp
from jax import lax
from jax.experimental import pallas as pl
from jax.experimental.pallas import tpu as pltpu
from jax.sharding import PartitionSpec as P

BLOCK = 512
SUMM = 4
HD = 128
COLS = 1024
NB = 128
HEADS = 4
OFFS = 4
WIDTH = HEADS * HD
PARTS = (8, 2, 4, 2)
VMEM3, VMEM4, VMEM5, VMEM6 = 32, 32, 48, 32

epsilon = 1e-06
scale = HD ** (-0.5)
F32 = jnp.float32
BF16 = jnp.bfloat16


def iotas(shape):
    return (
        lax.broadcasted_iota(jnp.int32, shape, 0),
        lax.broadcasted_iota(jnp.int32, shape, 1),
    )


def one_hot(hit):
    return jnp.where(hit, 1.0, 0.0).astype(BF16)


def dot(a, b):
    return jnp.dot(a, b, preferred_element_type=F32)


def dot_nt(a, b):
    return lax.dot_general(a, b, (((1,), (1,)), ((), ())), preferred_element_type=F32)


def dot_tn(a, b):
    return lax.dot_general(a, b, (((0,), (0,)), ((), ())), preferred_element_type=F32)


def batch_dot(a, b, left, right):
    return lax.dot_general(
        a, b, (((left,), (right,)), ((0,), (0,))), preferred_element_type=F32
    )


def flat(array):
    split = array.reshape(BLOCK, 2, HEADS, HD).transpose(0, 2, 1, 3)
    return split.reshape(BLOCK * HEADS * 2, HD)


def unflat(rows):
    return rows.reshape(BLOCK, HEADS, 2, HD).transpose(0, 2, 1, 3).reshape(BLOCK, 2, WIDTH)


def call(kernel, grid, in_specs, out_specs, out_shape, flops, nbytes, scratch=(), vmem=60):
    return pl.pallas_call(
        kernel,
        grid=(grid,),
        in_specs=in_specs,
        out_specs=out_specs,
        out_shape=out_shape,
        scratch_shapes=list(scratch),
        compiler_params=pltpu.CompilerParams(vmem_limit_bytes=vmem * 2**20),
        cost_estimate=pl.CostEstimate(flops=flops, bytes_accessed=nbytes, transcendentals=0),
    )


IN_HBM = pl.BlockSpec(memory_space=pltpu.HBM)


def in_hbm(array):
    return pltpu.with_memory_space_constraint(array, pltpu.HBM)


def copy_all(pairs, sems):
    copies = [
        pltpu.make_async_copy(source, target, sems.at[n]) for n, (source, target) in enumerate(pairs)
    ]
    for copy in copies:
        copy.start()
    return copies


def spec(block, *index):
    return pl.BlockSpec(block, lambda i: tuple(i if at == "i" else at for at in index))


def pack_strided_kernel(q_ref, k_ref, v_ref, c_ref, send_ref, rows_ref, out_ref, in_sem, out_sem):
    parts = 4
    size = BLOCK * 8 // parts
    copies = copy_all(
        [
            (ref.at[pl.ds(part * size, size)], rows_ref.at[array, pl.ds(part * size, size)])
            for part in range(parts)
            for array, ref in enumerate((q_ref, k_ref, v_ref, c_ref))
        ],
        in_sem,
    )
    row, col = iotas((128, 256))
    home, head, array, offset = row >> 6, (row >> 4) & 3, (row >> 2) & 3, row & 3
    pick = one_hot(col == array * 64 + ((home * OFFS + offset) * HEADS + head) * 2)
    sent = []
    for part in range(parts):
        for copy in copies[4 * part : 4 * part + 4]:
            copy.wait()
        for at in range(part * 64 // parts, (part + 1) * 64 // parts, 2):
            pair = [
                jnp.concatenate(
                    [rows_ref[array, 64 * n : 64 * (n + 1)] for n in (at, at + 1)], 1
                )
                for array in range(4)
            ]
            picked = dot(pick, jnp.concatenate(pair, 0)).astype(BF16)
            for n in range(2):
                for home in range(2):
                    for head in range(HEADS):
                        row = home * 64 + head * 16
                        out_ref[2 * (at + n) + home, :, head * HD : (head + 1) * HD] = picked[
                            row : row + 16, n * HD : (n + 1) * HD
                        ]
        where = pl.ds(part * NB // parts, NB // parts)
        copy = pltpu.make_async_copy(out_ref.at[where], send_ref.at[where], out_sem.at[part])
        copy.start()
        sent.append(copy)
    for copy in sent:
        copy.wait()


def pack_strided(arrays):
    return call(
        pack_strided_kernel,
        1,
        [IN_HBM] * 4,
        IN_HBM,
        jax.ShapeDtypeStruct((NB, 16, WIDTH), BF16),
        10**9,
        6 * 2**20,
        [
            pltpu.VMEM((4, BLOCK * 8, HD), BF16),
            pltpu.VMEM((NB, 16, WIDTH), BF16),
            pltpu.SemaphoreType.DMA((16,)),
            pltpu.SemaphoreType.DMA((4,)),
        ],
    )(*arrays)


def pack_summaries_kernel(key_ref, value_ref, out_ref):
    row, col = iotas((8, 32))
    parts = []
    for head in range(HEADS):
        pick = one_hot(col == row * 2 * HEADS + 2 * head + 1)
        parts += [dot(pick, ref[...])[:SUMM] for ref in (key_ref, value_ref)]
    rows = jnp.concatenate(parts, 1).astype(BF16)
    for z in range(out_ref.shape[0]):
        out_ref[z] = rows


def pack_summaries(keys, values):
    last = spec((8 * SUMM, HD), BLOCK // SUMM - 1, 0)
    shape = (PARTS[0], SUMM, 2 * WIDTH)
    return call(
        pack_summaries_kernel,
        1,
        [last, last],
        spec(shape, 0, 0, 0),
        jax.ShapeDtypeStruct(shape, BF16),
        10**6,
        2**17,
    )(in_hbm(keys), in_hbm(values))


def pack_fixed_kernel(q_ref, k_ref, v_ref, c_ref, out_ref):
    row, col = iotas((64, 128))
    pick = one_hot(col == ((row & 15) * HEADS + (row >> 4)) * 2 + 1)
    for at in range(16):
        rows = [ref[128 * at : 128 * (at + 1)] for ref in (q_ref, k_ref, v_ref, c_ref)]
        picked = dot(pick, jnp.concatenate(rows, 1)).astype(BF16)
        for array in range(4):
            for head in range(HEADS):
                out_ref[array, 16 * at : 16 * (at + 1), head * HD : (head + 1) * HD] = picked[
                    16 * head : 16 * (head + 1), array * HD : (array + 1) * HD
                ]


def pack_fixed(arrays):
    return call(
        pack_fixed_kernel,
        2,
        [spec((2048, HD), "i", 0)] * 4,
        spec((4, BLOCK // 2, WIDTH), 0, "i", 0),
        jax.ShapeDtypeStruct((4, BLOCK, WIDTH), BF16),
        10**9,
        6 * 2**20,
    )(*arrays)


def fixed_probabilities(query, key, summ_key, seen):
    row, col = iotas((BLOCK, BLOCK))
    own = jnp.where(col <= row, dot_nt(query, key) * scale, -jnp.inf)
    far = jnp.where(seen > 0, dot_nt(query, summ_key) * scale, -jnp.inf)
    top = jnp.maximum(
        jnp.max(own, axis=-1, keepdims=True), jnp.max(far, axis=-1, keepdims=True)
    )
    own = jnp.exp(own - top)
    far = jnp.exp(far - top)
    total = jnp.sum(own, axis=-1, keepdims=True) + jnp.sum(far, axis=-1, keepdims=True)
    inverse = 1.0 / total
    return own * inverse, far * inverse


def fixed_forward_kernel(rows_ref, summ_ref, seen_ref, attn_ref, own_ref, far_ref, sums_ref):
    own, far = fixed_probabilities(rows_ref[0], rows_ref[1], summ_ref[:, :HD], seen_ref[...])
    own_ref[0] = own.astype(BF16)
    far_ref[0] = far.astype(BF16)
    attn = (dot(own_ref[0], rows_ref[2]) + dot(far_ref[0], summ_ref[:, HD:])).astype(BF16)
    attn_ref[...] = attn
    wide = attn.astype(F32)
    square = jnp.sum(wide * wide, axis=-1, keepdims=True)
    cross = jnp.sum(wide * rows_ref[3].astype(F32), axis=-1, keepdims=True)
    lane = lax.broadcasted_iota(jnp.int32, (BLOCK, 8), 1)
    part = jnp.where(lane == 0, square, jnp.where(lane == 1, cross, 0.0))

    @pl.when(pl.program_id(0) == 0)
    def _():
        sums_ref[...] = part

    @pl.when(pl.program_id(0) > 0)
    def _():
        sums_ref[...] += part


def fixed_forward(rows, summ, seen):
    return call(
        fixed_forward_kernel,
        HEADS,
        [
            spec((4, BLOCK, HD), 0, 0, "i"),
            spec((BLOCK, 2 * HD), 0, "i"),
            spec((1, BLOCK), 0, 0),
        ],
        [
            spec((BLOCK, HD), 0, "i"),
            spec((1, BLOCK, BLOCK), "i", 0, 0),
            spec((1, BLOCK, BLOCK), "i", 0, 0),
            spec((BLOCK, 8), 0, 0),
        ],
        [
            jax.ShapeDtypeStruct((BLOCK, WIDTH), BF16),
            pltpu.HBM((HEADS, BLOCK, BLOCK), BF16),
            pltpu.HBM((HEADS, BLOCK, BLOCK), BF16),
            jax.ShapeDtypeStruct((BLOCK, 8), F32),
        ],
        4 * 10**9,
        4 * 2**20,
    )(rows, summ, seen)


def swap_matrix():
    row, col = iotas((256, 256))
    return one_hot(col == ((row & 15) << 4) + (row >> 4))


def strided_forward_kernel(
    recv_ref, fixed_ref, keys_out, prob_out, grp_ref, sums_ref, send_ref, keys_ref, prob_ref, sem
):
    swap = swap_matrix()
    for at in range(0, NB, 16):
        rows = dot(swap, recv_ref[at : at + 16].reshape(256, WIDTH)).astype(BF16)
        for head in range(HEADS):
            tiles = rows[:, head * HD : (head + 1) * HD].reshape(4, OFFS, 16, HD)
            keys_ref[head, :, :, at : at + 16, :] = tiles[:3]
            grp_ref[head, 0, :, at : at + 16, :] = tiles[3]
    copies = copy_all([(keys_ref, keys_out)], sem.at[0])
    row, col = iotas((NB, NB))
    heads = range(HEADS)
    scores = [batch_dot(keys_ref[head, 0], keys_ref[head, 1], 2, 2) * scale for head in heads]
    scores = [jnp.where((col <= row)[None], score, -jnp.inf) for score in scores]
    expos = [jnp.exp(score - jnp.max(score, axis=-1, keepdims=True)) for score in scores]
    probs = [
        (expo * (1.0 / jnp.sum(expo, axis=-1, keepdims=True))).astype(BF16) for expo in expos
    ]
    attns = [batch_dot(probs[head], keys_ref[head, 2], 2, 1).astype(BF16) for head in heads]
    square, cross = 0.0, 0.0
    for head in heads:
        prob_ref[head] = probs[head]
        copies += copy_all([(prob_ref.at[head], prob_out.at[head])], sem.at[head + 1])
        wide = attns[head].astype(F32)
        square += wide * wide
        cross += wide * grp_ref[head, 0].astype(F32)
        grp_ref[head, 1] = attns[head]
    square = jnp.sum(square, axis=-1, keepdims=True)
    cross = jnp.sum(cross, axis=-1, keepdims=True)
    lane = lax.broadcasted_iota(jnp.int32, (NB, HD), 1)
    part = fixed_ref[...]
    for at in range(OFFS):
        part += jnp.where(lane == 8 + at, square[at], jnp.where(lane == 12 + at, cross[at], 0.0))
    sums_ref[...] = part
    send_ref[...] = part.reshape(NB, 1, HD)
    for copy in copies:
        copy.wait()


def strided_forward(recv, fixed_sums):
    return call(
        strided_forward_kernel,
        1,
        [spec((NB, 16, WIDTH), 0, 0, 0), spec((NB, HD), 0, 0)],
        [
            IN_HBM,
            IN_HBM,
            spec((HEADS, 2, OFFS, NB, HD), 0, 0, 0, 0, 0),
            spec((NB, HD), 0, 0),
            spec((NB, 1, HD), 0, 0, 0),
        ],
        [
            pltpu.HBM((HEADS, 3, OFFS, NB, HD), BF16),
            pltpu.HBM((HEADS, OFFS, NB, NB), BF16),
            jax.ShapeDtypeStruct((HEADS, 2, OFFS, NB, HD), BF16),
            jax.ShapeDtypeStruct((NB, HD), F32),
            jax.ShapeDtypeStruct((NB, 1, HD), F32),
        ],
        10**9,
        6 * 2**20,
        [
            pltpu.VMEM((HEADS, 3, OFFS, NB, HD), BF16),
            pltpu.VMEM((HEADS, OFFS, NB, NB), BF16),
            pltpu.SemaphoreType.DMA((HEADS + 1, 1)),
        ],
        vmem=VMEM3,
    )(recv, fixed_sums)


def normalize(wide, cotangent, square, cross):
    scaling = lax.rsqrt(square / (2 * COLS) + epsilon)
    normed = (wide * scaling).astype(BF16)
    grad = (
        scaling * cotangent.astype(F32) - wide * (scaling * scaling * scaling * cross / (2 * COLS))
    ).astype(BF16)
    return normed, grad, jnp.sum(grad.astype(F32) * wide, axis=-1, keepdims=True)


def factors(sums_ref):
    row, col = iotas((BLOCK, NB))
    spread = one_hot(col == row >> 2)
    rest, columns = sums_ref[...], 0.0
    for _ in range(3):
        part = rest.astype(BF16)
        rest = rest - part.astype(F32)
        columns += dot_nt(spread, part)
    row, col = iotas((BLOCK, 8))
    square, cross = (
        jnp.sum(jnp.where(col == (row & 3) + at, columns, 0.0), axis=-1, keepdims=True)
        for at in (0, OFFS)
    )
    scaling = lax.rsqrt(square / (2 * COLS) + epsilon)
    other = scaling * scaling * scaling * cross / (2 * COLS)
    return jnp.broadcast_to(scaling, (BLOCK, HD)), jnp.broadcast_to(other, (BLOCK, HD))


def gradient(wide, cotangent, scaling, other):
    grad = (scaling * cotangent.astype(F32) - wide * other).astype(BF16)
    return grad, jnp.sum(grad.astype(F32) * wide, axis=-1, keepdims=True)


def strided_backward_kernel(
    keys_in, prob_in, grp_ref, sums_ref, other_ref, recv_ref, send_out,
    keys_ref, prob_ref, out_ref, send_ref, in_sem, out_sem,
):
    fetched = [
        copy_all(
            [(keys_in.at[head], keys_ref.at[head]), (prob_in.at[head], prob_ref.at[head])],
            in_sem.at[head],
        )
        for head in range(HEADS)
    ]
    moved = recv_ref[...].reshape(NB, HD)
    total = sums_ref[:, 8:16] + other_ref[...] + moved[:, :8]
    square = jnp.stack([total[:, at : at + 1] for at in range(OFFS)])
    cross = jnp.stack([total[:, OFFS + at : OFFS + at + 1] for at in range(OFFS)])
    grads = []
    for head in range(HEADS):
        wide = grp_ref[head, 1].astype(F32)
        normed, grad, row_dot = normalize(wide, grp_ref[head, 0], square, cross)
        out_ref[head, 0] = normed
        grads.append((grad, row_dot))
    heads = range(HEADS)
    for head in heads:
        for copy in fetched[head]:
            copy.wait()
    probs = [prob_ref[head] for head in heads]
    grad_probs = [batch_dot(grads[head][0], keys_ref[head, 2], 2, 2) for head in heads]
    scores = [
        (probs[head].astype(F32) * (grad_probs[head] - grads[head][1]) * scale).astype(BF16)
        for head in heads
    ]
    for head in heads:
        out_ref[head, 3] = batch_dot(probs[head], grads[head][0], 1, 1).astype(BF16)
    for head in heads:
        out_ref[head, 1] = batch_dot(scores[head], keys_ref[head, 1], 2, 1).astype(BF16)
    for head in heads:
        out_ref[head, 2] = batch_dot(scores[head], keys_ref[head, 0], 1, 1).astype(BF16)
    swap = swap_matrix()
    copies = []
    for at in range(0, NB, 16):
        rows = [out_ref[head, :, :, at : at + 16, :].reshape(256, HD) for head in range(HEADS)]
        moved = dot(swap, jnp.concatenate(rows, 1)).astype(BF16)
        send_ref[at : at + 16] = moved.reshape(16, 16, WIDTH)
        where = pl.ds(at, 16)
        copies += copy_all([(send_ref.at[where], send_out.at[where])], out_sem.at[at // 16])
    for copy in copies:
        copy.wait()


def strided_backward(keys, prob, grp, sums, other, recv):
    return call(
        strided_backward_kernel,
        1,
        [
            IN_HBM,
            IN_HBM,
            spec((HEADS, 2, OFFS, NB, HD), 0, 0, 0, 0, 0),
            spec((NB, HD), 0, 0),
            spec((NB, 8), 0, 0),
            spec((NB, 1, HD), 0, 0, 0),
        ],
        IN_HBM,
        pltpu.HBM((NB, 16, WIDTH), BF16),
        10**9,
        6 * 2**20,
        [
            pltpu.VMEM((HEADS, 3, OFFS, NB, HD), BF16),
            pltpu.VMEM((HEADS, OFFS, NB, NB), BF16),
            pltpu.VMEM((HEADS, 4, OFFS, NB, HD), BF16),
            pltpu.VMEM((NB, 16, WIDTH), BF16),
            pltpu.SemaphoreType.DMA((HEADS, 2)),
            pltpu.SemaphoreType.DMA((NB // 16, 1)),
        ],
        vmem=VMEM4,
    )(in_hbm(keys), in_hbm(prob), grp, sums, other, recv)


def summary_backward_kernel(
    rows_in, summ_in, far_in, attn_in, sums_ref, query_ref, keep_ref, send_ref,
    attn_ref, cot_ref, summ_ref, rows_ref, far_ref, sem,
):
    copies = copy_all(
        [
            (attn_in, attn_ref),
            (rows_in.at[3], cot_ref),
            (summ_in, summ_ref),
        ]
        + [(far_in.at[head], far_ref.at[head]) for head in range(HEADS)]
        + [(rows_in.at[0], rows_ref)],
        sem,
    )
    heads = range(HEADS)
    at = [slice(head * HD, (head + 1) * HD) for head in heads]
    to_key = [slice(2 * head * HD, (2 * head + 1) * HD) for head in heads]
    to_value = [slice((2 * head + 1) * HD, (2 * head + 2) * HD) for head in heads]
    scaling, other = factors(sums_ref)
    copies[0].wait()
    copies[1].wait()
    grads = [
        gradient(attn_ref[:, at[head]].astype(F32), cot_ref[:, at[head]], scaling, other)
        for head in heads
    ]
    scores = []
    copies[2].wait()
    for head in heads:
        copies[3 + head].wait()
        grad, row_dot = grads[head]
        grad_prob = dot_nt(grad, summ_ref[:, to_value[head]])
        score = far_ref[head].astype(F32) * (grad_prob - row_dot) * scale
        scores.append(score.astype(BF16))

    def put(to, grads):
        grads = grads.reshape(2, 8, 2, 16, HD)
        keep = jnp.stack([grads[0, :, 0], grads[1, :, 1]], 1)
        send = jnp.stack([grads[1, :, 0], grads[0, :, 1]], 1)
        keep_ref[:, to] = keep.reshape(BLOCK // 2, HD)
        send_ref[:, to] = send.reshape(BLOCK // 2, HD).astype(BF16)

    for head in heads:
        put(to_value[head], dot_tn(far_ref[head], grads[head][0]))
    copies[3 + HEADS].wait()
    for head in heads:
        put(to_key[head], dot_tn(scores[head], rows_ref[:, at[head]]))
    for head in heads:
        query_ref[:, at[head]] = dot(scores[head], summ_ref[:, to_key[head]])


def summary_backward(rows, summ, far, attn, sums):
    return call(
        summary_backward_kernel,
        1,
        [IN_HBM] * 4 + [spec((8, NB), 0, 0)],
        [
            spec((BLOCK, WIDTH), 0, 0),
            spec((BLOCK // 2, 2 * WIDTH), 0, 0),
            spec((BLOCK // 2, 2 * WIDTH), 0, 0),
        ],
        [
            pltpu.HBM((BLOCK, WIDTH), F32),
            jax.ShapeDtypeStruct((BLOCK // 2, 2 * WIDTH), F32),
            jax.ShapeDtypeStruct((BLOCK // 2, 2 * WIDTH), BF16),
        ],
        3 * 10**9,
        8 * 2**20,
        [
            pltpu.VMEM((BLOCK, WIDTH), BF16),
            pltpu.VMEM((BLOCK, WIDTH), BF16),
            pltpu.VMEM((BLOCK, 2 * WIDTH), BF16),
            pltpu.VMEM((BLOCK, WIDTH), BF16),
            pltpu.VMEM((HEADS, BLOCK, BLOCK), BF16),
            pltpu.SemaphoreType.DMA((8,)),
        ],
        vmem=VMEM5,
    )(*[in_hbm(array) for array in (rows, summ, far, attn)], sums)


def fixed_backward_kernel(
    rows_in, own_in, attn_in, sums_ref, query_in, out_out, tail_ref,
    rows_ref, own_ref, attn_ref, query_ref, out_ref, sem, out_sem,
):
    copies = copy_all(
        [(attn_in, attn_ref)]
        + [(rows_in.at[array], rows_ref.at[array]) for array in (3, 2)]
        + [(own_in.at[head], own_ref.at[head]) for head in range(HEADS)]
        + [(rows_in.at[array], rows_ref.at[array]) for array in (0, 1)]
        + [(query_in, query_ref)],
        sem,
    )
    heads = range(HEADS)
    at = [slice(head * HD, (head + 1) * HD) for head in heads]
    low, high = slice(0, BLOCK // 2), slice(BLOCK // 2, BLOCK)
    scaling, other = factors(sums_ref)
    copies[0].wait()
    copies[1].wait()
    grads = []
    for head in heads:
        wide = attn_ref[:, at[head]].astype(F32)
        out_ref[0, :, at[head]] = (wide * scaling).astype(BF16)
        grads.append(gradient(wide, rows_ref[3, :, at[head]], scaling, other))
    sent = copy_all([(out_ref.at[0], out_out.at[0])], out_sem.at[0])
    scores = []
    copies[2].wait()
    for head in heads:
        copies[3 + head].wait()
        grad, row_dot = grads[head]
        first = dot_nt(grad[low], rows_ref[2, low, at[head]]) - row_dot[low]
        second = dot_nt(grad[high], rows_ref[2, :, at[head]]) - row_dot[high]
        first = (own_ref[head, low, low].astype(F32) * first * scale).astype(BF16)
        second = (own_ref[head, high, :].astype(F32) * second * scale).astype(BF16)
        scores.append((first, second))

    def put(array, head, first, second, b):
        grads_low = dot_tn(first, b[low]) + dot_tn(second[:, low], b[high])
        grads_high = dot_tn(second[:, high], b[high])
        out_ref[array, low, at[head]] = grads_low.astype(BF16)
        out_ref[array, high, at[head]] = grads_high.astype(BF16)
        tail_ref[array - 2, :, at[head]] = grads_high[BLOCK // 2 - 8 :]

    for head in heads:
        put(3, head, own_ref[head, low, low], own_ref[head, high, :], grads[head][0])
    sent += copy_all([(out_ref.at[3], out_out.at[3])], out_sem.at[3])
    copies[3 + HEADS].wait()
    for head in heads:
        put(2, head, *scores[head], rows_ref[0, :, at[head]])
    sent += copy_all([(out_ref.at[2], out_out.at[2])], out_sem.at[2])
    copies[4 + HEADS].wait()
    copies[5 + HEADS].wait()
    for head in heads:
        first, second = scores[head]
        out_ref[1, low, at[head]] = (
            dot(first, rows_ref[1, low, at[head]]) + query_ref[low, at[head]]
        ).astype(BF16)
        out_ref[1, high, at[head]] = (
            dot(second, rows_ref[1, :, at[head]]) + query_ref[high, at[head]]
        ).astype(BF16)
    sent += copy_all([(out_ref.at[1], out_out.at[1])], out_sem.at[1])
    for copy in sent:
        copy.wait()


def fixed_backward(rows, own, attn, sums, far_query):
    return call(
        fixed_backward_kernel,
        1,
        [IN_HBM, IN_HBM, IN_HBM, spec((8, NB), 0, 0), IN_HBM],
        [IN_HBM, spec((2, 8, WIDTH), 0, 0, 0)],
        [
            pltpu.HBM((4, BLOCK, WIDTH), BF16),
            jax.ShapeDtypeStruct((2, 8, WIDTH), F32),
        ],
        5 * 10**9,
        8 * 2**20,
        [
            pltpu.VMEM((4, BLOCK, WIDTH), BF16),
            pltpu.VMEM((HEADS, BLOCK, BLOCK), BF16),
            pltpu.VMEM((BLOCK, WIDTH), BF16),
            pltpu.VMEM((BLOCK, WIDTH), F32),
            pltpu.VMEM((4, BLOCK, WIDTH), BF16),
            pltpu.SemaphoreType.DMA((HEADS + 6,)),
            pltpu.SemaphoreType.DMA((4, 1)),
        ],
        vmem=VMEM5,
    )(*[in_hbm(array) for array in (rows, own, attn)], sums, in_hbm(far_query))


def unpack_kernel(recv_ref, fixed_in, parts_ref, moved_ref, tails_ref, *refs):
    outs, fixed_ref, out_ref, in_sem, out_sem = refs[:4], refs[4], refs[5], refs[6], refs[7]
    parts = 4
    size = BLOCK // parts
    copies = copy_all(
        [
            (fixed_in.at[:, pl.ds(part * size, size)], fixed_ref.at[:, pl.ds(part * size, size)])
            for part in range(parts)
        ],
        in_sem,
    )
    sent = []
    row, col = iotas((512, 512))
    array, token, head, kind = row >> 7, (row >> 3) & 15, (row >> 1) & 3, row & 1
    strided = (token >> 2) * 64 + head * 16 + array * OFFS + (token & 3)
    fixed = 256 + array * 64 + head * 16 + token
    pick = one_hot(col == jnp.where(kind == 0, strided, fixed))
    end = lax.broadcasted_iota(jnp.int32, (16, WIDTH), 0) >= 16 - SUMM
    totals = parts_ref[...] + moved_ref[...].astype(F32)
    tails = []
    for array in range(2):
        part = [totals[:, n * HD : (n + 1) * HD] for n in range(array, 2 * HEADS, 2)]
        part = jnp.concatenate(part, 1) + tails_ref[array, 8 - SUMM :]
        part = jnp.concatenate([jnp.zeros((16 - SUMM, WIDTH), F32), part], 0)
        tails.append(part.astype(BF16))
    for at in range(0, 32, 2):
        if at * 16 % size == 0:
            copies[at * 16 // size].wait()
        pair = []
        for n in (at, at + 1):
            tile = 16 * n
            fixed = [fixed_ref[array, tile : tile + 16] for array in range(4)]
            if tile == BLOCK - 16:
                for array in (2, 3):
                    fixed[array] = jnp.where(end, tails[array - 2], fixed[array])
            heads = [slice(head * HD, (head + 1) * HD) for head in range(HEADS)]
            rows = [recv_ref[4 * n + home, :, head] for home in range(4) for head in heads]
            rows += [part[:, head] for part in fixed for head in heads]
            pair.append(jnp.concatenate(rows, 0))
        picked = dot(pick, jnp.concatenate(pair, 1)).astype(BF16)
        for n in range(2):
            for array in range(4):
                out_ref[array, 128 * (at + n) : 128 * (at + n + 1)] = picked[
                    array * 128 : (array + 1) * 128, n * HD : (n + 1) * HD
                ]
        if (at + 2) * 16 % size == 0:
            part = at * 16 // size
            where = pl.ds(part * size * 8, size * 8)
            sent += copy_all(
                [(out_ref.at[array, where], outs[array].at[where]) for array in range(4)],
                out_sem.at[part],
            )
    for copy in sent:
        copy.wait()


def unpack(recv, fixed, parts, moved, tails):
    rows = call(
        unpack_kernel,
        1,
        [spec((NB, 16, WIDTH), 0, 0, 0), IN_HBM]
        + [spec((SUMM, 2 * WIDTH), 0, 0)] * 2
        + [spec((2, 8, WIDTH), 0, 0, 0)],
        [IN_HBM] * 4,
        [jax.ShapeDtypeStruct((BLOCK * 8, HD), BF16)] * 4,
        2 * 10**9,
        8 * 2**20,
        [
            pltpu.VMEM((4, BLOCK, WIDTH), BF16),
            pltpu.VMEM((4, BLOCK * 8, HD), BF16),
            pltpu.SemaphoreType.DMA((4,)),
            pltpu.SemaphoreType.DMA((4, 4)),
        ],
        vmem=VMEM6,
    )(recv, in_hbm(fixed), parts, moved, tails)
    return tuple(unflat(array) for array in rows)


def place(index):
    coords = []
    for size in PARTS[::-1]:
        coords.append(index % size)
        index = index // size
    return coords[::-1]


def joined(coords):
    index = 0
    for size, at in zip(PARTS, coords):
        index = index * size + at
    return index


def shift(array, part, step):
    perm = []
    for source in range(NB):
        coords = place(source)
        coords[part] = (coords[part] + step) % PARTS[part]
        perm.append((source, joined(coords)))
    return lax.ppermute(array, "seq", perm)


def other_head(array):
    return lax.ppermute(array, "head", [(0, 1), (1, 0)])


Z, X, Y, CORE = range(4)
Y_BACK = (0, 1, -1, 2)
SLAB = 2 * WIDTH


def gather_along_z(sent, me):
    size = PARTS[Z]
    step = NB // size
    groups = [[at + step * z for z in range(size)] for at in range(step)]
    held = lax.all_to_all(sent, "seq", 0, 0, axis_index_groups=groups, tiled=True)
    held = jnp.concatenate([held, held], 0)
    first = (me // step + 4 * (me % 2)) % size
    return lax.dynamic_slice_in_dim(held, first, size, 0).reshape(size * SUMM, SLAB)


def gather_summaries(held):
    held = jnp.concatenate([held, shift(held, X, 1)], 0)
    held = jnp.concatenate([held] + [shift(held, Y, back) for back in Y_BACK[1:]], 0)
    return jnp.concatenate([held, shift(held, CORE, 1)], 0)


def add_up(own, moved):
    return sum((part.astype(F32) for part in moved), own)


def scatter_along_core(kept, sent):
    return add_up(kept, [shift(sent, CORE, 1)])


def scatter_along_y(parts):
    parts = parts.reshape(4, -1, SLAB)
    sent = parts.astype(BF16)
    return add_up(parts[0], [shift(sent[n], Y, -Y_BACK[n]) for n in range(1, 4)])


def scatter_summaries(parts):
    parts = parts.reshape(2, -1, SLAB)
    parts = add_up(parts[0], [shift(parts[1].astype(BF16), X, -1)])
    sent = parts.astype(BF16).reshape(2, 4, SUMM, SLAB)
    moved = []
    for n in range(4):
        perm = []
        for source in range(NB):
            coords = place(source)
            coords[Z] = (coords[Z] + 4 * coords[CORE] + n) % PARTS[Z]
            perm.append((source, joined(coords)))
        moved.append(lax.ppermute(sent[:, n].reshape(2 * SUMM, SLAB), "seq", perm))
    parts = add_up(0.0, moved)
    return parts[:SUMM], shift(parts[SUMM:].astype(BF16), CORE, 1)


def slot_blocks(me):
    slots = jnp.arange(NB, dtype=jnp.int32)
    z, x, y, core = place(me)
    core_of = (core - (slots >> 6)) % 2
    y_of = (y - jnp.array(Y_BACK, jnp.int32)[(slots >> 4) & 3]) % PARTS[Y]
    x_of = (x - ((slots >> 3) & 1)) % PARTS[X]
    z_of = (z + 4 * core_of + (slots & 7)) % PARTS[Z]
    return joined((z_of, x_of, y_of, core_of))


def shards(queries, key_rows, value_rows, cotangent):
    me = lax.axis_index("seq")
    arrays = tuple(flat(array) for array in (queries, key_rows, value_rows, cotangent))
    send = pack_strided(arrays)
    summ = gather_along_z(pack_summaries(arrays[1], arrays[2]), me)
    send, summ = lax.optimization_barrier((send, summ))
    recv = lax.all_to_all(send, "seq", 0, 0, tiled=True)
    summ = gather_summaries(summ)
    seen = jnp.repeat((slot_blocks(me) < me).astype(jnp.int32), SUMM)[None]
    rows = pack_fixed(arrays)
    fixed_attn, own_prob, far_prob, fixed_sums = fixed_forward(rows, summ, seen)
    fixed_send = fixed_sums[:, :2].reshape(NB, OFFS, 2).transpose(0, 2, 1).reshape(NB, 8)
    fixed_both = fixed_send + other_head(fixed_send)
    keys, prob, grp, sums, sums_send = strided_forward(recv, jnp.pad(fixed_both, ((0, 0), (0, HD - 8))))
    sums_in = lax.all_to_all(sums_send, "seq", 0, 0, tiled=True)
    sums_other = other_head(sums[:, 8:16])
    own_sums = sums_in[:, 0, 8:16].T
    block_sums = fixed_both.T + own_sums + other_head(own_sums)
    send_back = strided_backward(keys, prob, grp, sums, sums_other, sums_in)
    recv_back = lax.all_to_all(send_back, "seq", 0, 0, tiled=True)
    far_query, kept, sent = summary_backward(rows, summ, far_prob, fixed_attn, block_sums)
    fixed_out, tails = fixed_backward(rows, own_prob, fixed_attn, block_sums, far_query)
    parts = scatter_along_y(scatter_along_core(kept, sent))
    parts, fixed_out, tails = lax.optimization_barrier((parts, fixed_out, tails))
    parts, moved = scatter_summaries(parts)
    return unpack(recv_back, fixed_out, parts, moved, tails)


def solution(mesh):
    specs = (P("seq", None, "head"),) * 4
    return jax.shard_map(shards, mesh=mesh, in_specs=specs, out_specs=specs, check_vma=False)
```

```python
import jax
import jax.numpy as jnp
from jax import lax
from jax.experimental import pallas as pl
from jax.experimental.pallas import tpu as pltpu
from jax.sharding import PartitionSpec as P

BLOCK = 512
SUMM = 4
HD = 128
COLS = 1024
NB = 128
HEADS = 4
EIGHTS = BLOCK // 8
OFFS = 4
WIDTH = HEADS * HD
PARTS = (8, 2, 4, 2)
VMEM3, VMEM4, VMEM5, VMEM6 = 32, 32, 48, 32

epsilon = 1e-06
scale = HD ** (-0.5)
F32 = jnp.float32
BF16 = jnp.bfloat16


def iotas(shape):
    return (
        lax.broadcasted_iota(jnp.int32, shape, 0),
        lax.broadcasted_iota(jnp.int32, shape, 1),
    )


def index_columns(rows, columns):
    return (
        lax.broadcasted_iota(jnp.int32, (rows, 1), 0),
        lax.broadcasted_iota(jnp.int32, (1, columns), 1),
    )


def one_hot(hit):
    return jnp.where(hit, 1.0, 0.0).astype(BF16)


def dot(a, b):
    return jnp.dot(a, b, preferred_element_type=F32)


def dot_nt(a, b):
    return lax.dot_general(a, b, (((1,), (1,)), ((), ())), preferred_element_type=F32)


def dot_tn(a, b):
    return lax.dot_general(a, b, (((0,), (0,)), ((), ())), preferred_element_type=F32)


def batch_dot(a, b, left, right):
    return lax.dot_general(
        a, b, (((left,), (right,)), ((0,), (0,))), preferred_element_type=F32
    )


def flat(array):
    split = array.reshape(BLOCK, 2, HEADS, HD).transpose(0, 2, 1, 3)
    return split.reshape(BLOCK * HEADS * 2, HD)


def unflat(rows):
    return rows.reshape(BLOCK, HEADS, 2, HD).transpose(0, 2, 1, 3).reshape(BLOCK, 2, WIDTH)


def call(kernel, grid, in_specs, out_specs, out_shape, flops, nbytes, scratch=(), vmem=60):
    return pl.pallas_call(
        kernel,
        grid=(grid,),
        in_specs=in_specs,
        out_specs=out_specs,
        out_shape=out_shape,
        scratch_shapes=list(scratch),
        compiler_params=pltpu.CompilerParams(vmem_limit_bytes=vmem * 2**20),
        cost_estimate=pl.CostEstimate(flops=flops, bytes_accessed=nbytes, transcendentals=0),
    )


IN_HBM = pl.BlockSpec(memory_space=pltpu.HBM)


def in_hbm(array):
    return pltpu.with_memory_space_constraint(array, pltpu.HBM)


def copy_all(pairs, sems):
    copies = [
        pltpu.make_async_copy(source, target, sems.at[n]) for n, (source, target) in enumerate(pairs)
    ]
    for copy in copies:
        copy.start()
    return copies


def spec(block, *index):
    return pl.BlockSpec(block, lambda i: tuple(i if at == "i" else at for at in index))


def pack_strided_kernel(q_ref, k_ref, v_ref, c_ref, send_ref, rows_ref, out_ref, in_sem, out_sem):
    parts = 4
    size = BLOCK * 8 // parts
    copies = copy_all(
        [
            (ref.at[pl.ds(part * size, size)], rows_ref.at[array, pl.ds(part * size, size)])
            for part in range(parts)
            for array, ref in enumerate((q_ref, k_ref, v_ref, c_ref))
        ],
        in_sem,
    )
    row, col = iotas((128, 256))
    home, head, array, offset = row >> 6, (row >> 4) & 3, (row >> 2) & 3, row & 3
    pick = one_hot(col == array * 64 + ((home * OFFS + offset) * HEADS + head) * 2)
    sent = []
    for part in range(parts):
        for copy in copies[4 * part : 4 * part + 4]:
            copy.wait()
        for at in range(part * 64 // parts, (part + 1) * 64 // parts, 2):
            pair = [
                jnp.concatenate(
                    [rows_ref[array, 64 * n : 64 * (n + 1)] for n in (at, at + 1)], 1
                )
                for array in range(4)
            ]
            picked = dot(pick, jnp.concatenate(pair, 0)).astype(BF16)
            for n in range(2):
                for home in range(2):
                    for head in range(HEADS):
                        row = home * 64 + head * 16
                        out_ref[2 * (at + n) + home, :, head * HD : (head + 1) * HD] = picked[
                            row : row + 16, n * HD : (n + 1) * HD
                        ]
        where = pl.ds(part * NB // parts, NB // parts)
        copy = pltpu.make_async_copy(out_ref.at[where], send_ref.at[where], out_sem.at[part])
        copy.start()
        sent.append(copy)
    for copy in sent:
        copy.wait()


def pack_strided(arrays):
    return call(
        pack_strided_kernel,
        1,
        [IN_HBM] * 4,
        IN_HBM,
        jax.ShapeDtypeStruct((NB, 16, WIDTH), BF16),
        10**9,
        6 * 2**20,
        [
            pltpu.VMEM((4, BLOCK * 8, HD), BF16),
            pltpu.VMEM((NB, 16, WIDTH), BF16),
            pltpu.SemaphoreType.DMA((16,)),
            pltpu.SemaphoreType.DMA((4,)),
        ],
    )(*arrays)


def pack_summaries_kernel(key_ref, value_ref, out_ref):
    row, col = iotas((8, 32))
    parts = []
    for head in range(HEADS):
        pick = one_hot(col == row * 2 * HEADS + 2 * head + 1)
        parts += [dot(pick, ref[...])[:SUMM] for ref in (key_ref, value_ref)]
    rows = jnp.concatenate(parts, 1).astype(BF16)
    for z in range(out_ref.shape[0]):
        out_ref[z] = rows


def pack_summaries(keys, values):
    last = spec((8 * SUMM, HD), BLOCK // SUMM - 1, 0)
    shape = (PARTS[0], SUMM, 2 * WIDTH)
    return call(
        pack_summaries_kernel,
        1,
        [last, last],
        spec(shape, 0, 0, 0),
        jax.ShapeDtypeStruct(shape, BF16),
        10**6,
        2**17,
    )(in_hbm(keys), in_hbm(values))


def pack_fixed_kernel(q_ref, k_ref, v_ref, c_ref, out_ref):
    row, col = iotas((64, 128))
    pick = one_hot(col == ((row & 15) * HEADS + (row >> 4)) * 2 + 1)
    for at in range(16):
        rows = [ref[128 * at : 128 * (at + 1)] for ref in (q_ref, k_ref, v_ref, c_ref)]
        picked = dot(pick, jnp.concatenate(rows, 1)).astype(BF16)
        for array in range(4):
            for head in range(HEADS):
                out_ref[array, 16 * at : 16 * (at + 1), head * HD : (head + 1) * HD] = picked[
                    16 * head : 16 * (head + 1), array * HD : (array + 1) * HD
                ]


def pack_fixed(arrays):
    return call(
        pack_fixed_kernel,
        2,
        [spec((2048, HD), "i", 0)] * 4,
        spec((4, BLOCK // 2, WIDTH), 0, "i", 0),
        jax.ShapeDtypeStruct((4, BLOCK, WIDTH), BF16),
        10**9,
        6 * 2**20,
    )(*arrays)


def fixed_probabilities(query, key, summ_key, seen):
    row, col = iotas((BLOCK, BLOCK))
    own = jnp.where(col <= row, dot_nt(query, key) * scale, -jnp.inf)
    far = jnp.where(seen > 0, dot_nt(query, summ_key) * scale, -jnp.inf)
    top = jnp.maximum(
        jnp.max(own, axis=-1, keepdims=True), jnp.max(far, axis=-1, keepdims=True)
    )
    own = jnp.exp(own - top)
    far = jnp.exp(far - top)
    total = jnp.sum(own, axis=-1, keepdims=True) + jnp.sum(far, axis=-1, keepdims=True)
    inverse = 1.0 / total
    return own * inverse, far * inverse


def fixed_forward_kernel(rows_ref, summ_ref, seen_ref, attn_ref, own_ref, far_ref, sums_ref):
    own, far = fixed_probabilities(rows_ref[0], rows_ref[1], summ_ref[:, :HD], seen_ref[...])
    own_ref[0] = own.astype(BF16)
    far_ref[0] = far.astype(BF16)
    attn = (dot(own_ref[0], rows_ref[2]) + dot(far_ref[0], summ_ref[:, HD:])).astype(BF16)
    attn_ref[...] = attn
    wide = attn.astype(F32)
    square = jnp.sum(wide * wide, axis=-1, keepdims=True)
    cross = jnp.sum(wide * rows_ref[3].astype(F32), axis=-1, keepdims=True)
    lane = lax.broadcasted_iota(jnp.int32, (BLOCK, 8), 1)
    part = jnp.where(lane == 0, square, jnp.where(lane == 1, cross, 0.0))

    @pl.when(pl.program_id(0) == 0)
    def _():
        sums_ref[...] = part

    @pl.when(pl.program_id(0) > 0)
    def _():
        sums_ref[...] += part


def fixed_forward(rows, summ, seen):
    return call(
        fixed_forward_kernel,
        HEADS,
        [
            spec((4, BLOCK, HD), 0, 0, "i"),
            spec((BLOCK, 2 * HD), 0, "i"),
            spec((1, BLOCK), 0, 0),
        ],
        [
            spec((BLOCK, HD), 0, "i"),
            spec((1, BLOCK, BLOCK), "i", 0, 0),
            spec((1, BLOCK, BLOCK), "i", 0, 0),
            spec((BLOCK, 8), 0, 0),
        ],
        [
            jax.ShapeDtypeStruct((BLOCK, WIDTH), BF16),
            pltpu.HBM((HEADS, BLOCK, BLOCK), BF16),
            pltpu.HBM((HEADS, BLOCK, BLOCK), BF16),
            jax.ShapeDtypeStruct((BLOCK, 8), F32),
        ],
        4 * 10**9,
        4 * 2**20,
    )(rows, summ, seen)


def swap_matrix():
    row, col = iotas((256, 256))
    return one_hot(col == ((row & 15) << 4) + (row >> 4))


def strided_forward_kernel(
    recv_ref, fixed_ref, keys_out, prob_out, grp_ref, sums_ref, send_ref, keys_ref, prob_ref, sem
):
    swap = swap_matrix()
    for at in range(0, NB, 16):
        rows = dot(swap, recv_ref[at : at + 16].reshape(256, WIDTH)).astype(BF16)
        for head in range(HEADS):
            tiles = rows[:, head * HD : (head + 1) * HD].reshape(4, OFFS, 16, HD)
            keys_ref[head, :, :, at : at + 16, :] = tiles[:3]
            grp_ref[head, 0, :, at : at + 16, :] = tiles[3]
    copies = copy_all([(keys_ref, keys_out)], sem.at[0])
    row, col = iotas((NB, NB))
    heads = range(HEADS)
    scores = [batch_dot(keys_ref[head, 0], keys_ref[head, 1], 2, 2) * scale for head in heads]
    scores = [jnp.where((col <= row)[None], score, -jnp.inf) for score in scores]
    expos = [jnp.exp(score - jnp.max(score, axis=-1, keepdims=True)) for score in scores]
    probs = [
        (expo * (1.0 / jnp.sum(expo, axis=-1, keepdims=True))).astype(BF16) for expo in expos
    ]
    attns = [batch_dot(probs[head], keys_ref[head, 2], 2, 1).astype(BF16) for head in heads]
    square, cross = 0.0, 0.0
    for head in heads:
        prob_ref[head] = probs[head]
        copies += copy_all([(prob_ref.at[head], prob_out.at[head])], sem.at[head + 1])
        wide = attns[head].astype(F32)
        square += wide * wide
        cross += wide * grp_ref[head, 0].astype(F32)
        grp_ref[head, 1] = attns[head]
    square = jnp.sum(square, axis=-1, keepdims=True)
    cross = jnp.sum(cross, axis=-1, keepdims=True)
    lane = lax.broadcasted_iota(jnp.int32, (NB, HD), 1)
    part = fixed_ref[...]
    for at in range(OFFS):
        part += jnp.where(lane == 8 + at, square[at], jnp.where(lane == 12 + at, cross[at], 0.0))
    sums_ref[...] = part
    send_ref[...] = part.reshape(NB, 1, HD)
    for copy in copies:
        copy.wait()


def strided_forward(recv, fixed_sums):
    return call(
        strided_forward_kernel,
        1,
        [spec((NB, 16, WIDTH), 0, 0, 0), spec((NB, HD), 0, 0)],
        [
            IN_HBM,
            IN_HBM,
            spec((HEADS, 2, OFFS, NB, HD), 0, 0, 0, 0, 0),
            spec((NB, HD), 0, 0),
            spec((NB, 1, HD), 0, 0, 0),
        ],
        [
            pltpu.HBM((HEADS, 3, OFFS, NB, HD), BF16),
            pltpu.HBM((HEADS, OFFS, NB, NB), BF16),
            jax.ShapeDtypeStruct((HEADS, 2, OFFS, NB, HD), BF16),
            jax.ShapeDtypeStruct((NB, HD), F32),
            jax.ShapeDtypeStruct((NB, 1, HD), F32),
        ],
        10**9,
        6 * 2**20,
        [
            pltpu.VMEM((HEADS, 3, OFFS, NB, HD), BF16),
            pltpu.VMEM((HEADS, OFFS, NB, NB), BF16),
            pltpu.SemaphoreType.DMA((HEADS + 1, 1)),
        ],
        vmem=VMEM3,
    )(recv, fixed_sums)


def normalize(wide, cotangent, square, cross):
    scaling = lax.rsqrt(square / (2 * COLS) + epsilon)
    normed = (wide * scaling).astype(BF16)
    grad = (
        scaling * cotangent.astype(F32) - wide * (scaling * scaling * scaling * cross / (2 * COLS))
    ).astype(BF16)
    return normed, grad, jnp.sum(grad.astype(F32) * wide, axis=-1, keepdims=True)


def factors(sums_ref):
    row, col = iotas((BLOCK, NB))
    spread = one_hot(col == row >> 2)
    rest, columns = sums_ref[...], 0.0
    for _ in range(3):
        part = rest.astype(BF16)
        rest = rest - part.astype(F32)
        columns += dot_nt(spread, part)
    row, col = iotas((BLOCK, 8))
    square, cross = (
        jnp.sum(jnp.where(col == (row & 3) + at, columns, 0.0), axis=-1, keepdims=True)
        for at in (0, OFFS)
    )
    scaling = lax.rsqrt(square / (2 * COLS) + epsilon)
    other = scaling * scaling * scaling * cross / (2 * COLS)
    return jnp.broadcast_to(scaling, (BLOCK, HD)), jnp.broadcast_to(other, (BLOCK, HD))


def gradient(wide, cotangent, scaling, other):
    grad = (scaling * cotangent.astype(F32) - wide * other).astype(BF16)
    return grad, jnp.sum(grad.astype(F32) * wide, axis=-1, keepdims=True)


def strided_backward_kernel(
    keys_in, prob_in, grp_ref, sums_ref, other_ref, recv_ref, send_out,
    keys_ref, prob_ref, out_ref, send_ref, in_sem, out_sem,
):
    fetched = [
        copy_all(
            [(keys_in.at[head], keys_ref.at[head]), (prob_in.at[head], prob_ref.at[head])],
            in_sem.at[head],
        )
        for head in range(HEADS)
    ]
    moved = recv_ref[...].reshape(NB, HD)
    total = sums_ref[:, 8:16] + other_ref[...] + moved[:, :8]
    square = jnp.stack([total[:, at : at + 1] for at in range(OFFS)])
    cross = jnp.stack([total[:, OFFS + at : OFFS + at + 1] for at in range(OFFS)])
    grads = []
    for head in range(HEADS):
        wide = grp_ref[head, 1].astype(F32)
        normed, grad, row_dot = normalize(wide, grp_ref[head, 0], square, cross)
        out_ref[head, 0] = normed
        grads.append((grad, row_dot))
    heads = range(HEADS)
    for head in heads:
        for copy in fetched[head]:
            copy.wait()
    probs = [prob_ref[head] for head in heads]
    grad_probs = [batch_dot(grads[head][0], keys_ref[head, 2], 2, 2) for head in heads]
    scores = [
        (probs[head].astype(F32) * (grad_probs[head] - grads[head][1]) * scale).astype(BF16)
        for head in heads
    ]
    for head in heads:
        out_ref[head, 3] = batch_dot(probs[head], grads[head][0], 1, 1).astype(BF16)
    for head in heads:
        out_ref[head, 1] = batch_dot(scores[head], keys_ref[head, 1], 2, 1).astype(BF16)
    for head in heads:
        out_ref[head, 2] = batch_dot(scores[head], keys_ref[head, 0], 1, 1).astype(BF16)
    swap = swap_matrix()
    copies = []
    for at in range(0, NB, 16):
        rows = [out_ref[head, :, :, at : at + 16, :].reshape(256, HD) for head in range(HEADS)]
        moved = dot(swap, jnp.concatenate(rows, 1)).astype(BF16)
        send_ref[at : at + 16] = moved.reshape(16, 16, WIDTH)
        where = pl.ds(at, 16)
        copies += copy_all([(send_ref.at[where], send_out.at[where])], out_sem.at[at // 16])
    for copy in copies:
        copy.wait()


def strided_backward(keys, prob, grp, sums, other, recv):
    return call(
        strided_backward_kernel,
        1,
        [
            IN_HBM,
            IN_HBM,
            spec((HEADS, 2, OFFS, NB, HD), 0, 0, 0, 0, 0),
            spec((NB, HD), 0, 0),
            spec((NB, 8), 0, 0),
            spec((NB, 1, HD), 0, 0, 0),
        ],
        IN_HBM,
        pltpu.HBM((NB, 16, WIDTH), BF16),
        10**9,
        6 * 2**20,
        [
            pltpu.VMEM((HEADS, 3, OFFS, NB, HD), BF16),
            pltpu.VMEM((HEADS, OFFS, NB, NB), BF16),
            pltpu.VMEM((HEADS, 4, OFFS, NB, HD), BF16),
            pltpu.VMEM((NB, 16, WIDTH), BF16),
            pltpu.SemaphoreType.DMA((HEADS, 2)),
            pltpu.SemaphoreType.DMA((NB // 16, 1)),
        ],
        vmem=VMEM4,
    )(in_hbm(keys), in_hbm(prob), grp, sums, other, recv)


def summary_backward_kernel(
    rows_in, summ_in, far_in, attn_in, sums_ref, query_ref, keep_ref, send_ref,
    attn_ref, cot_ref, summ_ref, rows_ref, far_ref, sem,
):
    copies = copy_all(
        [
            (attn_in, attn_ref),
            (rows_in.at[3], cot_ref),
            (summ_in, summ_ref),
        ]
        + [(far_in.at[head], far_ref.at[head]) for head in range(HEADS)]
        + [(rows_in.at[0], rows_ref)],
        sem,
    )
    heads = range(HEADS)
    at = [slice(head * HD, (head + 1) * HD) for head in heads]
    to_key = [slice(2 * head * HD, (2 * head + 1) * HD) for head in heads]
    to_value = [slice((2 * head + 1) * HD, (2 * head + 2) * HD) for head in heads]
    scaling, other = factors(sums_ref)
    copies[0].wait()
    copies[1].wait()
    grads = [
        gradient(attn_ref[:, at[head]].astype(F32), cot_ref[:, at[head]], scaling, other)
        for head in heads
    ]
    scores = []
    copies[2].wait()
    for head in heads:
        copies[3 + head].wait()
        grad, row_dot = grads[head]
        grad_prob = dot_nt(grad, summ_ref[:, to_value[head]])
        score = far_ref[head].astype(F32) * (grad_prob - row_dot) * scale
        scores.append(score.astype(BF16))

    def put(to, grads):
        grads = grads.reshape(2, 8, 2, 16, HD)
        keep = jnp.stack([grads[0, :, 0], grads[1, :, 1]], 1)
        send = jnp.stack([grads[1, :, 0], grads[0, :, 1]], 1)
        keep_ref[:, to] = keep.reshape(BLOCK // 2, HD)
        send_ref[:, to] = send.reshape(BLOCK // 2, HD).astype(BF16)

    for head in heads:
        put(to_value[head], dot_tn(far_ref[head], grads[head][0]))
    copies[3 + HEADS].wait()
    for head in heads:
        put(to_key[head], dot_tn(scores[head], rows_ref[:, at[head]]))
    for head in heads:
        query_ref[:, at[head]] = dot(scores[head], summ_ref[:, to_key[head]])


def summary_backward(rows, summ, far, attn, sums):
    return call(
        summary_backward_kernel,
        1,
        [IN_HBM] * 4 + [spec((8, NB), 0, 0)],
        [
            spec((BLOCK, WIDTH), 0, 0),
            spec((BLOCK // 2, 2 * WIDTH), 0, 0),
            spec((BLOCK // 2, 2 * WIDTH), 0, 0),
        ],
        [
            pltpu.HBM((BLOCK, WIDTH), F32),
            jax.ShapeDtypeStruct((BLOCK // 2, 2 * WIDTH), F32),
            jax.ShapeDtypeStruct((BLOCK // 2, 2 * WIDTH), BF16),
        ],
        3 * 10**9,
        8 * 2**20,
        [
            pltpu.VMEM((BLOCK, WIDTH), BF16),
            pltpu.VMEM((BLOCK, WIDTH), BF16),
            pltpu.VMEM((BLOCK, 2 * WIDTH), BF16),
            pltpu.VMEM((BLOCK, WIDTH), BF16),
            pltpu.VMEM((HEADS, BLOCK, BLOCK), BF16),
            pltpu.SemaphoreType.DMA((8,)),
        ],
        vmem=VMEM5,
    )(*[in_hbm(array) for array in (rows, summ, far, attn)], sums)


def fixed_backward_kernel(
    rows_in, own_in, attn_in, sums_ref, query_in, out_out, tail_ref,
    rows_ref, own_ref, attn_ref, query_ref, out_ref, sem, out_sem,
):
    copies = copy_all(
        [(attn_in, attn_ref)]
        + [(rows_in.at[array], rows_ref.at[array]) for array in (3, 2)]
        + [(own_in.at[head], own_ref.at[head]) for head in range(HEADS)]
        + [(rows_in.at[array], rows_ref.at[array]) for array in (0, 1)]
        + [(query_in, query_ref)],
        sem,
    )
    heads = range(HEADS)
    at = [slice(head * HD, (head + 1) * HD) for head in heads]
    low, high = slice(0, BLOCK // 2), slice(BLOCK // 2, BLOCK)
    scaling, other = factors(sums_ref)

    def keep(pair, slot, chunks, columns, rows):
        rows = rows.reshape(-1, 8, HD).astype(BF16)
        out_ref[pair, chunks, 8 * slot : 8 * slot + 8, columns] = rows

    copies[0].wait()
    copies[1].wait()
    grads = []
    for head in heads:
        wide = attn_ref[:, at[head]].astype(F32)
        keep(0, 0, slice(0, EIGHTS), at[head], wide * scaling)
        grads.append(gradient(wide, rows_ref[3, :, at[head]], scaling, other))
    scores = []
    copies[2].wait()
    for head in heads:
        copies[3 + head].wait()
        grad, row_dot = grads[head]
        first = dot_nt(grad[low], rows_ref[2, low, at[head]]) - row_dot[low]
        second = dot_nt(grad[high], rows_ref[2, :, at[head]]) - row_dot[high]
        first = (own_ref[head, low, low].astype(F32) * first * scale).astype(BF16)
        second = (own_ref[head, high, :].astype(F32) * second * scale).astype(BF16)
        scores.append((first, second))

    first_chunks, last_chunks = slice(0, EIGHTS // 2), slice(EIGHTS // 2, EIGHTS)

    def put(pair, slot, head, first, second, b):
        grads_low = dot_tn(first, b[low]) + dot_tn(second[:, low], b[high])
        grads_high = dot_tn(second[:, high], b[high])
        keep(pair, slot, first_chunks, at[head], grads_low)
        keep(pair, slot, last_chunks, at[head], grads_high)
        tail_ref[slot, :, at[head]] = grads_high[BLOCK // 2 - 8 :]

    for head in heads:
        put(0, 1, head, own_ref[head, low, low], own_ref[head, high, :], grads[head][0])
    sent = copy_all([(out_ref.at[0], out_out.at[0])], out_sem.at[0])
    copies[3 + HEADS].wait()
    for head in heads:
        put(1, 0, head, *scores[head], rows_ref[0, :, at[head]])
    copies[4 + HEADS].wait()
    copies[5 + HEADS].wait()
    for head in heads:
        first, second = scores[head]
        first = dot(first, rows_ref[1, low, at[head]]) + query_ref[low, at[head]]
        second = dot(second, rows_ref[1, :, at[head]]) + query_ref[high, at[head]]
        keep(1, 1, first_chunks, at[head], first)
        keep(1, 1, last_chunks, at[head], second)
    sent += copy_all([(out_ref.at[1], out_out.at[1])], out_sem.at[1])
    for copy in sent:
        copy.wait()


def fixed_backward(rows, own, attn, sums, far_query):
    return call(
        fixed_backward_kernel,
        1,
        [IN_HBM, IN_HBM, IN_HBM, spec((8, NB), 0, 0), IN_HBM],
        [IN_HBM, spec((2, 8, WIDTH), 0, 0, 0)],
        [
            pltpu.HBM((2, EIGHTS, 16, WIDTH), BF16),
            jax.ShapeDtypeStruct((2, 8, WIDTH), F32),
        ],
        5 * 10**9,
        8 * 2**20,
        [
            pltpu.VMEM((4, BLOCK, WIDTH), BF16),
            pltpu.VMEM((HEADS, BLOCK, BLOCK), BF16),
            pltpu.VMEM((BLOCK, WIDTH), BF16),
            pltpu.VMEM((BLOCK, WIDTH), F32),
            pltpu.VMEM((2, EIGHTS, 16, WIDTH), BF16),
            pltpu.SemaphoreType.DMA((HEADS + 6,)),
            pltpu.SemaphoreType.DMA((2, 1)),
        ],
        vmem=VMEM5,
    )(*[in_hbm(array) for array in (rows, own, attn)], sums, in_hbm(far_query))


def unpack_kernel(recv_ref, fixed_in, parts_ref, moved_ref, tails_ref, *refs):
    outs, fixed_ref, out_ref, in_sem, out_sem = refs[:4], refs[4], refs[5], refs[6], refs[7]
    parts = 4
    size = EIGHTS // parts
    copies = copy_all(
        [
            (fixed_in.at[:, pl.ds(part * size, size)], fixed_ref.at[:, pl.ds(part * size, size)])
            for part in range(parts)
        ],
        in_sem,
    )
    sent = []
    row, col = index_columns(256, 256)
    array, token, head, kind = row >> 6, (row >> 3) & 7, (row >> 1) & 3, row & 1
    strided = (token >> 2) * 64 + head * 16 + array * OFFS + (token & 3)
    fixed = 128 + (((array + 1) >> 1) & 1) * 64 + head * 16 + (array & 1) * 8 + token
    pick = one_hot(col == jnp.where(kind == 0, strided, fixed))
    row = lax.broadcasted_iota(jnp.int32, (16, WIDTH), 0)
    totals = parts_ref[...] + moved_ref[...].astype(F32)
    tails = []
    for array in range(2):
        part = [totals[:, n * HD : (n + 1) * HD] for n in range(array, 2 * HEADS, 2)]
        part = jnp.concatenate(part, 1) + tails_ref[array, 8 - SUMM :]
        tails.append(jnp.concatenate([part] * 4, 0).astype(BF16))
    heads = [slice(head * HD, (head + 1) * HD) for head in range(HEADS)]
    for at in range(0, EIGHTS, 4):
        if at % size == 0:
            copies[at // size].wait()
        four = []
        for n in range(at, at + 4):
            fixed = [fixed_ref[pair, n] for pair in range(2)]
            if n == EIGHTS - 1:
                fixed[0] = jnp.where(row >= 16 - SUMM, tails[1], fixed[0])
                fixed[1] = jnp.where((row >= 8 - SUMM) & (row < 8), tails[0], fixed[1])
            rows = [recv_ref[2 * n + home, :, head] for home in range(2) for head in heads]
            rows += [part[:, head] for part in fixed for head in heads]
            four.append(jnp.concatenate(rows, 0))
        picked = dot(pick, jnp.concatenate(four, 1)).astype(BF16)
        for n in range(4):
            for array in range(4):
                out_ref[array, 64 * (at + n) : 64 * (at + n + 1)] = picked[
                    array * 64 : (array + 1) * 64, n * HD : (n + 1) * HD
                ]
        if (at + 4) % size == 0:
            part = at // size
            where = pl.ds(part * size * 64, size * 64)
            sent += copy_all(
                [(out_ref.at[array, where], outs[array].at[where]) for array in range(4)],
                out_sem.at[part],
            )
    for copy in sent:
        copy.wait()


def unpack(recv, fixed, parts, moved, tails):
    rows = call(
        unpack_kernel,
        1,
        [spec((NB, 16, WIDTH), 0, 0, 0), IN_HBM]
        + [spec((SUMM, 2 * WIDTH), 0, 0)] * 2
        + [spec((2, 8, WIDTH), 0, 0, 0)],
        [IN_HBM] * 4,
        [jax.ShapeDtypeStruct((BLOCK * 8, HD), BF16)] * 4,
        2 * 10**9,
        8 * 2**20,
        [
            pltpu.VMEM((2, EIGHTS, 16, WIDTH), BF16),
            pltpu.VMEM((4, BLOCK * 8, HD), BF16),
            pltpu.SemaphoreType.DMA((4,)),
            pltpu.SemaphoreType.DMA((4, 4)),
        ],
        vmem=VMEM6,
    )(recv, in_hbm(fixed), parts, moved, tails)
    return tuple(unflat(array) for array in rows)


def place(index):
    coords = []
    for size in PARTS[::-1]:
        coords.append(index % size)
        index = index // size
    return coords[::-1]


def joined(coords):
    index = 0
    for size, at in zip(PARTS, coords):
        index = index * size + at
    return index


def shift(array, part, step):
    perm = []
    for source in range(NB):
        coords = place(source)
        coords[part] = (coords[part] + step) % PARTS[part]
        perm.append((source, joined(coords)))
    return lax.ppermute(array, "seq", perm)


def other_head(array):
    return lax.ppermute(array, "head", [(0, 1), (1, 0)])


Z, X, Y, CORE = range(4)
Y_BACK = (0, 1, -1, 2)
SLAB = 2 * WIDTH


def gather_along_z(sent, me):
    size = PARTS[Z]
    step = NB // size
    groups = [[at + step * z for z in range(size)] for at in range(step)]
    held = lax.all_to_all(sent, "seq", 0, 0, axis_index_groups=groups, tiled=True)
    held = jnp.concatenate([held, held], 0)
    first = (me // step + 4 * (me % 2)) % size
    return lax.dynamic_slice_in_dim(held, first, size, 0).reshape(size * SUMM, SLAB)


def gather_summaries(held):
    held = jnp.concatenate([held, shift(held, X, 1)], 0)
    held = jnp.concatenate([held] + [shift(held, Y, back) for back in Y_BACK[1:]], 0)
    return jnp.concatenate([held, shift(held, CORE, 1)], 0)


def add_up(own, moved):
    return sum((part.astype(F32) for part in moved), own)


def scatter_along_core(kept, sent):
    return add_up(kept, [shift(sent, CORE, 1)])


def scatter_along_y(parts):
    parts = parts.reshape(4, -1, SLAB)
    sent = parts.astype(BF16)
    return add_up(parts[0], [shift(sent[n], Y, -Y_BACK[n]) for n in range(1, 4)])


def scatter_summaries(parts):
    parts = parts.reshape(2, -1, SLAB)
    parts = add_up(parts[0], [shift(parts[1].astype(BF16), X, -1)])
    sent = parts.astype(BF16).reshape(2, 4, SUMM, SLAB)
    moved = []
    for n in range(4):
        perm = []
        for source in range(NB):
            coords = place(source)
            coords[Z] = (coords[Z] + 4 * coords[CORE] + n) % PARTS[Z]
            perm.append((source, joined(coords)))
        moved.append(lax.ppermute(sent[:, n].reshape(2 * SUMM, SLAB), "seq", perm))
    parts = add_up(0.0, moved)
    return parts[:SUMM], shift(parts[SUMM:].astype(BF16), CORE, 1)


def slot_blocks(me):
    slots = jnp.arange(NB, dtype=jnp.int32)
    z, x, y, core = place(me)
    core_of = (core - (slots >> 6)) % 2
    y_of = (y - jnp.array(Y_BACK, jnp.int32)[(slots >> 4) & 3]) % PARTS[Y]
    x_of = (x - ((slots >> 3) & 1)) % PARTS[X]
    z_of = (z + 4 * core_of + (slots & 7)) % PARTS[Z]
    return joined((z_of, x_of, y_of, core_of))


def shards(queries, key_rows, value_rows, cotangent):
    me = lax.axis_index("seq")
    arrays = tuple(flat(array) for array in (queries, key_rows, value_rows, cotangent))
    send = pack_strided(arrays)
    summ = gather_along_z(pack_summaries(arrays[1], arrays[2]), me)
    send, summ = lax.optimization_barrier((send, summ))
    recv = lax.all_to_all(send, "seq", 0, 0, tiled=True)
    summ = gather_summaries(summ)
    seen = jnp.repeat((slot_blocks(me) < me).astype(jnp.int32), SUMM)[None]
    rows = pack_fixed(arrays)
    fixed_attn, own_prob, far_prob, fixed_sums = fixed_forward(rows, summ, seen)
    fixed_send = fixed_sums[:, :2].reshape(NB, OFFS, 2).transpose(0, 2, 1).reshape(NB, 8)
    fixed_both = fixed_send + other_head(fixed_send)
    keys, prob, grp, sums, sums_send = strided_forward(recv, jnp.pad(fixed_both, ((0, 0), (0, HD - 8))))
    sums_in = lax.all_to_all(sums_send, "seq", 0, 0, tiled=True)
    sums_other = other_head(sums[:, 8:16])
    own_sums = sums_in[:, 0, 8:16].T
    block_sums = fixed_both.T + own_sums + other_head(own_sums)
    send_back = strided_backward(keys, prob, grp, sums, sums_other, sums_in)
    recv_back = lax.all_to_all(send_back, "seq", 0, 0, tiled=True)
    far_query, kept, sent = summary_backward(rows, summ, far_prob, fixed_attn, block_sums)
    fixed_out, tails = fixed_backward(rows, own_prob, fixed_attn, block_sums, far_query)
    parts = scatter_along_y(scatter_along_core(kept, sent))
    parts, fixed_out, tails = lax.optimization_barrier((parts, fixed_out, tails))
    parts, moved = scatter_summaries(parts)
    return unpack(recv_back, fixed_out, parts, moved, tails)


def solution(mesh):
    specs = (P("seq", None, "head"),) * 4
    return jax.shard_map(shards, mesh=mesh, in_specs=specs, out_specs=specs, check_vma=False)
```

```python
import jax
import jax.numpy as jnp
from jax import lax
from jax.experimental import pallas as pl
from jax.experimental.pallas import tpu as pltpu
from jax.sharding import PartitionSpec as P

BLOCK = 512
SUMM = 4
HD = 128
COLS = 1024
NB = 128
HEADS = 4
EIGHTS = BLOCK // 8
OFFS = 4
WIDTH = HEADS * HD
PARTS = (8, 2, 4, 2)
VMEM3, VMEM4, VMEM5, VMEM6 = 32, 32, 48, 32

epsilon = 1e-06
scale = HD ** (-0.5)
F32 = jnp.float32
BF16 = jnp.bfloat16


def iotas(shape):
    return (
        lax.broadcasted_iota(jnp.int32, shape, 0),
        lax.broadcasted_iota(jnp.int32, shape, 1),
    )


def index_columns(rows, columns):
    return (
        lax.broadcasted_iota(jnp.int32, (rows, 1), 0),
        lax.broadcasted_iota(jnp.int32, (1, columns), 1),
    )


def one_hot(hit):
    return jnp.where(hit, 1.0, 0.0).astype(BF16)


def dot(a, b):
    return jnp.dot(a, b, preferred_element_type=F32)


def dot_nt(a, b):
    return lax.dot_general(a, b, (((1,), (1,)), ((), ())), preferred_element_type=F32)


def dot_tn(a, b):
    return lax.dot_general(a, b, (((0,), (0,)), ((), ())), preferred_element_type=F32)


def batch_dot(a, b, left, right):
    return lax.dot_general(
        a, b, (((left,), (right,)), ((0,), (0,))), preferred_element_type=F32
    )


def flat(array):
    split = array.reshape(BLOCK, 2, HEADS, HD).transpose(0, 2, 1, 3)
    return split.reshape(BLOCK * HEADS * 2, HD)


def unflat(rows):
    return rows.reshape(BLOCK, HEADS, 2, HD).transpose(0, 2, 1, 3).reshape(BLOCK, 2, WIDTH)


def call(kernel, grid, in_specs, out_specs, out_shape, flops, nbytes, scratch=(), vmem=60):
    return pl.pallas_call(
        kernel,
        grid=(grid,),
        in_specs=in_specs,
        out_specs=out_specs,
        out_shape=out_shape,
        scratch_shapes=list(scratch),
        compiler_params=pltpu.CompilerParams(vmem_limit_bytes=vmem * 2**20),
        cost_estimate=pl.CostEstimate(flops=flops, bytes_accessed=nbytes, transcendentals=0),
    )


IN_HBM = pl.BlockSpec(memory_space=pltpu.HBM)


def in_hbm(array):
    return pltpu.with_memory_space_constraint(array, pltpu.HBM)


def copy_all(pairs, sems):
    copies = [
        pltpu.make_async_copy(source, target, sems.at[n]) for n, (source, target) in enumerate(pairs)
    ]
    for copy in copies:
        copy.start()
    return copies


def spec(block, *index):
    return pl.BlockSpec(block, lambda i: tuple(i if at == "i" else at for at in index))


def pack_strided_kernel(q_ref, k_ref, v_ref, c_ref, send_ref, rows_ref, out_ref, in_sem, out_sem):
    parts = 4
    size = BLOCK * 8 // parts
    copies = copy_all(
        [
            (ref.at[pl.ds(part * size, size)], rows_ref.at[array, pl.ds(part * size, size)])
            for part in range(parts)
            for array, ref in enumerate((q_ref, k_ref, v_ref, c_ref))
        ],
        in_sem,
    )
    row, col = iotas((128, 256))
    home, head, array, offset = row >> 6, (row >> 4) & 3, (row >> 2) & 3, row & 3
    pick = one_hot(col == array * 64 + ((home * OFFS + offset) * HEADS + head) * 2)
    sent = []
    for part in range(parts):
        for copy in copies[4 * part : 4 * part + 4]:
            copy.wait()
        for at in range(part * 64 // parts, (part + 1) * 64 // parts, 2):
            pair = [
                jnp.concatenate(
                    [rows_ref[array, 64 * n : 64 * (n + 1)] for n in (at, at + 1)], 1
                )
                for array in range(4)
            ]
            picked = dot(pick, jnp.concatenate(pair, 0)).astype(BF16)
            for n in range(2):
                for home in range(2):
                    for head in range(HEADS):
                        row = home * 64 + head * 16
                        out_ref[2 * (at + n) + home, :, head * HD : (head + 1) * HD] = picked[
                            row : row + 16, n * HD : (n + 1) * HD
                        ]
        where = pl.ds(part * NB // parts, NB // parts)
        copy = pltpu.make_async_copy(out_ref.at[where], send_ref.at[where], out_sem.at[part])
        copy.start()
        sent.append(copy)
    for copy in sent:
        copy.wait()


def pack_strided(arrays):
    return call(
        pack_strided_kernel,
        1,
        [IN_HBM] * 4,
        IN_HBM,
        jax.ShapeDtypeStruct((NB, 16, WIDTH), BF16),
        10**9,
        6 * 2**20,
        [
            pltpu.VMEM((4, BLOCK * 8, HD), BF16),
            pltpu.VMEM((NB, 16, WIDTH), BF16),
            pltpu.SemaphoreType.DMA((16,)),
            pltpu.SemaphoreType.DMA((4,)),
        ],
    )(*arrays)


def pack_summaries_kernel(key_ref, value_ref, out_ref):
    row, col = iotas((8, 32))
    parts = []
    for head in range(HEADS):
        pick = one_hot(col == row * 2 * HEADS + 2 * head + 1)
        parts += [dot(pick, ref[...])[:SUMM] for ref in (key_ref, value_ref)]
    rows = jnp.concatenate(parts, 1).astype(BF16)
    for z in range(out_ref.shape[0]):
        out_ref[z] = rows


def pack_summaries(keys, values):
    last = spec((8 * SUMM, HD), BLOCK // SUMM - 1, 0)
    shape = (PARTS[0], SUMM, 2 * WIDTH)
    return call(
        pack_summaries_kernel,
        1,
        [last, last],
        spec(shape, 0, 0, 0),
        jax.ShapeDtypeStruct(shape, BF16),
        10**6,
        2**17,
    )(in_hbm(keys), in_hbm(values))


def pack_fixed_kernel(q_ref, k_ref, v_ref, c_ref, out_ref):
    row, col = iotas((64, 128))
    pick = one_hot(col == ((row & 15) * HEADS + (row >> 4)) * 2 + 1)
    for at in range(16):
        rows = [ref[128 * at : 128 * (at + 1)] for ref in (q_ref, k_ref, v_ref, c_ref)]
        picked = dot(pick, jnp.concatenate(rows, 1)).astype(BF16)
        for array in range(4):
            for head in range(HEADS):
                out_ref[array, 16 * at : 16 * (at + 1), head * HD : (head + 1) * HD] = picked[
                    16 * head : 16 * (head + 1), array * HD : (array + 1) * HD
                ]


def pack_fixed(arrays):
    return call(
        pack_fixed_kernel,
        2,
        [spec((2048, HD), "i", 0)] * 4,
        spec((4, BLOCK // 2, WIDTH), 0, "i", 0),
        jax.ShapeDtypeStruct((4, BLOCK, WIDTH), BF16),
        10**9,
        6 * 2**20,
    )(*arrays)


def fixed_probabilities(query, key, summ_key, seen):
    row, col = iotas((BLOCK, BLOCK))
    own = jnp.where(col <= row, dot_nt(query, key) * scale, -jnp.inf)
    far = jnp.where(seen > 0, dot_nt(query, summ_key) * scale, -jnp.inf)
    top = jnp.maximum(
        jnp.max(own, axis=-1, keepdims=True), jnp.max(far, axis=-1, keepdims=True)
    )
    own = jnp.exp(own - top)
    far = jnp.exp(far - top)
    total = jnp.sum(own, axis=-1, keepdims=True) + jnp.sum(far, axis=-1, keepdims=True)
    inverse = 1.0 / total
    return own * inverse, far * inverse


def fixed_forward_kernel(rows_ref, summ_ref, seen_ref, attn_ref, own_ref, far_ref, sums_ref):
    own, far = fixed_probabilities(rows_ref[0], rows_ref[1], summ_ref[:, :HD], seen_ref[...])
    own_ref[0] = own.astype(BF16)
    far_ref[0] = far.astype(BF16)
    attn = (dot(own_ref[0], rows_ref[2]) + dot(far_ref[0], summ_ref[:, HD:])).astype(BF16)
    attn_ref[...] = attn
    wide = attn.astype(F32)
    square = jnp.sum(wide * wide, axis=-1, keepdims=True)
    cross = jnp.sum(wide * rows_ref[3].astype(F32), axis=-1, keepdims=True)
    lane = lax.broadcasted_iota(jnp.int32, (BLOCK, 8), 1)
    part = jnp.where(lane == 0, square, jnp.where(lane == 1, cross, 0.0))

    @pl.when(pl.program_id(0) == 0)
    def _():
        sums_ref[...] = part

    @pl.when(pl.program_id(0) > 0)
    def _():
        sums_ref[...] += part


def fixed_forward(rows, summ, seen):
    return call(
        fixed_forward_kernel,
        HEADS,
        [
            spec((4, BLOCK, HD), 0, 0, "i"),
            spec((BLOCK, 2 * HD), 0, "i"),
            spec((1, BLOCK), 0, 0),
        ],
        [
            spec((BLOCK, HD), 0, "i"),
            spec((1, BLOCK, BLOCK), "i", 0, 0),
            spec((1, BLOCK, BLOCK), "i", 0, 0),
            spec((BLOCK, 8), 0, 0),
        ],
        [
            jax.ShapeDtypeStruct((BLOCK, WIDTH), BF16),
            pltpu.HBM((HEADS, BLOCK, BLOCK), BF16),
            pltpu.HBM((HEADS, BLOCK, BLOCK), BF16),
            jax.ShapeDtypeStruct((BLOCK, 8), F32),
        ],
        4 * 10**9,
        4 * 2**20,
    )(rows, summ, seen)


def swap_matrix():
    row, col = iotas((256, 256))
    return one_hot(col == ((row & 15) << 4) + (row >> 4))


def strided_forward_kernel(
    recv_ref, fixed_ref, keys_out, prob_out, grp_ref, sums_ref, send_ref, keys_ref, prob_ref, sem
):
    swap = swap_matrix()
    for at in range(0, NB, 16):
        rows = dot(swap, recv_ref[at : at + 16].reshape(256, WIDTH)).astype(BF16)
        for head in range(HEADS):
            tiles = rows[:, head * HD : (head + 1) * HD].reshape(4, OFFS, 16, HD)
            keys_ref[head, :, :, at : at + 16, :] = tiles[:3]
            grp_ref[head, 0, :, at : at + 16, :] = tiles[3]
    copies = copy_all([(keys_ref, keys_out)], sem.at[0])
    row, col = iotas((NB, NB))
    heads = range(HEADS)
    scores = [batch_dot(keys_ref[head, 0], keys_ref[head, 1], 2, 2) * scale for head in heads]
    scores = [jnp.where((col <= row)[None], score, -jnp.inf) for score in scores]
    expos = [jnp.exp(score - jnp.max(score, axis=-1, keepdims=True)) for score in scores]
    probs = [
        (expo * (1.0 / jnp.sum(expo, axis=-1, keepdims=True))).astype(BF16) for expo in expos
    ]
    attns = [batch_dot(probs[head], keys_ref[head, 2], 2, 1).astype(BF16) for head in heads]
    square, cross = 0.0, 0.0
    for head in heads:
        prob_ref[head] = probs[head]
        copies += copy_all([(prob_ref.at[head], prob_out.at[head])], sem.at[head + 1])
        wide = attns[head].astype(F32)
        square += wide * wide
        cross += wide * grp_ref[head, 0].astype(F32)
        grp_ref[head, 1] = attns[head]
    square = jnp.sum(square, axis=-1, keepdims=True)
    cross = jnp.sum(cross, axis=-1, keepdims=True)
    lane = lax.broadcasted_iota(jnp.int32, (NB, HD), 1)
    part = fixed_ref[...]
    for at in range(OFFS):
        part += jnp.where(lane == 8 + at, square[at], jnp.where(lane == 12 + at, cross[at], 0.0))
    sums_ref[...] = part
    send_ref[...] = part.reshape(NB, 1, HD)
    for copy in copies:
        copy.wait()


def strided_forward(recv, fixed_sums):
    return call(
        strided_forward_kernel,
        1,
        [spec((NB, 16, WIDTH), 0, 0, 0), spec((NB, HD), 0, 0)],
        [
            IN_HBM,
            IN_HBM,
            spec((HEADS, 2, OFFS, NB, HD), 0, 0, 0, 0, 0),
            spec((NB, HD), 0, 0),
            spec((NB, 1, HD), 0, 0, 0),
        ],
        [
            pltpu.HBM((HEADS, 3, OFFS, NB, HD), BF16),
            pltpu.HBM((HEADS, OFFS, NB, NB), BF16),
            jax.ShapeDtypeStruct((HEADS, 2, OFFS, NB, HD), BF16),
            jax.ShapeDtypeStruct((NB, HD), F32),
            jax.ShapeDtypeStruct((NB, 1, HD), F32),
        ],
        10**9,
        6 * 2**20,
        [
            pltpu.VMEM((HEADS, 3, OFFS, NB, HD), BF16),
            pltpu.VMEM((HEADS, OFFS, NB, NB), BF16),
            pltpu.SemaphoreType.DMA((HEADS + 1, 1)),
        ],
        vmem=VMEM3,
    )(recv, fixed_sums)


def normalize(wide, cotangent, square, cross):
    scaling = lax.rsqrt(square / (2 * COLS) + epsilon)
    normed = (wide * scaling).astype(BF16)
    grad = (
        scaling * cotangent.astype(F32) - wide * (scaling * scaling * scaling * cross / (2 * COLS))
    ).astype(BF16)
    return normed, grad, jnp.sum(grad.astype(F32) * wide, axis=-1, keepdims=True)


def factors(sums_ref):
    row, col = iotas((BLOCK, NB))
    spread = one_hot(col == row >> 2)
    rest, columns = sums_ref[...], 0.0
    for _ in range(3):
        part = rest.astype(BF16)
        rest = rest - part.astype(F32)
        columns += dot_nt(spread, part)
    row, col = iotas((BLOCK, 8))
    square, cross = (
        jnp.sum(jnp.where(col == (row & 3) + at, columns, 0.0), axis=-1, keepdims=True)
        for at in (0, OFFS)
    )
    scaling = lax.rsqrt(square / (2 * COLS) + epsilon)
    other = scaling * scaling * scaling * cross / (2 * COLS)
    return jnp.broadcast_to(scaling, (BLOCK, HD)), jnp.broadcast_to(other, (BLOCK, HD))


def gradient(wide, cotangent, scaling, other):
    grad = (scaling * cotangent.astype(F32) - wide * other).astype(BF16)
    return grad, jnp.sum(grad.astype(F32) * wide, axis=-1, keepdims=True)


def strided_backward_kernel(
    keys_in, prob_in, grp_ref, sums_ref, other_ref, recv_ref, send_out,
    keys_ref, prob_ref, out_ref, send_ref, in_sem, out_sem,
):
    fetched = [
        copy_all(
            [(keys_in.at[head], keys_ref.at[head]), (prob_in.at[head], prob_ref.at[head])],
            in_sem.at[head],
        )
        for head in range(HEADS)
    ]
    moved = recv_ref[...].reshape(NB, HD)
    total = sums_ref[:, 8:16] + other_ref[...] + moved[:, :8]
    square = jnp.stack([total[:, at : at + 1] for at in range(OFFS)])
    cross = jnp.stack([total[:, OFFS + at : OFFS + at + 1] for at in range(OFFS)])
    grads = []
    for head in range(HEADS):
        wide = grp_ref[head, 1].astype(F32)
        normed, grad, row_dot = normalize(wide, grp_ref[head, 0], square, cross)
        out_ref[head, 0] = normed
        grads.append((grad, row_dot))
    heads = range(HEADS)
    probs, grad_probs = [], []
    for head in heads:
        for copy in fetched[head]:
            copy.wait()
        probs.append(prob_ref[head])
        grad_probs.append(batch_dot(grads[head][0], keys_ref[head, 2], 2, 2))
    scores = [
        (probs[head].astype(F32) * (grad_probs[head] - grads[head][1]) * scale).astype(BF16)
        for head in heads
    ]
    for head in heads:
        out_ref[head, 3] = batch_dot(probs[head], grads[head][0], 1, 1).astype(BF16)
    for head in heads:
        out_ref[head, 1] = batch_dot(scores[head], keys_ref[head, 1], 2, 1).astype(BF16)
    for head in heads:
        out_ref[head, 2] = batch_dot(scores[head], keys_ref[head, 0], 1, 1).astype(BF16)
    swap = swap_matrix()
    copies = []
    for at in range(0, NB, 16):
        rows = [out_ref[head, :, :, at : at + 16, :].reshape(256, HD) for head in range(HEADS)]
        moved = dot(swap, jnp.concatenate(rows, 1)).astype(BF16)
        send_ref[at : at + 16] = moved.reshape(16, 16, WIDTH)
        where = pl.ds(at, 16)
        copies += copy_all([(send_ref.at[where], send_out.at[where])], out_sem.at[at // 16])
    for copy in copies:
        copy.wait()


def strided_backward(keys, prob, grp, sums, other, recv):
    return call(
        strided_backward_kernel,
        1,
        [
            IN_HBM,
            IN_HBM,
            spec((HEADS, 2, OFFS, NB, HD), 0, 0, 0, 0, 0),
            spec((NB, HD), 0, 0),
            spec((NB, 8), 0, 0),
            spec((NB, 1, HD), 0, 0, 0),
        ],
        IN_HBM,
        pltpu.HBM((NB, 16, WIDTH), BF16),
        10**9,
        6 * 2**20,
        [
            pltpu.VMEM((HEADS, 3, OFFS, NB, HD), BF16),
            pltpu.VMEM((HEADS, OFFS, NB, NB), BF16),
            pltpu.VMEM((HEADS, 4, OFFS, NB, HD), BF16),
            pltpu.VMEM((NB, 16, WIDTH), BF16),
            pltpu.SemaphoreType.DMA((HEADS, 2)),
            pltpu.SemaphoreType.DMA((NB // 16, 1)),
        ],
        vmem=VMEM4,
    )(in_hbm(keys), in_hbm(prob), grp, sums, other, recv)


def summary_backward_kernel(
    rows_in, summ_in, far_in, attn_in, sums_ref, query_ref, keep_ref, send_ref,
    attn_ref, cot_ref, summ_ref, rows_ref, far_ref, sem,
):
    copies = copy_all(
        [
            (attn_in, attn_ref),
            (rows_in.at[3], cot_ref),
            (summ_in, summ_ref),
        ]
        + [(far_in.at[head], far_ref.at[head]) for head in range(HEADS)]
        + [(rows_in.at[0], rows_ref)],
        sem,
    )
    heads = range(HEADS)
    at = [slice(head * HD, (head + 1) * HD) for head in heads]
    to_key = [slice(2 * head * HD, (2 * head + 1) * HD) for head in heads]
    to_value = [slice((2 * head + 1) * HD, (2 * head + 2) * HD) for head in heads]
    scaling, other = factors(sums_ref)
    copies[0].wait()
    copies[1].wait()
    grads = [
        gradient(attn_ref[:, at[head]].astype(F32), cot_ref[:, at[head]], scaling, other)
        for head in heads
    ]
    scores = []
    copies[2].wait()
    for head in heads:
        copies[3 + head].wait()
        grad, row_dot = grads[head]
        grad_prob = dot_nt(grad, summ_ref[:, to_value[head]])
        score = far_ref[head].astype(F32) * (grad_prob - row_dot) * scale
        scores.append(score.astype(BF16))

    def put(to, grads):
        grads = grads.reshape(2, 8, 2, 16, HD)
        keep = jnp.stack([grads[0, :, 0], grads[1, :, 1]], 1)
        send = jnp.stack([grads[1, :, 0], grads[0, :, 1]], 1)
        keep_ref[:, to] = keep.reshape(BLOCK // 2, HD)
        send_ref[:, to] = send.reshape(BLOCK // 2, HD).astype(BF16)

    for head in heads:
        put(to_value[head], dot_tn(far_ref[head], grads[head][0]))
    copies[3 + HEADS].wait()
    for head in heads:
        put(to_key[head], dot_tn(scores[head], rows_ref[:, at[head]]))
    for head in heads:
        query_ref[:, at[head]] = dot(scores[head], summ_ref[:, to_key[head]])


def summary_backward(rows, summ, far, attn, sums):
    return call(
        summary_backward_kernel,
        1,
        [IN_HBM] * 4 + [spec((8, NB), 0, 0)],
        [
            spec((BLOCK, WIDTH), 0, 0),
            spec((BLOCK // 2, 2 * WIDTH), 0, 0),
            spec((BLOCK // 2, 2 * WIDTH), 0, 0),
        ],
        [
            pltpu.HBM((BLOCK, WIDTH), F32),
            jax.ShapeDtypeStruct((BLOCK // 2, 2 * WIDTH), F32),
            jax.ShapeDtypeStruct((BLOCK // 2, 2 * WIDTH), BF16),
        ],
        3 * 10**9,
        8 * 2**20,
        [
            pltpu.VMEM((BLOCK, WIDTH), BF16),
            pltpu.VMEM((BLOCK, WIDTH), BF16),
            pltpu.VMEM((BLOCK, 2 * WIDTH), BF16),
            pltpu.VMEM((BLOCK, WIDTH), BF16),
            pltpu.VMEM((HEADS, BLOCK, BLOCK), BF16),
            pltpu.SemaphoreType.DMA((8,)),
        ],
        vmem=VMEM5,
    )(*[in_hbm(array) for array in (rows, summ, far, attn)], sums)


def fixed_backward_kernel(
    rows_in, own_in, attn_in, sums_ref, query_in, out_out, tail_ref,
    rows_ref, own_ref, attn_ref, query_ref, out_ref, sem, out_sem,
):
    copies = copy_all(
        [(attn_in, attn_ref)]
        + [(rows_in.at[array], rows_ref.at[array]) for array in (3, 2)]
        + [(own_in.at[head], own_ref.at[head]) for head in range(HEADS)]
        + [(rows_in.at[array], rows_ref.at[array]) for array in (0, 1)]
        + [(query_in, query_ref)],
        sem,
    )
    heads = range(HEADS)
    at = [slice(head * HD, (head + 1) * HD) for head in heads]
    low, high = slice(0, BLOCK // 2), slice(BLOCK // 2, BLOCK)
    scaling, other = factors(sums_ref)

    def keep(pair, slot, chunks, columns, rows):
        rows = rows.reshape(-1, 8, HD).astype(BF16)
        out_ref[pair, chunks, 8 * slot : 8 * slot + 8, columns] = rows

    copies[0].wait()
    copies[1].wait()
    grads = []
    for head in heads:
        wide = attn_ref[:, at[head]].astype(F32)
        keep(0, 0, slice(0, EIGHTS), at[head], wide * scaling)
        grads.append(gradient(wide, rows_ref[3, :, at[head]], scaling, other))
    scores = []
    copies[2].wait()
    for head in heads:
        copies[3 + head].wait()
        grad, row_dot = grads[head]
        first = dot_nt(grad[low], rows_ref[2, low, at[head]]) - row_dot[low]
        second = dot_nt(grad[high], rows_ref[2, :, at[head]]) - row_dot[high]
        first = (own_ref[head, low, low].astype(F32) * first * scale).astype(BF16)
        second = (own_ref[head, high, :].astype(F32) * second * scale).astype(BF16)
        scores.append((first, second))

    first_chunks, last_chunks = slice(0, EIGHTS // 2), slice(EIGHTS // 2, EIGHTS)

    def put(pair, slot, head, first, second, b):
        grads_low = dot_tn(first, b[low]) + dot_tn(second[:, low], b[high])
        grads_high = dot_tn(second[:, high], b[high])
        keep(pair, slot, first_chunks, at[head], grads_low)
        keep(pair, slot, last_chunks, at[head], grads_high)
        tail_ref[slot, :, at[head]] = grads_high[BLOCK // 2 - 8 :]

    for head in heads:
        put(0, 1, head, own_ref[head, low, low], own_ref[head, high, :], grads[head][0])
    sent = copy_all([(out_ref.at[0], out_out.at[0])], out_sem.at[0])
    copies[3 + HEADS].wait()
    for head in heads:
        put(1, 0, head, *scores[head], rows_ref[0, :, at[head]])
    copies[4 + HEADS].wait()
    copies[5 + HEADS].wait()
    for head in heads:
        first, second = scores[head]
        first = dot(first, rows_ref[1, low, at[head]]) + query_ref[low, at[head]]
        second = dot(second, rows_ref[1, :, at[head]]) + query_ref[high, at[head]]
        keep(1, 1, first_chunks, at[head], first)
        keep(1, 1, last_chunks, at[head], second)
    sent += copy_all([(out_ref.at[1], out_out.at[1])], out_sem.at[1])
    for copy in sent:
        copy.wait()


def fixed_backward(rows, own, attn, sums, far_query):
    return call(
        fixed_backward_kernel,
        1,
        [IN_HBM, IN_HBM, IN_HBM, spec((8, NB), 0, 0), IN_HBM],
        [IN_HBM, spec((2, 8, WIDTH), 0, 0, 0)],
        [
            pltpu.HBM((2, EIGHTS, 16, WIDTH), BF16),
            jax.ShapeDtypeStruct((2, 8, WIDTH), F32),
        ],
        5 * 10**9,
        8 * 2**20,
        [
            pltpu.VMEM((4, BLOCK, WIDTH), BF16),
            pltpu.VMEM((HEADS, BLOCK, BLOCK), BF16),
            pltpu.VMEM((BLOCK, WIDTH), BF16),
            pltpu.VMEM((BLOCK, WIDTH), F32),
            pltpu.VMEM((2, EIGHTS, 16, WIDTH), BF16),
            pltpu.SemaphoreType.DMA((HEADS + 6,)),
            pltpu.SemaphoreType.DMA((2, 1)),
        ],
        vmem=VMEM5,
    )(*[in_hbm(array) for array in (rows, own, attn)], sums, in_hbm(far_query))


def unpack_kernel(recv_ref, fixed_in, parts_ref, moved_ref, tails_ref, *refs):
    outs, fixed_ref, out_ref, in_sem, out_sem = refs[:4], refs[4], refs[5], refs[6], refs[7]
    parts = 4
    size = EIGHTS // parts
    copies = copy_all(
        [
            (fixed_in.at[:, pl.ds(part * size, size)], fixed_ref.at[:, pl.ds(part * size, size)])
            for part in range(parts)
        ],
        in_sem,
    )
    sent = []
    row, col = index_columns(256, 256)
    array, token, head, kind = row >> 6, (row >> 3) & 7, (row >> 1) & 3, row & 1
    strided = (token >> 2) * 64 + head * 16 + array * OFFS + (token & 3)
    fixed = 128 + (((array + 1) >> 1) & 1) * 64 + head * 16 + (array & 1) * 8 + token
    pick = one_hot(col == jnp.where(kind == 0, strided, fixed))
    row = lax.broadcasted_iota(jnp.int32, (16, WIDTH), 0)
    totals = parts_ref[...] + moved_ref[...].astype(F32)
    tails = []
    for array in range(2):
        part = [totals[:, n * HD : (n + 1) * HD] for n in range(array, 2 * HEADS, 2)]
        part = jnp.concatenate(part, 1) + tails_ref[array, 8 - SUMM :]
        tails.append(jnp.concatenate([part] * 4, 0).astype(BF16))
    heads = [slice(head * HD, (head + 1) * HD) for head in range(HEADS)]
    for at in range(0, EIGHTS, 4):
        if at % size == 0:
            copies[at // size].wait()
        four = []
        for n in range(at, at + 4):
            fixed = [fixed_ref[pair, n] for pair in range(2)]
            if n == EIGHTS - 1:
                fixed[0] = jnp.where(row >= 16 - SUMM, tails[1], fixed[0])
                fixed[1] = jnp.where((row >= 8 - SUMM) & (row < 8), tails[0], fixed[1])
            rows = [recv_ref[2 * n + home, :, head] for home in range(2) for head in heads]
            rows += [part[:, head] for part in fixed for head in heads]
            four.append(jnp.concatenate(rows, 0))
        picked = dot(pick, jnp.concatenate(four, 1)).astype(BF16)
        for n in range(4):
            for array in range(4):
                out_ref[array, 64 * (at + n) : 64 * (at + n + 1)] = picked[
                    array * 64 : (array + 1) * 64, n * HD : (n + 1) * HD
                ]
        if (at + 4) % size == 0:
            part = at // size
            where = pl.ds(part * size * 64, size * 64)
            sent += copy_all(
                [(out_ref.at[array, where], outs[array].at[where]) for array in range(4)],
                out_sem.at[part],
            )
    for copy in sent:
        copy.wait()


def unpack(recv, fixed, parts, moved, tails):
    rows = call(
        unpack_kernel,
        1,
        [spec((NB, 16, WIDTH), 0, 0, 0), IN_HBM]
        + [spec((SUMM, 2 * WIDTH), 0, 0)] * 2
        + [spec((2, 8, WIDTH), 0, 0, 0)],
        [IN_HBM] * 4,
        [jax.ShapeDtypeStruct((BLOCK * 8, HD), BF16)] * 4,
        2 * 10**9,
        8 * 2**20,
        [
            pltpu.VMEM((2, EIGHTS, 16, WIDTH), BF16),
            pltpu.VMEM((4, BLOCK * 8, HD), BF16),
            pltpu.SemaphoreType.DMA((4,)),
            pltpu.SemaphoreType.DMA((4, 4)),
        ],
        vmem=VMEM6,
    )(recv, in_hbm(fixed), parts, moved, tails)
    return tuple(unflat(array) for array in rows)


def place(index):
    coords = []
    for size in PARTS[::-1]:
        coords.append(index % size)
        index = index // size
    return coords[::-1]


def joined(coords):
    index = 0
    for size, at in zip(PARTS, coords):
        index = index * size + at
    return index


def shift(array, part, step):
    perm = []
    for source in range(NB):
        coords = place(source)
        coords[part] = (coords[part] + step) % PARTS[part]
        perm.append((source, joined(coords)))
    return lax.ppermute(array, "seq", perm)


def other_head(array):
    return lax.ppermute(array, "head", [(0, 1), (1, 0)])


Z, X, Y, CORE = range(4)
Y_BACK = (0, 1, -1, 2)
SLAB = 2 * WIDTH


def gather_along_z(sent, me):
    size = PARTS[Z]
    step = NB // size
    groups = [[at + step * z for z in range(size)] for at in range(step)]
    held = lax.all_to_all(sent, "seq", 0, 0, axis_index_groups=groups, tiled=True)
    held = jnp.concatenate([held, held], 0)
    first = (me // step + 4 * (me % 2)) % size
    return lax.dynamic_slice_in_dim(held, first, size, 0).reshape(size * SUMM, SLAB)


def gather_summaries(held):
    held = jnp.concatenate([held, shift(held, X, 1)], 0)
    held = jnp.concatenate([held] + [shift(held, Y, back) for back in Y_BACK[1:]], 0)
    return jnp.concatenate([held, shift(held, CORE, 1)], 0)


def add_up(own, moved):
    return sum((part.astype(F32) for part in moved), own)


def scatter_along_core(kept, sent):
    return add_up(kept, [shift(sent, CORE, 1)])


def scatter_along_y(parts):
    parts = parts.reshape(4, -1, SLAB)
    sent = parts.astype(BF16)
    return add_up(parts[0], [shift(sent[n], Y, -Y_BACK[n]) for n in range(1, 4)])


def scatter_summaries(parts):
    parts = parts.reshape(2, -1, SLAB)
    parts = add_up(parts[0], [shift(parts[1].astype(BF16), X, -1)])
    sent = parts.astype(BF16).reshape(2, 4, SUMM, SLAB)
    moved = []
    for n in range(4):
        perm = []
        for source in range(NB):
            coords = place(source)
            coords[Z] = (coords[Z] + 4 * coords[CORE] + n) % PARTS[Z]
            perm.append((source, joined(coords)))
        moved.append(lax.ppermute(sent[:, n].reshape(2 * SUMM, SLAB), "seq", perm))
    parts = add_up(0.0, moved)
    return parts[:SUMM], shift(parts[SUMM:].astype(BF16), CORE, 1)


def slot_blocks(me):
    slots = jnp.arange(NB, dtype=jnp.int32)
    z, x, y, core = place(me)
    core_of = (core - (slots >> 6)) % 2
    y_of = (y - jnp.array(Y_BACK, jnp.int32)[(slots >> 4) & 3]) % PARTS[Y]
    x_of = (x - ((slots >> 3) & 1)) % PARTS[X]
    z_of = (z + 4 * core_of + (slots & 7)) % PARTS[Z]
    return joined((z_of, x_of, y_of, core_of))


def shards(queries, key_rows, value_rows, cotangent):
    me = lax.axis_index("seq")
    arrays = tuple(flat(array) for array in (queries, key_rows, value_rows, cotangent))
    send = pack_strided(arrays)
    summ = gather_along_z(pack_summaries(arrays[1], arrays[2]), me)
    send, summ = lax.optimization_barrier((send, summ))
    recv = lax.all_to_all(send, "seq", 0, 0, tiled=True)
    summ = gather_summaries(summ)
    seen = jnp.repeat((slot_blocks(me) < me).astype(jnp.int32), SUMM)[None]
    rows = pack_fixed(arrays)
    fixed_attn, own_prob, far_prob, fixed_sums = fixed_forward(rows, summ, seen)
    fixed_send = fixed_sums[:, :2].reshape(NB, OFFS, 2).transpose(0, 2, 1).reshape(NB, 8)
    fixed_both = fixed_send + other_head(fixed_send)
    keys, prob, grp, sums, sums_send = strided_forward(recv, jnp.pad(fixed_both, ((0, 0), (0, HD - 8))))
    sums_in = lax.all_to_all(sums_send, "seq", 0, 0, tiled=True)
    sums_other = other_head(sums[:, 8:16])
    own_sums = sums_in[:, 0, 8:16].T
    block_sums = fixed_both.T + own_sums + other_head(own_sums)
    send_back = strided_backward(keys, prob, grp, sums, sums_other, sums_in)
    recv_back = lax.all_to_all(send_back, "seq", 0, 0, tiled=True)
    far_query, kept, sent = summary_backward(rows, summ, far_prob, fixed_attn, block_sums)
    fixed_out, tails = fixed_backward(rows, own_prob, fixed_attn, block_sums, far_query)
    parts = scatter_along_y(scatter_along_core(kept, sent))
    parts, fixed_out, tails = lax.optimization_barrier((parts, fixed_out, tails))
    parts, moved = scatter_summaries(parts)
    return unpack(recv_back, fixed_out, parts, moved, tails)


def solution(mesh):
    specs = (P("seq", None, "head"),) * 4
    return jax.shard_map(shards, mesh=mesh, in_specs=specs, out_specs=specs, check_vma=False)
```
